128 devices in a mesh: cols: 32 (over y, z, core), rows: 4 (over x).
Axes of the slice: x: 4, y: 4, z: 4, core: 2. Of those that a mesh axis runs over, the one named last changes fastest.
Arguments:
- observed: float32 [1024, 32768], P('rows', 'cols'), may hold values from -14 to 14
- class_map: int32 [1024, 32768], P('rows', 'cols'), may hold values from 0 to 3
- class_weights: float32 [4], replicated, may hold values from 0.5 to 8
- blur_kernel: float32 [3, 3], replicated, may hold values from 0.02 to 0.25
Outputs:
- solution: float32 [1024, 32768], P('rows', 'cols')
- residual: float32 [1024, 32768], P('rows', 'cols')
The draws below stay inside these ranges and needn't reach their ends.
All inputs are finite; a program needn't handle non-finite values.
Results may differ from the reference program's by a relative error of at most 0.0003.
Values sent between devices are 32-bit elements; how exact they have to be, the bound alone decides.
A program may use at most 128 MiB of HBM per device.

```python
import math
import jax
import jax.numpy as jnp

COARSE = 8
SWEEPS = 8
ITERS = 2
CLASSES = 4
HEIGHT = 1024
BAND_LEN = 32768


def draw_observed(key, part):
    key_base, key_rows, key_cols = jax.random.split(key, 3)
    row_scale = jnp.exp(jax.random.uniform(key_rows, (HEIGHT, 1), jnp.float32) * (0.5 * math.log(10.0)))
    col_scale = jnp.exp(jax.random.uniform(key_cols, (1, BAND_LEN), jnp.float32) * (0.5 * math.log(10.0)))
    base = jnp.clip(jax.random.normal(key_base, (HEIGHT, BAND_LEN), jnp.float32), -4.0, 4.0)
    return (base * row_scale * col_scale / 3.0).astype(jnp.float32)


def touch_ends(values, key, smallest, largest):
    longest = values.shape.index(max(values.shape))
    spots = []
    for shift in (0, 1):
        where = [jax.random.randint(jax.random.fold_in(key, axis), (), 0, length) for axis, length in enumerate(values.shape)]
        where[longest] = (where[longest] + shift) % values.shape[longest]
        spots.append(tuple(where))
    return values.at[spots[0]].set(smallest).at[spots[1]].set(largest)


def setup_inputs(seed: int = 0) -> dict:
    key_of = jax.random.split(jax.random.key(seed), 5)
    return {
        "observed": draw_observed(jax.random.fold_in(key_of[4], 71), 0),
        "class_map": touch_ends(jax.random.randint(key_of[1], (HEIGHT, BAND_LEN), 0, CLASSES), jax.random.fold_in(key_of[1], 1), 0, CLASSES - 1).astype(jnp.int32),
        "class_weights": jnp.clip(jnp.exp(jax.random.uniform(key_of[2], (CLASSES,), jnp.float32, math.log(0.5), math.log(8.0))), 0.5, 8.0),
        "blur_kernel": jnp.clip(jnp.exp(jax.random.uniform(key_of[3], (3, 3), jnp.float32, math.log(0.02), math.log(0.25))), 0.02, 0.25),
    }


OMEGA = 0.8


def blurred(padded, kernel):
    height = padded.shape[0] - 2
    breadth = padded.shape[1] - 2
    summed = jnp.zeros((height, breadth), jnp.float32)
    for across in range(3):
        for along in range(3):
            summed = summed + kernel[across, along] * padded[across:across + height, along:along + breadth]
    return summed


def adjoint(padded, kernel):
    height = padded.shape[0] - 2
    breadth = padded.shape[1] - 2
    summed = jnp.zeros((height, breadth), jnp.float32)
    for across in range(3):
        for along in range(3):
            summed = summed + kernel[across, along] * padded[2 - across:2 - across + height, 2 - along:2 - along + breadth]
    return summed


def edge_weights(cond_pad):
    center = cond_pad[1:-1, 1:-1]
    return (0.5 * (center + cond_pad[1:-1, 2:]), 0.5 * (center + cond_pad[1:-1, :-2]),
            0.5 * (center + cond_pad[:-2, 1:-1]), 0.5 * (center + cond_pad[2:, 1:-1]))


def laplace(padded, edge_set):
    east, west, north, south = edge_set
    center = padded[1:-1, 1:-1]
    return ((east + west + north + south) * center - east * padded[1:-1, 2:] - west * padded[1:-1, :-2]
            - north * padded[:-2, 1:-1] - south * padded[2:, 1:-1])


def coarse_weights(edge_set, kernel):
    east, west, north, south = edge_set
    blocks_down = east.shape[0] // COARSE
    blocks_across = east.shape[1] // COARSE
    c_east = east[:, COARSE - 1::COARSE].reshape(blocks_down, COARSE, blocks_across).sum(axis=1)
    c_west = west[:, 0::COARSE].reshape(blocks_down, COARSE, blocks_across).sum(axis=1)
    c_north = north[0::COARSE, :].reshape(blocks_down, blocks_across, COARSE).sum(axis=2)
    c_south = south[COARSE - 1::COARSE, :].reshape(blocks_down, blocks_across, COARSE).sum(axis=2)
    c_diag = COARSE * COARSE * jnp.square(jnp.sum(kernel)) + c_east + c_west + c_north + c_south
    return jnp.stack([c_east, c_west, c_north, c_south, c_diag])


def jacobi(source, coarse_table, widen):
    c_east, c_west, c_north, c_south, c_diag = coarse_table[0], coarse_table[1], coarse_table[2], coarse_table[3], coarse_table[4]
    iterate = OMEGA * source / c_diag
    for repeat in range(SWEEPS - 1):
        padded = widen(iterate)
        applied = (c_diag * iterate - c_east * padded[1:-1, 2:] - c_west * padded[1:-1, :-2]
                   - c_north * padded[:-2, 1:-1] - c_south * padded[2:, 1:-1])
        iterate = iterate + OMEGA * (source - applied) / c_diag
    return iterate


def pad_zero(field):
    return jnp.pad(field, 1)


def reference(observed, class_map, class_weights, blur_kernel):
    conductance = jnp.zeros(observed.shape, jnp.float32)
    for class_id in range(CLASSES):
        conductance = conductance + jnp.where(class_map == class_id, class_weights[class_id], 0.0)
    edge_set = edge_weights(jnp.pad(conductance, 1))
    right_side = adjoint(jnp.pad(observed, 1), blur_kernel)
    fine_diag = jnp.sum(blur_kernel * blur_kernel) + edge_set[0] + edge_set[1] + edge_set[2] + edge_set[3]
    coarse_table = coarse_weights(edge_set, blur_kernel)
    blocks_down = HEIGHT // COARSE
    blocks_across = BAND_LEN // COARSE

    def precondition(residual):
        source = residual.reshape(blocks_down, COARSE, blocks_across, COARSE).sum(axis=(1, 3))
        coarse = jacobi(source, coarse_table, pad_zero)
        spread = jnp.broadcast_to(coarse[:, None, :, None], (blocks_down, COARSE, blocks_across, COARSE))
        return residual / fine_diag + spread.reshape(HEIGHT, BAND_LEN)

    def apply_operator(field):
        padded = jnp.pad(field, 1)
        image = blurred(padded, blur_kernel)
        return adjoint(jnp.pad(image, 1), blur_kernel) + laplace(padded, edge_set)

    solution = jnp.zeros(observed.shape, jnp.float32)
    residual = right_side
    precond = precondition(residual)
    gamma_now = jnp.sum(residual * precond)
    direction = precond
    for iteration in range(ITERS):
        product_field = apply_operator(direction)
        step_size = gamma_now / jnp.sum(direction * product_field)
        solution = solution + step_size * direction
        residual = residual - step_size * product_field
        if iteration + 1 < ITERS:
            precond = precondition(residual)
            gamma_next = jnp.sum(residual * precond)
            direction = precond + (gamma_next / gamma_now) * direction
            gamma_now = gamma_next
    return solution, residual
```

```python
import functools

import jax
import jax.numpy as jnp
from jax import lax
from jax.experimental import pallas as pl
from jax.experimental.pallas import tpu as pltpu
from jax.sharding import PartitionSpec as P

MESH = pl.DeviceIdType.MESH
OMEGA = 0.8
SWEEPS = 8
NB = ((-1, 0), (1, 0), (0, -1), (0, 1), (-1, -1), (-1, 1), (1, -1), (1, 1))
F32 = jnp.float32
BF16 = jnp.bfloat16


def split2(x):
    hi = x.astype(BF16)
    lo = (x - hi.astype(F32)).astype(BF16)
    return hi, lo


def kernel(
    n_rows, n_cols, zk,
    cw, bk, obs_hbm, cls_hbm, sol_hbm, res_hbm,
    obs, cls, cond, r0, rfd, ce, cs, d0, img, q0, w, lw, sol, res,
    zup, cmat, umat, tbuf, tt0, tt1, tt2, hbuf, ctab, zs,
    sn0, ss0, rn0, rs0, rx0, sn1, rn1, rs1, rx1, sn2, ss2, rn2, rs2, rx2,
    red0, red1, redx, redy,
    in_sem, out_sem, send_sem, recv_sem, rsend, rrecv,
):
    r = lax.axis_index("rows")
    c = lax.axis_index("cols")
    ny = n_cols // zk
    y, k8 = c // zk, lax.rem(c, zk)

    def ok(dr, dc):
        return (r + dr >= 0) & (r + dr < n_rows) & (c + dc >= 0) & (c + dc < n_cols)

    def dev(dr, dc):
        return (c + dc, r + dr)

    loads = []
    for t in range(8):
        lanes = pl.ds(t * 128, 128)
        loads.append(pltpu.make_async_copy(cls_hbm.at[:, lanes], cls.at[t], in_sem.at[t]))
        loads.append(pltpu.make_async_copy(
            obs_hbm.at[:, lanes], obs.at[t, pl.ds(16, 256), :], in_sem.at[8 + t]))
    for x in loads:
        x.start()

    for buf in (rn0, rs0, rx0, rn1, rs1, rx1, rn2, rs2, rx2, hbuf, zs):
        buf[...] = jnp.zeros(buf.shape, F32)

    bar = pltpu.get_barrier_semaphore()
    peers = zk + n_rows * ny - 2
    for dr, dc in NB:
        if dc == 0:
            continue
        fresh = ok(dr, dc)
        if dr == 0:
            fresh = fresh & (k8 == (zk - 1 if dc > 0 else 0))
        peers = peers + fresh.astype(jnp.int32)

        @pl.when(fresh)
        def _():
            pl.semaphore_signal(bar, inc=1, device_id=dev(dr, dc), device_id_type=MESH)
    zk_group = [(y * zk + i, r) for i in range(zk)]
    xy_me = r * ny + y
    xy_group = [(j * zk + k8, i) for i in range(n_rows) for j in range(ny)]
    for i in range(zk):
        @pl.when(k8 != i)
        def _():
            pl.semaphore_signal(bar, inc=1, device_id=zk_group[i], device_id_type=MESH)
    for i in range(n_rows * ny):
        @pl.when(xy_me != i)
        def _():
            pl.semaphore_signal(bar, inc=1, device_id=xy_group[i], device_id_type=MESH)

    lane = lax.broadcasted_iota(jnp.int32, (8, 128), 1)
    sub = lax.broadcasted_iota(jnp.int32, (8, 128), 0)
    first_lane = lane == 0
    last_lane = lane == 127

    ii = lax.broadcasted_iota(jnp.int32, (1024, 128), 0)
    jj = lax.broadcasted_iota(jnp.int32, (1024, 128), 1)
    cmat[:, 0:128] = jnp.where(ii // 8 == jj, 1.0, 0.0).astype(BF16)
    cmat[:, 128:256] = jnp.where(ii == jj * 8 + 7, 1.0, 0.0).astype(BF16)
    ui = lax.broadcasted_iota(jnp.int32, (128, 1024), 0)
    uj = lax.broadcasted_iota(jnp.int32, (128, 1024), 1)
    umat[:, 0:1024] = jnp.where(uj // 8 == ui, 1.0, 0.0).astype(BF16)
    vi = lax.broadcasted_iota(jnp.int32, (128, 128), 0)
    vj = lax.broadcasted_iota(jnp.int32, (128, 128), 1)
    umat[:, 1024:1152] = jnp.where(
        ((vj < 64) & (vi == 0)) | ((vj >= 64) & (vi == 127)), 1.0, 0.0).astype(BF16)

    kk = [[bk[a * 3 + b] for b in range(3)] for a in range(3)]
    ksum = kk[0][0]
    ksq = kk[0][0] * kk[0][0]
    for a in range(3):
        for b in range(3):
            if a + b:
                ksum = ksum + kk[a][b]
                ksq = ksq + kk[a][b] * kk[a][b]

    def sh_east(v):
        rolled = [pltpu.roll(x, 127, 1) for x in v]
        n = len(v)
        return [jnp.where(last_lane, rolled[(t + 1) % n], rolled[t]) for t in range(n)]

    def sh_west(v):
        rolled = [pltpu.roll(x, 1, 1) for x in v]
        n = len(v)
        return [jnp.where(first_lane, rolled[(t - 1) % n], rolled[t]) for t in range(n)]

    def rows_of(ref, base, n=9):
        return [ref[t, pl.ds(base, 8), :] for t in range(n)]

    for x in loads:
        x.wait()

    w0, w1, w2, w3 = cw[0], cw[1], cw[2], cw[3]

    def cond_body(i, _):
        src = pl.multiple_of(i * 8, 8)
        dst = pl.multiple_of(i * 8 + 16, 8)
        for t in range(8):
            m = cls[t, pl.ds(src, 8), :]
            cond[t, pl.ds(dst, 8), :] = jnp.where(
                m == 0, w0, jnp.where(m == 1, w1, jnp.where(m == 2, w2, w3)))
        return 0

    lax.fori_loop(0, 32, cond_body, 0)

    for t in range(8):
        sn0[t] = jnp.where(sub < 4, obs[t, 16:24, :], pltpu.roll(cond[t, 16:24, :], 4, 0))
        ss0[t] = jnp.where(sub >= 4, obs[t, 264:272, :], pltpu.roll(cond[t, 264:272, :], 4, 0))

    def rim_tile(start, n):
        lanes = lax.broadcasted_iota(jnp.int32, (n, 128), 1)
        rows = pl.ds(start, n)
        left = jnp.where(lanes < 4, obs[0, rows, :], pltpu.roll(cond[0, rows, :], 4, 1))
        right = jnp.where(lanes >= 124, obs[7, rows, :], pltpu.roll(cond[7, rows, :], 124, 1))
        return jnp.where(lanes < 64, left, right)

    tt0[0] = rim_tile(16, 128).T
    tt0[1] = rim_tile(144, 128).T
    tbuf[...] = jnp.zeros(tbuf.shape, F32)
    tbuf[64:72, :] = rim_tile(264, 8)
    tbuf[72:80, :] = rim_tile(16, 8)
    tt0[2] = tbuf[...].T

    def side_copies(tt, rx, groups_diag):
        low, high = pl.ds(0, 8), pl.ds(120, 8)
        out = []
        for n, (dr, dc) in enumerate(NB):
            if dc == 0:
                continue
            groups = pl.ds(0, 3) if dr == 0 else groups_diag
            rows = low if dc < 0 else high
            out.append((n, tt.at[groups, rows, :], rx.at[n, groups]))
        return out

    def start_all(phase, copies):
        for n, src, dst in copies:
            dr, dc = NB[n]
            @pl.when(ok(dr, dc))
            def _():
                pltpu.make_async_remote_copy(
                    src, dst, send_sem.at[phase, n], recv_sem.at[phase, n],
                    device_id=dev(dr, dc), device_id_type=MESH).start()

    def wait_recv_all(phase, copies):
        for n, src, dst in copies:
            dr, dc = NB[n]
            @pl.when(ok(-dr, -dc))
            def _():
                pltpu.make_async_remote_copy(
                    src, dst, send_sem.at[phase, n], recv_sem.at[phase, n],
                    device_id=dev(-dr, -dc), device_id_type=MESH).wait_recv()

    def wait_send_all(phase, copies):
        for n, src, dst in copies:
            dr, dc = NB[n]
            @pl.when(ok(dr, dc))
            def _():
                pltpu.make_async_remote_copy(
                    src, dst, send_sem.at[phase, n], recv_sem.at[phase, n],
                    device_id=dev(dr, dc), device_id_type=MESH).wait_send()

    third = pl.ds(2, 1)
    copies0 = [(0, sn0, rs0), (1, ss0, rn0)] + side_copies(tt0, rx0, third)

    pl.semaphore_wait(bar, peers)

    start_all(0, copies0)
    wait_recv_all(0, copies0)

    def side(rx, group, dc, in_north, in_center):
        north = rx[NB.index((1, dc)), group]
        center = rx[NB.index((0, dc)), group]
        south = rx[NB.index((-1, dc)), group]
        return jnp.where(in_north, north, jnp.where(in_center, center, south))

    fine_north = (lane < 8) | ((lane >= 64) & (lane < 72))
    fine_center = (lane >= 8) & (lane < 40)
    lane64 = lax.rem(lane, 64)

    def unpack_fine(rx):
        for dc, rows in ((-1, slice(0, 8)), (1, slice(120, 128))):
            here = NB.index((0, dc))
            hbuf[0, rows, :] = rx[here, 0]
            hbuf[1, rows, :] = rx[here, 1]
            hbuf[2, rows, :] = side(rx, 2, dc, fine_north, fine_center)

    unpack_fine(rx0)

    def cond_of(x):
        lanes = lax.broadcasted_iota(jnp.int32, x.shape, 1)
        return jnp.where(lanes < 64, pltpu.roll(x, 124, 1), pltpu.roll(x, 4, 1))

    for g in range(2):
        tile = hbuf[g].T
        rows = slice(16 + 128 * g, 144 + 128 * g)
        obs[8, rows, :] = tile
        cond[8, rows, :] = cond_of(tile)
    tile = hbuf[2].T
    for rows, lo in ((slice(8, 16), 64), (slice(272, 280), 72)):
        obs[8, rows, :] = tile[lo:lo + 8]
        cond[8, rows, :] = cond_of(tile[lo:lo + 8])
    for t in range(8):
        obs[t, 8:16, :] = rn0[t]
        cond[t, 8:16, :] = pltpu.roll(rn0[t], 4, 0)
        obs[t, 272:280, :] = rs0[t]
        cond[t, 272:280, :] = pltpu.roll(rs0[t], 4, 0)

    def fine_body(i, _):
        base = pl.multiple_of(i * 8 + 8, 8)
        up, mid, down = rows_of(obs, base - 1), rows_of(obs, base), rows_of(obs, base + 1)
        v = [[kk[0][b] * down[t] + kk[1][b] * mid[t] + kk[2][b] * up[t] for t in range(9)]
             for b in range(3)]
        e0, w2_ = sh_east(v[0]), sh_west(v[2])
        for t in range(9):
            r0[t, pl.ds(base, 8), :] = v[1][t] + e0[t] + w2_[t]
        return 0

    lax.fori_loop(0, 34, fine_body, 0)

    def edge_body(i, _):
        base = pl.multiple_of(i * 8 + 8, 8)
        north, mid, south = rows_of(cond, base - 1), rows_of(cond, base), rows_of(cond, base + 1)
        east, west = sh_east(mid), sh_west(mid)
        for t in range(9):
            here = pl.ds(base, 8)
            total = (east[t] + west[t]) + (north[t] + south[t])
            rfd[t, here, :] = 1.0 / (ksq + 2.0 * mid[t] + 0.5 * total)
            ce[t, here, :] = 0.5 * (mid[t] + east[t])
            cs[t, here, :] = 0.5 * (mid[t] + south[t])
        return 0

    lax.fori_loop(0, 34, edge_body, 0)

    def clear_outside(ref):
        @pl.when(r == 0)
        def _():
            for t in range(9):
                ref[t, 8:16, :] = jnp.zeros((8, 128), F32)

        @pl.when(r == n_rows - 1)
        def _():
            for t in range(9):
                ref[t, 272:280, :] = jnp.zeros((8, 128), F32)

        lanes = lax.broadcasted_iota(jnp.int32, (272, 128), 1)

        @pl.when(c == 0)
        def _():
            ref[8, 8:280, :] = jnp.where(lanes < 64, ref[8, 8:280, :], 0.0)

        @pl.when(c == n_cols - 1)
        def _():
            ref[8, 8:280, :] = jnp.where(lanes >= 64, ref[8, 8:280, :], 0.0)

    clear_outside(rfd)

    def row_sums(ref, t):
        total = ref[t, pl.ds(16, 32, stride=8), :]
        for s in range(1, 8):
            total = total + ref[t, pl.ds(16 + s, 32, stride=8), :]
        return total

    src = jnp.concatenate([row_sums(r0, t) for t in range(8)], axis=1)
    esum = jnp.concatenate([row_sums(ce, t) for t in range(8)], axis=1)
    srow = jnp.concatenate([cs[t, pl.ds(23, 32, stride=8), :] for t in range(8)], axis=1)
    nrow = jnp.concatenate([cs[t, 8:16, :] for t in range(8)], axis=1)
    stack = jnp.concatenate([src, esum, srow, nrow], axis=0)
    hi, lo = split2(stack)
    sums = jnp.dot(hi, cmat[...], preferred_element_type=F32) + jnp.dot(
        lo, cmat[...], preferred_element_type=F32)
    source = sums[0:32, 0:128]
    c_east = sums[32:64, 128:256]
    c_south = sums[64:96, 0:128]
    outer = row_sums(ce, 8)
    lane32 = lax.broadcasted_iota(jnp.int32, (32, 128), 1)
    c_west = jnp.where(lane32 == 0, pltpu.roll(outer, 1, 1), pltpu.roll(c_east, 1, 1))
    zs[0, 0:8, :] = sums[96:104, 0:128]
    zs[0, 8:40, :] = c_south
    c_north = zs[0, 7:39, :]
    zs[...] = jnp.zeros(zs.shape, F32)
    c_diag = 64.0 * (ksum * ksum) + c_east + c_west + c_north + c_south
    scale = OMEGA / c_diag
    fields = (source * scale, c_east * scale, c_west * scale, c_north * scale, c_south * scale)
    ctab[5, 0, 8:40, :] = scale
    for f in range(5):
        ctab[f, 0, 8:40, :] = fields[f]
        sn1[f] = fields[f]
    for g in range(3):
        for h in range(2):
            f = 2 * g + h
            if f < 5:
                tbuf[64 * h:64 * h + 8, :] = fields[f][24:32]
                tbuf[64 * h + 8:64 * h + 40, :] = fields[f]
                tbuf[64 * h + 40:64 * h + 48, :] = fields[f][0:8]
        tt1[g] = tbuf[...].T

    whole = pl.ds(0, 3)
    copies1 = [(0, sn1.at[:, pl.ds(0, 8), :], rs1), (1, sn1.at[:, pl.ds(24, 8), :], rn1)]
    copies1 += side_copies(tt1, rx1, whole)
    start_all(1, copies1)
    wait_recv_all(1, copies1)

    for f in range(5):
        ctab[f, 0, 0:8, :] = rn1[f]
        ctab[f, 0, 40:48, :] = rs1[f]
    for g in range(3):
        for dc, rows in ((-1, slice(0, 8)), (1, slice(120, 128))):
            hbuf[g, rows, :] = side(rx1, g, dc, lane64 < 8, lane64 < 40)
        tile = hbuf[g].T
        for h in range(2):
            f = 2 * g + h
            if f < 5:
                ctab[f, 1, :, :] = tile[64 * h:64 * h + 48]

    lane48 = lax.broadcasted_iota(jnp.int32, (48, 128), 1)
    last48, first48 = lane48 == 127, lane48 == 0

    def sweep(_, carry):
        z = [zs[t, 8:56, :] for t in range(2)]
        east = [pltpu.roll(x, 127, 1) for x in z]
        west = [pltpu.roll(x, 1, 1) for x in z]
        new = []
        for t in range(2):
            ze = jnp.where(last48, east[1 - t], east[t])
            zw = jnp.where(first48, west[1 - t], west[t])
            zn, zso = zs[t, 7:55, :], zs[t, 9:57, :]
            new.append((ctab[0, t] + (1.0 - OMEGA) * z[t])
                       + (ctab[1, t] * ze + ctab[2, t] * zw)
                       + (ctab[3, t] * zn + ctab[4, t] * zso))
        for t in range(2):
            zs[t, 8:56, :] = new[t]
        return carry

    def jacobi():
        for t in range(2):
            zs[t, 8:56, :] = ctab[0, t]
        lax.fori_loop(0, SWEEPS - 1, sweep, 0)
        hi0, lo0 = split2(zs[0, 8:56, :])
        hi1, lo1 = split2(zs[1, 8:56, :])
        up = jnp.dot(hi0, umat[:, 0:1024], preferred_element_type=F32) + jnp.dot(
            lo0, umat[:, 0:1024], preferred_element_type=F32)
        for t in range(8):
            zup[t] = up[:, 128 * t:128 * t + 128]
        zup[8] = jnp.dot(hi1, umat[:, 1024:1152], preferred_element_type=F32) + jnp.dot(
            lo1, umat[:, 1024:1152], preferred_element_type=F32)

    jacobi()

    def precond(field, out):
        def body(i, _):
            base = pl.multiple_of(i * 8 + 8, 8)
            here = pl.ds(base, 8)
            for t in range(9):
                out[t, here, :] = field[t, here, :] * rfd[t, here, :] + zup[t, pl.ds(i + 7, 1), :]
            return 0

        lax.fori_loop(0, 34, body, 0)

    precond(r0, d0)

    def blur_rows(ref, base):
        up, mid, down = rows_of(ref, base - 1), rows_of(ref, base), rows_of(ref, base + 1)
        u = [[kk[0][b] * up[t] + kk[1][b] * mid[t] + kk[2][b] * down[t] for t in range(9)]
             for b in range(3)]
        w_, e_ = sh_west(u[0]), sh_east(u[2])
        return [u[1][t] + w_[t] + e_[t] for t in range(9)], up, mid, down

    def blur0(i, _):
        base = pl.multiple_of(i * 8 + 8, 8)
        out, _, _, _ = blur_rows(d0, base)
        for t in range(9):
            img[t, pl.ds(base, 8), :] = out[t]
        return 0

    lax.fori_loop(0, 34, blur0, 0)
    clear_outside(img)

    def adjoint_parts(base):
        up, mid, down = rows_of(img, base - 1), rows_of(img, base), rows_of(img, base + 1)
        return [[kk[0][b] * down[t] + kk[1][b] * mid[t] + kk[2][b] * up[t] for t in range(9)]
                for b in range(3)]

    zero = jnp.zeros((8, 128), F32)

    def apply0(i, carry):
        gam, dad = carry
        base = pl.multiple_of(i * 8 + 16, 8)
        v = adjoint_parts(base)
        up, mid, down = rows_of(d0, base - 1), rows_of(d0, base), rows_of(d0, base + 1)
        east = sh_east(mid)
        flux = [ce[t, pl.ds(base, 8), :] * (mid[t] - east[t]) for t in range(9)]
        e0 = sh_east(v[0])
        w2_ = sh_west([v[2][t] - flux[t] for t in range(9)])
        for t in range(8):
            lap = (cs[t, pl.ds(base, 8), :] * (mid[t] - down[t])
                   - cs[t, pl.ds(base - 1, 8), :] * (up[t] - mid[t]))
            out = ((v[1][t] + e0[t]) + (w2_[t] + flux[t])) + lap
            q0[t, pl.ds(base, 8), :] = out
            gam = gam + r0[t, pl.ds(base, 8), :] * mid[t]
            dad = dad + mid[t] * out
        return gam, dad

    gam, dad = lax.fori_loop(0, 32, apply0, (zero, zero))

    src = jnp.concatenate([row_sums(q0, t) for t in range(8)], axis=1)
    hi, lo = split2(src)
    cells = jnp.dot(hi, cmat[:, 0:128], preferred_element_type=F32) + jnp.dot(
        lo, cmat[:, 0:128], preferred_element_type=F32)
    b2 = cells * ctab[5, 0, 8:40, :]
    ctab[0, 0, 8:40, :] = b2

    def q_tile(start, n):
        lanes = lax.broadcasted_iota(jnp.int32, (n, 128), 1)
        rows = pl.ds(start, n)
        return jnp.where(lanes < 64, q0[0, rows, :], q0[7, rows, :])

    tt2[0] = q_tile(16, 128).T
    tt2[1] = q_tile(144, 128).T
    tbuf[0:8, :] = b2[24:32]
    tbuf[8:40, :] = b2
    tbuf[40:48, :] = b2[0:8]
    tbuf[64:72, :] = q_tile(264, 8)
    tbuf[72:80, :] = q_tile(16, 8)
    tt2[2] = tbuf[...].T
    for t in range(8):
        sn2[t] = q0[t, 16:24, :]
        ss2[t] = q0[t, 264:272, :]
    sn2[8] = b2[0:8]
    ss2[8] = b2[24:32]
    copies2 = [(0, sn2, rs2), (1, ss2, rn2)] + side_copies(tt2, rx2, third)
    start_all(2, copies2)
    wait_recv_all(2, copies2)

    unpack_fine(rx2)
    for g in range(2):
        q0[8, 16 + 128 * g:144 + 128 * g, :] = hbuf[g].T
    tile = hbuf[2].T
    q0[8, 8:16, :] = tile[64:72]
    q0[8, 272:280, :] = tile[72:80]
    ctab[0, 1, :, :] = tile[0:48]
    for t in range(8):
        q0[t, 8:16, :] = rn2[t]
        q0[t, 272:280, :] = rs2[t]
    ctab[0, 0, 0:8, :] = rn2[8]
    ctab[0, 0, 40:48, :] = rs2[8]
    jacobi()
    precond(q0, w)

    def blur1_rim(base):
        out, _, _, _ = blur_rows(w, base)
        for t in range(9):
            img[t, pl.ds(base, 8), :] = out[t]

    def blur1(i, carry):
        qw, waw = carry
        base = pl.multiple_of(i * 8 + 16, 8)
        out, up, mid, down = blur_rows(w, base)
        east = sh_east(mid)
        flux = [ce[t, pl.ds(base, 8), :] * (mid[t] - east[t]) for t in range(9)]
        fw = sh_west(flux)
        img[8, pl.ds(base, 8), :] = out[8]
        for t in range(8):
            lap = (cs[t, pl.ds(base, 8), :] * (mid[t] - down[t])
                   - cs[t, pl.ds(base - 1, 8), :] * (up[t] - mid[t]))
            lap = lap + (flux[t] - fw[t])
            img[t, pl.ds(base, 8), :] = out[t]
            lw[t, pl.ds(base, 8), :] = lap
            qw = qw + q0[t, pl.ds(base, 8), :] * mid[t]
            waw = waw + (out[t] * out[t] + mid[t] * lap)
        return qw, waw

    blur1_rim(8)
    blur1_rim(272)
    qw, waw = lax.fori_loop(0, 32, blur1, (zero, zero))

    for n, part in enumerate((gam, dad, qw, waw)):
        red0[n:n + 1, :] = jnp.sum(part, axis=0, keepdims=True)
    red0[4:8, :] = jnp.zeros((4, 128), F32)
    redx[k8] = red0[...]
    for i in range(zk):
        @pl.when(k8 != i)
        def _():
            pltpu.make_async_remote_copy(
                red0, redx.at[k8], rsend.at[0], rrecv.at[0],
                device_id=zk_group[i], device_id_type=MESH).start()
    clear_outside(img)

    def apply1(i, _):
        base = pl.multiple_of(i * 8 + 16, 8)
        v = adjoint_parts(base)
        e0, w2_ = sh_east(v[0]), sh_west(v[2])
        for t in range(8):
            here = pl.ds(base, 8)
            lw[t, here, :] = ((v[1][t] + e0[t]) + w2_[t]) + lw[t, here, :]
        return 0

    def all_bytes(buf, n, sem):
        return pltpu.make_async_copy(buf.at[pl.ds(0, n)], buf.at[pl.ds(0, n)], sem)

    all_bytes(redx, zk - 1, rrecv.at[0]).wait()
    total = redx[0]
    for i in range(1, zk):
        total = total + redx[i]
    red1[...] = total
    redy[xy_me] = total
    for i in range(n_rows * ny):
        @pl.when(xy_me != i)
        def _():
            pltpu.make_async_remote_copy(
                red1, redy.at[xy_me], rsend.at[1], rrecv.at[1],
                device_id=xy_group[i], device_id_type=MESH).start()
    lax.fori_loop(0, 32, apply1, 0)
    all_bytes(redy, n_rows * ny - 1, rrecv.at[1]).wait()
    total = redy[0]
    for i in range(1, n_rows * ny):
        total = total + redy[i]
    value = jnp.broadcast_to(jnp.sum(total, axis=1, keepdims=True), (8, 128))
    g0 = jnp.broadcast_to(value[0:1], (8, 128))
    dq = jnp.broadcast_to(value[1:2], (8, 128))
    qws = jnp.broadcast_to(value[2:3], (8, 128))
    ws = jnp.broadcast_to(value[3:4], (8, 128))
    alpha = g0 / dq
    g1 = (g0 - alpha * dq) + alpha * (alpha * qws - dq)
    beta1 = 1.0 + g1 / g0
    dad1 = beta1 * (beta1 * dq - alpha * qws) + alpha * (alpha * ws - beta1 * qws)
    step = g1 / dad1
    ca = alpha + step * beta1
    cb = alpha * step

    stores = []
    for t in range(8):
        def finish(i, _):
            src_rows = pl.ds(pl.multiple_of(i * 8 + 16, 8), 8)
            dst_rows = pl.ds(pl.multiple_of(i * 8, 8), 8)
            sol[t, dst_rows, :] = ca * d0[t, src_rows, :] - cb * w[t, src_rows, :]
            res[t, dst_rows, :] = (r0[t, src_rows, :] - ca * q0[t, src_rows, :]) + cb * lw[t, src_rows, :]
            return 0

        lax.fori_loop(0, 32, finish, 0, unroll=4)
        lanes = pl.ds(t * 128, 128)
        stores.append(pltpu.make_async_copy(sol.at[t], sol_hbm.at[:, lanes], out_sem.at[t]))
        stores.append(pltpu.make_async_copy(res.at[t], res_hbm.at[:, lanes], out_sem.at[8 + t]))
        stores[-2].start()
        stores[-1].start()

    wait_send_all(0, copies0)
    wait_send_all(1, copies1)
    wait_send_all(2, copies2)
    all_bytes(redx, zk - 1, rsend.at[0]).wait()
    all_bytes(redy, n_rows * ny - 1, rsend.at[1]).wait()
    for x in stores:
        x.wait()


def body(n_rows, n_cols, observed, class_map, class_weights, blur_kernel):
    zk = min(8, n_cols)
    ny = n_cols // zk
    big = pltpu.VMEM((9, 288, 128), F32)
    half = pltpu.VMEM((8, 256, 128), F32)

    def v(*shape):
        return pltpu.VMEM(shape, F32)

    scratch = [
        big, pltpu.VMEM((8, 256, 128), jnp.int32), big, big, big, big, big, big, big, big, big, big,
        half, half,
        v(9, 48, 128), pltpu.VMEM((1024, 256), BF16), pltpu.VMEM((128, 1152), BF16),
        v(128, 128), v(3, 128, 128), v(3, 128, 128), v(3, 128, 128), v(3, 128, 128),
        v(6, 2, 48, 128), v(2, 64, 128),
        v(8, 8, 128), v(8, 8, 128), v(8, 8, 128), v(8, 8, 128), v(8, 3, 8, 128),
        v(5, 32, 128), v(5, 8, 128), v(5, 8, 128), v(8, 3, 8, 128),
        v(9, 8, 128), v(9, 8, 128), v(9, 8, 128), v(9, 8, 128), v(8, 3, 8, 128),
        v(8, 128), v(8, 128), v(zk, 8, 128), v(n_rows * ny, 8, 128),
        pltpu.SemaphoreType.DMA((16,)), pltpu.SemaphoreType.DMA((16,)),
        pltpu.SemaphoreType.DMA((3, 8)), pltpu.SemaphoreType.DMA((3, 8)),
        pltpu.SemaphoreType.DMA((2,)), pltpu.SemaphoreType.DMA((2,)),
    ]
    anywhere = pl.BlockSpec(memory_space=pl.ANY)
    scalars = pl.BlockSpec(memory_space=pltpu.SMEM)
    shape = jax.ShapeDtypeStruct(observed.shape, F32)
    return pl.pallas_call(
        functools.partial(kernel, n_rows, n_cols, zk),
        out_shape=(shape, shape),
        in_specs=[scalars, scalars, anywhere, anywhere],
        out_specs=(anywhere, anywhere),
        scratch_shapes=scratch,
        compiler_params=pltpu.CompilerParams(
            collective_id=0, has_side_effects=True, vmem_limit_bytes=40 * 2**20),
    )(class_weights, blur_kernel.reshape(9), observed, class_map)


def solution(mesh):
    n_rows, n_cols = mesh.shape["rows"], mesh.shape["cols"]
    return jax.shard_map(
        functools.partial(body, n_rows, n_cols),
        mesh=mesh,
        in_specs=(P("rows", "cols"), P("rows", "cols"), P(), P()),
        out_specs=(P("rows", "cols"), P("rows", "cols")),
        check_vma=False,
    )
```

```python
import functools

import jax
import jax.numpy as jnp
from jax import lax
from jax.experimental import pallas as pl
from jax.experimental.pallas import tpu as pltpu
from jax.sharding import PartitionSpec as P

MESH = pl.DeviceIdType.MESH
OMEGA = 0.8
SWEEPS = 8
NB = ((-1, 0), (1, 0), (0, -1), (0, 1), (-1, -1), (-1, 1), (1, -1), (1, 1))
F32 = jnp.float32
BF16 = jnp.bfloat16
KERNEL_VMEM = 55 * 2**20
FINISH_VMEM = 16 * 2**20


def exact_dot(x, ones):
    hi = x.astype(BF16)
    lo = (x - hi.astype(F32)).astype(BF16)
    both = jnp.dot(jnp.concatenate([hi, lo], axis=0), ones, preferred_element_type=F32)
    return both[: x.shape[0]] + both[x.shape[0] :]


def kernel(
    n_rows, n_cols, zk,
    cw, bk, obs_hbm, cls_hbm, r0, d0, q0, w, lw, coef,
    obs, cls, cond, rfd, ce, cs, img,
    zup, cmat, umat, tbuf, tt0, tt1, tt2, hbuf, ctab, zs,
    sn0, ss0, rn0, rs0, rx0, sn1, rn1, rs1, rx1, sn2, ss2, rn2, rs2, rx2,
    red0, red1, redx, redy,
    in_sem, send_sem, recv_sem, rsend, rrecv,
):
    r = lax.axis_index("rows")
    c = lax.axis_index("cols")
    ny = n_cols // zk
    y, k8 = c // zk, lax.rem(c, zk)

    def ok(dr, dc):
        return (r + dr >= 0) & (r + dr < n_rows) & (c + dc >= 0) & (c + dc < n_cols)

    def dev(dr, dc):
        return (c + dc, r + dr)

    loads = []
    for t in range(8):
        lanes = pl.ds(t * 128, 128)
        loads.append(pltpu.make_async_copy(cls_hbm.at[:, lanes], cls.at[t], in_sem.at[t]))
        loads.append(pltpu.make_async_copy(
            obs_hbm.at[:, lanes], obs.at[t, pl.ds(16, 256), :], in_sem.at[8 + t]))
    for x in loads:
        x.start()

    for buf in (rn0, rs0, rx0, rn1, rs1, rx1, rn2, rs2, rx2, hbuf, zs):
        buf[...] = jnp.zeros(buf.shape, F32)

    bar = pltpu.get_barrier_semaphore()
    peers = zk + n_rows * ny - 2
    for dr, dc in NB:
        if dc == 0:
            continue
        fresh = ok(dr, dc)
        if dr == 0:
            fresh = fresh & (k8 == (zk - 1 if dc > 0 else 0))
        peers = peers + fresh.astype(jnp.int32)

        @pl.when(fresh)
        def _():
            pl.semaphore_signal(bar, inc=1, device_id=dev(dr, dc), device_id_type=MESH)
    zk_group = [(y * zk + i, r) for i in range(zk)]
    xy_me = r * ny + y
    xy_group = [(j * zk + k8, i) for i in range(n_rows) for j in range(ny)]
    for i in range(zk):
        @pl.when(k8 != i)
        def _():
            pl.semaphore_signal(bar, inc=1, device_id=zk_group[i], device_id_type=MESH)
    for i in range(n_rows * ny):
        @pl.when(xy_me != i)
        def _():
            pl.semaphore_signal(bar, inc=1, device_id=xy_group[i], device_id_type=MESH)

    lane = lax.broadcasted_iota(jnp.int32, (8, 128), 1)
    sub = lax.broadcasted_iota(jnp.int32, (8, 128), 0)
    first_lane = lane == 0
    last_lane = lane == 127

    ii = lax.broadcasted_iota(jnp.int32, (1024, 128), 0)
    jj = lax.broadcasted_iota(jnp.int32, (1024, 128), 1)
    cmat[:, 0:128] = jnp.where(ii // 8 == jj, 1.0, 0.0).astype(BF16)
    cmat[:, 128:256] = jnp.where(ii == jj * 8 + 7, 1.0, 0.0).astype(BF16)
    ui = lax.broadcasted_iota(jnp.int32, (128, 1024), 0)
    uj = lax.broadcasted_iota(jnp.int32, (128, 1024), 1)
    umat[:, 0:1024] = jnp.where(uj // 8 == ui, 1.0, 0.0).astype(BF16)
    vi = lax.broadcasted_iota(jnp.int32, (128, 128), 0)
    vj = lax.broadcasted_iota(jnp.int32, (128, 128), 1)
    umat[:, 1024:1152] = jnp.where(
        ((vj < 64) & (vi == 0)) | ((vj >= 64) & (vi == 127)), 1.0, 0.0).astype(BF16)

    kk = [[bk[a, b] for b in range(3)] for a in range(3)]
    ksum = kk[0][0]
    ksq = kk[0][0] * kk[0][0]
    for a in range(3):
        for b in range(3):
            if a + b:
                ksum = ksum + kk[a][b]
                ksq = ksq + kk[a][b] * kk[a][b]

    def sh_east(v):
        rolled = [pltpu.roll(x, 127, 1) for x in v]
        n = len(v)
        return [jnp.where(last_lane, rolled[(t + 1) % n], rolled[t]) for t in range(n)]

    def sh_west(v):
        rolled = [pltpu.roll(x, 1, 1) for x in v]
        n = len(v)
        return [jnp.where(first_lane, rolled[(t - 1) % n], rolled[t]) for t in range(n)]

    def rows_of(ref, base, n=9):
        return [ref[t, pl.ds(base, 8), :] for t in range(n)]

    for x in loads:
        x.wait()

    w0, w1, w2, w3 = cw[0], cw[1], cw[2], cw[3]

    def cond_body(i, _):
        src = pl.multiple_of(i * 8, 8)
        dst = pl.multiple_of(i * 8 + 16, 8)
        for t in range(8):
            m = cls[t, pl.ds(src, 8), :]
            cond[t, pl.ds(dst, 8), :] = jnp.where(
                m == 0, w0, jnp.where(m == 1, w1, jnp.where(m == 2, w2, w3)))
        return 0

    lax.fori_loop(0, 32, cond_body, 0)

    for t in range(8):
        sn0[t] = jnp.where(sub < 4, obs[t, 16:24, :], pltpu.roll(cond[t, 16:24, :], 4, 0))
        ss0[t] = jnp.where(sub >= 4, obs[t, 264:272, :], pltpu.roll(cond[t, 264:272, :], 4, 0))

    def rim_tile(start, n):
        lanes = lax.broadcasted_iota(jnp.int32, (n, 128), 1)
        rows = pl.ds(start, n)
        left = jnp.where(lanes < 4, obs[0, rows, :], pltpu.roll(cond[0, rows, :], 4, 1))
        right = jnp.where(lanes >= 124, obs[7, rows, :], pltpu.roll(cond[7, rows, :], 124, 1))
        return jnp.where(lanes < 64, left, right)

    tt0[0] = rim_tile(16, 128).T
    tt0[1] = rim_tile(144, 128).T
    tbuf[...] = jnp.zeros(tbuf.shape, F32)
    tbuf[64:72, :] = rim_tile(264, 8)
    tbuf[72:80, :] = rim_tile(16, 8)
    tt0[2] = tbuf[...].T

    def side_copies(tt, rx, groups_diag):
        low, high = pl.ds(0, 8), pl.ds(120, 8)
        out = []
        for n, (dr, dc) in enumerate(NB):
            if dc == 0:
                continue
            groups = pl.ds(0, 3) if dr == 0 else groups_diag
            rows = low if dc < 0 else high
            out.append((n, tt.at[groups, rows, :], rx.at[n, groups]))
        return out

    def start_all(phase, copies):
        for n, src, dst in copies:
            dr, dc = NB[n]
            @pl.when(ok(dr, dc))
            def _():
                pltpu.make_async_remote_copy(
                    src, dst, send_sem.at[phase, n], recv_sem.at[phase, n],
                    device_id=dev(dr, dc), device_id_type=MESH).start()

    def wait_recv_all(phase, copies):
        for n, src, dst in copies:
            dr, dc = NB[n]
            @pl.when(ok(-dr, -dc))
            def _():
                pltpu.make_async_remote_copy(
                    src, dst, send_sem.at[phase, n], recv_sem.at[phase, n],
                    device_id=dev(-dr, -dc), device_id_type=MESH).wait_recv()

    def wait_send_all(phase, copies):
        for n, src, dst in copies:
            dr, dc = NB[n]
            @pl.when(ok(dr, dc))
            def _():
                pltpu.make_async_remote_copy(
                    src, dst, send_sem.at[phase, n], recv_sem.at[phase, n],
                    device_id=dev(dr, dc), device_id_type=MESH).wait_send()

    third = pl.ds(2, 1)
    copies0 = [(0, sn0, rs0), (1, ss0, rn0)] + side_copies(tt0, rx0, third)
    pl.semaphore_wait(bar, peers)
    start_all(0, copies0)

    def blur_adjoint(up, mid, down, b):
        return kk[0][b] * down + kk[1][b] * mid + kk[2][b] * up

    def own_body(i, _):
        base = pl.multiple_of(i * 8 + 24, 8)
        here = pl.ds(base, 8)
        up, mid, down = rows_of(obs, base - 1, 8), rows_of(obs, base, 8), rows_of(obs, base + 1, 8)
        v = [[blur_adjoint(up[t], mid[t], down[t], b) for t in range(8)] for b in range(3)]
        e0 = [pltpu.roll(x, 127, 1) for x in v[0]]
        w2_ = [pltpu.roll(x, 1, 1) for x in v[2]]
        cm, csouth = rows_of(cond, base, 8), rows_of(cond, base + 1, 8)
        ceast = [pltpu.roll(x, 127, 1) for x in cm]
        for t in range(8):
            e = jnp.where(last_lane, e0[t + 1] if t < 7 else 0.0, e0[t])
            w_ = jnp.where(first_lane, w2_[t - 1] if t else 0.0, w2_[t])
            r0[t, here, :] = v[1][t] + e + w_
            ce[t, here, :] = 0.5 * (cm[t] + jnp.where(last_lane, ceast[t + 1] if t < 7 else 0.0, ceast[t]))
            cs[t, here, :] = 0.5 * (cm[t] + csouth[t])
        return 0

    lax.fori_loop(0, 30, own_body, 0, unroll=3)
    wait_recv_all(0, copies0)

    def side(rx, group, dc, in_north, in_center):
        north = rx[NB.index((1, dc)), group]
        center = rx[NB.index((0, dc)), group]
        south = rx[NB.index((-1, dc)), group]
        return jnp.where(in_north, north, jnp.where(in_center, center, south))

    fine_north = (lane < 8) | ((lane >= 64) & (lane < 72))
    fine_center = (lane >= 8) & (lane < 40)
    lane64 = lax.rem(lane, 64)

    def unpack_fine(rx):
        for dc, rows in ((-1, slice(0, 8)), (1, slice(120, 128))):
            here = NB.index((0, dc))
            hbuf[0, rows, :] = rx[here, 0]
            hbuf[1, rows, :] = rx[here, 1]
            hbuf[2, rows, :] = side(rx, 2, dc, fine_north, fine_center)

    unpack_fine(rx0)

    def cond_of(x):
        lanes = lax.broadcasted_iota(jnp.int32, x.shape, 1)
        return jnp.where(lanes < 64, pltpu.roll(x, 124, 1), pltpu.roll(x, 4, 1))

    for g in range(2):
        tile = hbuf[g].T
        rows = slice(16 + 128 * g, 144 + 128 * g)
        obs[8, rows, :] = tile
        cond[8, rows, :] = cond_of(tile)
    tile = hbuf[2].T
    for rows, lo in ((slice(8, 16), 64), (slice(272, 280), 72)):
        obs[8, rows, :] = tile[lo:lo + 8]
        cond[8, rows, :] = cond_of(tile[lo:lo + 8])
    for t in range(8):
        obs[t, 8:16, :] = rn0[t]
        cond[t, 8:16, :] = pltpu.roll(rn0[t], 4, 0)
        obs[t, 272:280, :] = rs0[t]
        cond[t, 272:280, :] = pltpu.roll(rs0[t], 4, 0)

    def side_body(i, _):
        base = pl.multiple_of(i * 8 + 24, 8)
        here = pl.ds(base, 8)
        def v(t, b):
            return blur_adjoint(obs[t, pl.ds(base - 1, 8), :], obs[t, here, :],
                                obs[t, pl.ds(base + 1, 8), :], b)
        e8, w8 = pltpu.roll(v(8, 0), 127, 1), pltpu.roll(v(8, 2), 1, 1)
        e0, w7 = pltpu.roll(v(0, 0), 127, 1), pltpu.roll(v(7, 2), 1, 1)
        r0[8, here, :] = v(8, 1) + jnp.where(last_lane, e0, e8) + jnp.where(first_lane, w7, w8)
        r0[7, here, :] = r0[7, here, :] + jnp.where(last_lane, e8, 0.0)
        r0[0, here, :] = r0[0, here, :] + jnp.where(first_lane, w8, 0.0)
        c8 = cond[8, here, :]
        ce8, ce0 = pltpu.roll(c8, 127, 1), pltpu.roll(cond[0, here, :], 127, 1)
        ce[8, here, :] = 0.5 * (c8 + jnp.where(last_lane, ce0, ce8))
        ce[7, here, :] = ce[7, here, :] + 0.5 * jnp.where(last_lane, ce8, 0.0)
        cs[8, here, :] = 0.5 * (c8 + cond[8, pl.ds(base + 1, 8), :])
        return 0

    lax.fori_loop(0, 30, side_body, 0, unroll=6)

    def outer_body(i, _):
        base = pl.multiple_of(jnp.where(i < 2, i * 8 + 8, i * 8 + 248), 8)
        here = pl.ds(base, 8)
        up, mid, down = rows_of(obs, base - 1), rows_of(obs, base), rows_of(obs, base + 1)
        v = [[blur_adjoint(up[t], mid[t], down[t], b) for t in range(9)] for b in range(3)]
        e0, w2_ = sh_east(v[0]), sh_west(v[2])
        cm, csouth = rows_of(cond, base), rows_of(cond, base + 1)
        ceast = sh_east(cm)
        for t in range(9):
            r0[t, here, :] = v[1][t] + e0[t] + w2_[t]
            ce[t, here, :] = 0.5 * (cm[t] + ceast[t])
            cs[t, here, :] = 0.5 * (cm[t] + csouth[t])
        return 0

    lax.fori_loop(0, 4, outer_body, 0, unroll=2)

    def clear_outside(ref):
        @pl.when(r == 0)
        def _():
            for t in range(9):
                ref[t, 8:16, :] = jnp.zeros((8, 128), F32)

        @pl.when(r == n_rows - 1)
        def _():
            for t in range(9):
                ref[t, 272:280, :] = jnp.zeros((8, 128), F32)

        lanes = lax.broadcasted_iota(jnp.int32, (272, 128), 1)

        @pl.when(c == 0)
        def _():
            ref[8, 8:280, :] = jnp.where(lanes < 64, ref[8, 8:280, :], 0.0)

        @pl.when(c == n_cols - 1)
        def _():
            ref[8, 8:280, :] = jnp.where(lanes >= 64, ref[8, 8:280, :], 0.0)

    def row_sums(ref, t):
        total = ref[t, pl.ds(16, 32, stride=8), :]
        for s in range(1, 8):
            total = total + ref[t, pl.ds(16 + s, 32, stride=8), :]
        return total

    src = jnp.concatenate([row_sums(r0, t) for t in range(8)], axis=1)
    esum = jnp.concatenate([row_sums(ce, t) for t in range(8)], axis=1)
    srow = jnp.concatenate([cs[t, pl.ds(23, 32, stride=8), :] for t in range(8)], axis=1)
    nrow = jnp.concatenate([cs[t, 8:16, :] for t in range(8)], axis=1)
    stack = jnp.concatenate([src, esum, srow, nrow], axis=0)
    sums = exact_dot(stack, cmat[...])
    source = sums[0:32, 0:128]
    c_east = sums[32:64, 128:256]
    c_south = sums[64:96, 0:128]
    outer = row_sums(ce, 8)
    lane32 = lax.broadcasted_iota(jnp.int32, (32, 128), 1)
    c_west = jnp.where(lane32 == 0, pltpu.roll(outer, 1, 1), pltpu.roll(c_east, 1, 1))
    zs[0, 0:8, :] = sums[96:104, 0:128]
    zs[0, 8:40, :] = c_south
    c_north = zs[0, 7:39, :]
    zs[...] = jnp.zeros(zs.shape, F32)
    c_diag = 64.0 * (ksum * ksum) + c_east + c_west + c_north + c_south
    scale = OMEGA / c_diag
    fields = (source * scale, c_east * scale, c_west * scale, c_north * scale, c_south * scale)
    ctab[5, 0, 8:40, :] = scale
    for f in range(5):
        ctab[f, 0, 8:40, :] = fields[f]
        sn1[f] = fields[f]
    for g in range(3):
        for h in range(2):
            f = 2 * g + h
            if f < 5:
                tbuf[64 * h:64 * h + 8, :] = fields[f][24:32]
                tbuf[64 * h + 8:64 * h + 40, :] = fields[f]
                tbuf[64 * h + 40:64 * h + 48, :] = fields[f][0:8]
        tt1[g] = tbuf[...].T

    whole = pl.ds(0, 3)
    copies1 = [(0, sn1.at[:, pl.ds(0, 8), :], rs1), (1, sn1.at[:, pl.ds(24, 8), :], rn1)]
    copies1 += side_copies(tt1, rx1, whole)
    start_all(1, copies1)

    def diag_body(i, _):
        base = pl.multiple_of(i * 8 + 8, 8)
        here = pl.ds(base, 8)
        east = rows_of(ce, base)
        west = sh_west(east)
        for t in range(9):
            total = (east[t] + west[t]) + (cs[t, here, :] + cs[t, pl.ds(base - 1, 8), :])
            rfd[t, here, :] = 1.0 / (ksq + total)
        return 0

    lax.fori_loop(0, 34, diag_body, 0, unroll=4)
    clear_outside(rfd)
    wait_recv_all(1, copies1)

    for f in range(5):
        ctab[f, 0, 0:8, :] = rn1[f]
        ctab[f, 0, 40:48, :] = rs1[f]
    for g in range(3):
        for dc, rows in ((-1, slice(0, 8)), (1, slice(120, 128))):
            hbuf[g, rows, :] = side(rx1, g, dc, lane64 < 8, lane64 < 40)
        tile = hbuf[g].T
        for h in range(2):
            f = 2 * g + h
            if f < 5:
                ctab[f, 1, :, :] = tile[64 * h:64 * h + 48]

    lane48 = lax.broadcasted_iota(jnp.int32, (48, 128), 1)
    last48, first48 = lane48 == 127, lane48 == 0

    def sweep(_, carry):
        z = [zs[t, 8:56, :] for t in range(2)]
        east = [pltpu.roll(x, 127, 1) for x in z]
        west = [pltpu.roll(x, 1, 1) for x in z]
        new = []
        for t in range(2):
            ze = jnp.where(last48, east[1 - t], east[t])
            zw = jnp.where(first48, west[1 - t], west[t])
            zn, zso = zs[t, 7:55, :], zs[t, 9:57, :]
            new.append((ctab[0, t] + (1.0 - OMEGA) * z[t])
                       + (ctab[1, t] * ze + ctab[2, t] * zw)
                       + (ctab[3, t] * zn + ctab[4, t] * zso))
        for t in range(2):
            zs[t, 8:56, :] = new[t]
        return carry

    def jacobi():
        for t in range(2):
            zs[t, 8:56, :] = ctab[0, t]
        lax.fori_loop(0, SWEEPS - 1, sweep, 0)
        up = exact_dot(zs[0, 8:56, :], umat[:, 0:1024])
        for t in range(8):
            zup[t] = up[:, 128 * t:128 * t + 128]
        zup[8] = exact_dot(zs[1, 8:56, :], umat[:, 1024:1152])

    jacobi()

    def precond(field, out):
        def body(i, _):
            base = pl.multiple_of(i * 8 + 8, 8)
            here = pl.ds(base, 8)
            for t in range(9):
                out[t, here, :] = field[t, here, :] * rfd[t, here, :] + zup[t, pl.ds(i + 7, 1), :]
            return 0

        lax.fori_loop(0, 34, body, 0, unroll=4)

    precond(r0, d0)

    def blur_rows(ref, base):
        up, mid, down = rows_of(ref, base - 1), rows_of(ref, base), rows_of(ref, base + 1)
        u = [[kk[0][b] * up[t] + kk[1][b] * mid[t] + kk[2][b] * down[t] for t in range(9)]
             for b in range(3)]
        w_, e_ = sh_west(u[0]), sh_east(u[2])
        return [u[1][t] + w_[t] + e_[t] for t in range(9)], up, mid, down

    def blur0(i, _):
        base = pl.multiple_of(i * 8 + 8, 8)
        out, _, _, _ = blur_rows(d0, base)
        for t in range(9):
            img[t, pl.ds(base, 8), :] = out[t]
        return 0

    lax.fori_loop(0, 34, blur0, 0, unroll=4)
    clear_outside(img)

    def adjoint_parts(base):
        up, mid, down = rows_of(img, base - 1), rows_of(img, base), rows_of(img, base + 1)
        return [[kk[0][b] * down[t] + kk[1][b] * mid[t] + kk[2][b] * up[t] for t in range(9)]
                for b in range(3)]

    zero = jnp.zeros((8, 128), F32)

    def apply0(i, carry):
        gam, dad = carry
        base = pl.multiple_of(i * 8 + 16, 8)
        v = adjoint_parts(base)
        up, mid, down = rows_of(d0, base - 1), rows_of(d0, base), rows_of(d0, base + 1)
        east = sh_east(mid)
        flux = [ce[t, pl.ds(base, 8), :] * (mid[t] - east[t]) for t in range(9)]
        e0 = sh_east(v[0])
        w2_ = sh_west([v[2][t] - flux[t] for t in range(9)])
        for t in range(8):
            lap = (cs[t, pl.ds(base, 8), :] * (mid[t] - down[t])
                   - cs[t, pl.ds(base - 1, 8), :] * (up[t] - mid[t]))
            out = ((v[1][t] + e0[t]) + (w2_[t] + flux[t])) + lap
            q0[t, pl.ds(base, 8), :] = out
            gam = gam + r0[t, pl.ds(base, 8), :] * mid[t]
            dad = dad + mid[t] * out
        return gam, dad

    gam, dad = lax.fori_loop(0, 32, apply0, (zero, zero), unroll=4)

    src = jnp.concatenate([row_sums(q0, t) for t in range(8)], axis=1)
    cells = exact_dot(src, cmat[:, 0:128])
    b2 = cells * ctab[5, 0, 8:40, :]
    ctab[0, 0, 8:40, :] = b2

    def q_tile(start, n):
        lanes = lax.broadcasted_iota(jnp.int32, (n, 128), 1)
        rows = pl.ds(start, n)
        return jnp.where(lanes < 64, q0[0, rows, :], q0[7, rows, :])

    tt2[0] = q_tile(16, 128).T
    tt2[1] = q_tile(144, 128).T
    tbuf[0:8, :] = b2[24:32]
    tbuf[8:40, :] = b2
    tbuf[40:48, :] = b2[0:8]
    tbuf[64:72, :] = q_tile(264, 8)
    tbuf[72:80, :] = q_tile(16, 8)
    tt2[2] = tbuf[...].T
    for t in range(8):
        sn2[t] = q0[t, 16:24, :]
        ss2[t] = q0[t, 264:272, :]
    sn2[8] = b2[0:8]
    ss2[8] = b2[24:32]
    copies2 = [(0, sn2, rs2), (1, ss2, rn2)] + side_copies(tt2, rx2, third)
    start_all(2, copies2)
    wait_recv_all(2, copies2)

    unpack_fine(rx2)
    for g in range(2):
        q0[8, 16 + 128 * g:144 + 128 * g, :] = hbuf[g].T
    tile = hbuf[2].T
    q0[8, 8:16, :] = tile[64:72]
    q0[8, 272:280, :] = tile[72:80]
    ctab[0, 1, :, :] = tile[0:48]
    for t in range(8):
        q0[t, 8:16, :] = rn2[t]
        q0[t, 272:280, :] = rs2[t]
    ctab[0, 0, 0:8, :] = rn2[8]
    ctab[0, 0, 40:48, :] = rs2[8]
    jacobi()
    precond(q0, w)

    def blur1_rim(base):
        out, _, _, _ = blur_rows(w, base)
        for t in range(9):
            img[t, pl.ds(base, 8), :] = out[t]

    def blur1(i, carry):
        qw, waw = carry
        base = pl.multiple_of(i * 8 + 16, 8)
        out, up, mid, down = blur_rows(w, base)
        east = sh_east(mid)
        flux = [ce[t, pl.ds(base, 8), :] * (mid[t] - east[t]) for t in range(9)]
        fw = sh_west(flux)
        img[8, pl.ds(base, 8), :] = out[8]
        for t in range(8):
            lap = (cs[t, pl.ds(base, 8), :] * (mid[t] - down[t])
                   - cs[t, pl.ds(base - 1, 8), :] * (up[t] - mid[t]))
            lap = lap + (flux[t] - fw[t])
            img[t, pl.ds(base, 8), :] = out[t]
            lw[t, pl.ds(base, 8), :] = lap
            qw = qw + q0[t, pl.ds(base, 8), :] * mid[t]
            waw = waw + (out[t] * out[t] + mid[t] * lap)
        return qw, waw

    blur1_rim(8)
    blur1_rim(272)
    qw, waw = lax.fori_loop(0, 32, blur1, (zero, zero), unroll=4)

    for n, part in enumerate((gam, dad, qw, waw)):
        red0[n:n + 1, :] = jnp.sum(part, axis=0, keepdims=True)
    red0[4:8, :] = jnp.zeros((4, 128), F32)
    redx[k8] = red0[...]
    for i in range(zk):
        @pl.when(k8 != i)
        def _():
            pltpu.make_async_remote_copy(
                red0, redx.at[k8], rsend.at[0], rrecv.at[0],
                device_id=zk_group[i], device_id_type=MESH).start()
    clear_outside(img)

    def apply1(i, _):
        base = pl.multiple_of(i * 8 + 16, 8)
        v = adjoint_parts(base)
        e0, w2_ = sh_east(v[0]), sh_west(v[2])
        for t in range(8):
            here = pl.ds(base, 8)
            lw[t, here, :] = ((v[1][t] + e0[t]) + w2_[t]) + lw[t, here, :]
        return 0

    def all_bytes(buf, n, sem):
        return pltpu.make_async_copy(buf.at[pl.ds(0, n)], buf.at[pl.ds(0, n)], sem)

    all_bytes(redx, zk - 1, rrecv.at[0]).wait()
    total = redx[0]
    for i in range(1, zk):
        total = total + redx[i]
    red1[...] = total
    redy[xy_me] = total
    for i in range(n_rows * ny):
        @pl.when(xy_me != i)
        def _():
            pltpu.make_async_remote_copy(
                red1, redy.at[xy_me], rsend.at[1], rrecv.at[1],
                device_id=xy_group[i], device_id_type=MESH).start()
    lax.fori_loop(0, 32, apply1, 0, unroll=4)
    all_bytes(redy, n_rows * ny - 1, rrecv.at[1]).wait()
    total = redy[0]
    for i in range(1, n_rows * ny):
        total = total + redy[i]
    value = jnp.broadcast_to(jnp.sum(total, axis=1, keepdims=True), (8, 128))
    g0 = jnp.broadcast_to(value[0:1], (8, 128))
    dq = jnp.broadcast_to(value[1:2], (8, 128))
    qws = jnp.broadcast_to(value[2:3], (8, 128))
    ws = jnp.broadcast_to(value[3:4], (8, 128))
    alpha = g0 / dq
    g1 = (g0 - alpha * dq) + alpha * (alpha * qws - dq)
    beta1 = 1.0 + g1 / g0
    dad1 = beta1 * (beta1 * dq - alpha * qws) + alpha * (alpha * ws - beta1 * qws)
    step = g1 / dad1
    ca = alpha + step * beta1
    cb = alpha * step

    coef[0] = ca
    coef[1] = cb
    wait_send_all(0, copies0)
    wait_send_all(1, copies1)
    wait_send_all(2, copies2)
    all_bytes(redx, zk - 1, rsend.at[0]).wait()
    all_bytes(redy, n_rows * ny - 1, rsend.at[1]).wait()


def finish_kernel(r0, d0, q0, w, lw, coef, sol_hbm, res_hbm, sol, res, out_sem):
    ca, cb = coef[0], coef[1]
    stores = []
    for t in range(8):
        def finish(i, _):
            src_rows = pl.ds(pl.multiple_of(i * 8 + 16, 8), 8)
            dst_rows = pl.ds(pl.multiple_of(i * 8, 8), 8)
            sol[t, dst_rows, :] = ca * d0[t, src_rows, :] - cb * w[t, src_rows, :]
            res[t, dst_rows, :] = (r0[t, src_rows, :] - ca * q0[t, src_rows, :]) + cb * lw[t, src_rows, :]
            return 0

        lax.fori_loop(0, 32, finish, 0, unroll=8)
        lanes = pl.ds(t * 128, 128)
        stores.append(pltpu.make_async_copy(sol.at[t], sol_hbm.at[:, lanes], out_sem.at[t]))
        stores.append(pltpu.make_async_copy(res.at[t], res_hbm.at[:, lanes], out_sem.at[8 + t]))
        stores[-2].start()
        stores[-1].start()
    for x in stores:
        x.wait()


def body(n_rows, n_cols, observed, class_map, class_weights, blur_kernel):
    zk = min(8, n_cols)
    ny = n_cols // zk
    big = pltpu.VMEM((9, 288, 128), F32)
    half = pltpu.VMEM((8, 256, 128), F32)

    def v(*shape):
        return pltpu.VMEM(shape, F32)

    scratch = [
        big, pltpu.VMEM((8, 256, 128), jnp.int32), big, big, big, big, big,
        v(9, 48, 128), pltpu.VMEM((1024, 256), BF16), pltpu.VMEM((128, 1152), BF16),
        v(128, 128), v(3, 128, 128), v(3, 128, 128), v(3, 128, 128), v(3, 128, 128),
        v(6, 2, 48, 128), v(2, 64, 128),
        v(8, 8, 128), v(8, 8, 128), v(8, 8, 128), v(8, 8, 128), v(8, 3, 8, 128),
        v(5, 32, 128), v(5, 8, 128), v(5, 8, 128), v(8, 3, 8, 128),
        v(9, 8, 128), v(9, 8, 128), v(9, 8, 128), v(9, 8, 128), v(8, 3, 8, 128),
        v(8, 128), v(8, 128), v(zk, 8, 128), v(n_rows * ny, 8, 128),
        pltpu.SemaphoreType.DMA((16,)),
        pltpu.SemaphoreType.DMA((3, 8)), pltpu.SemaphoreType.DMA((3, 8)),
        pltpu.SemaphoreType.DMA((2,)), pltpu.SemaphoreType.DMA((2,)),
    ]
    hbm = pl.BlockSpec(memory_space=pltpu.HBM)
    vmem = pl.BlockSpec(memory_space=pltpu.VMEM)
    scalars = pl.BlockSpec(memory_space=pltpu.SMEM)
    field = pltpu.VMEM((9, 288, 128), F32)
    fields = pl.pallas_call(
        functools.partial(kernel, n_rows, n_cols, zk),
        out_shape=(field,) * 5 + (pltpu.VMEM((2, 8, 128), F32),),
        in_specs=[scalars, scalars, hbm, hbm],
        out_specs=(vmem,) * 6,
        scratch_shapes=scratch,
        compiler_params=pltpu.CompilerParams(
            collective_id=0, has_side_effects=True, vmem_limit_bytes=KERNEL_VMEM),
    )(class_weights, blur_kernel, observed, class_map)
    shape = jax.ShapeDtypeStruct(observed.shape, F32)
    return pl.pallas_call(
        finish_kernel,
        out_shape=(shape, shape),
        in_specs=[vmem] * 6,
        out_specs=(hbm, hbm),
        scratch_shapes=[half, half, pltpu.SemaphoreType.DMA((16,))],
        compiler_params=pltpu.CompilerParams(vmem_limit_bytes=FINISH_VMEM),
    )(*fields)


def solution(mesh):
    n_rows, n_cols = mesh.shape["rows"], mesh.shape["cols"]
    return jax.shard_map(
        functools.partial(body, n_rows, n_cols),
        mesh=mesh,
        in_specs=(P("rows", "cols"), P("rows", "cols"), P(), P()),
        out_specs=(P("rows", "cols"), P("rows", "cols")),
        check_vma=False,
    )
```

```python
import functools

import jax
import jax.numpy as jnp
from jax import lax
from jax.experimental import pallas as pl
from jax.experimental.pallas import tpu as pltpu
from jax.sharding import PartitionSpec as P

MESH = pl.DeviceIdType.MESH
OMEGA = 0.8
SWEEPS = 8
NB = ((-1, 0), (1, 0), (0, -1), (0, 1), (-1, -1), (-1, 1), (1, -1), (1, 1))
F32 = jnp.float32
BF16 = jnp.bfloat16
KERNEL_VMEM = 55 * 2**20
FINISH_VMEM = 16 * 2**20


def exact_dot(x, ones):
    hi = x.astype(BF16)
    lo = (x - hi.astype(F32)).astype(BF16)
    both = jnp.dot(jnp.concatenate([hi, lo], axis=0), ones, preferred_element_type=F32)
    return both[: x.shape[0]] + both[x.shape[0] :]


def kernel(
    n_rows, n_cols, zk,
    cw, bk, obs_hbm, cls_hbm, r0, d0, q0, w, lw, coef,
    obs, cls, cond, rfd, ce, cs, img,
    zup, cmat, umat, tbuf, tt0, tt1, tt2, hbuf, ctab, zs,
    rx0, sn1, rn1, rs1, rx1, sn2, rn2, rs2, rx2, zeast, zwest,
    red0, red1, redx, redy,
    in_sem, send_sem, recv_sem, rsend, rrecv,
):
    r = lax.axis_index("rows")
    c = lax.axis_index("cols")
    ny = n_cols // zk
    y, k8 = c // zk, lax.rem(c, zk)

    def ok(dr, dc):
        return (r + dr >= 0) & (r + dr < n_rows) & (c + dc >= 0) & (c + dc < n_cols)

    def dev(dr, dc):
        return (c + dc, r + dr)

    loads = []
    for t in range(8):
        lanes = pl.ds(t * 128, 128)
        loads.append(pltpu.make_async_copy(cls_hbm.at[:, lanes], cls.at[t], in_sem.at[t]))
        loads.append(pltpu.make_async_copy(
            obs_hbm.at[:, lanes], obs.at[t, pl.ds(16, 256), :], in_sem.at[8 + t]))
    for x in loads:
        x.start()

    for buf in (rx0, rn1, rs1, rx1, rn2, rs2, rx2, hbuf, zs):
        buf[...] = jnp.zeros(buf.shape, F32)
    for buf in (obs, cond):
        for t in range(8):
            buf[t, 8:16, :] = jnp.zeros((8, 128), F32)
            buf[t, 272:280, :] = jnp.zeros((8, 128), F32)

    bar = pltpu.get_barrier_semaphore()
    peers = zk + n_rows * ny - 2
    for dr, dc in NB:
        if dc == 0:
            continue
        fresh = ok(dr, dc)
        if dr == 0:
            fresh = fresh & (k8 == (zk - 1 if dc > 0 else 0))
        peers = peers + fresh.astype(jnp.int32)

        @pl.when(fresh)
        def _():
            pl.semaphore_signal(bar, inc=1, device_id=dev(dr, dc), device_id_type=MESH)
    nz = zk // 2
    z_me, core = k8 // 2, lax.rem(k8, 2)
    xy_me = r * ny + y

    def ring(o, n):
        return min(o, n - o)

    zk_far = sorted(((a, b) for a in range(nz) for b in range(2) if a or b),
                    key=lambda o: -(2 * ring(o[0], nz) + o[1]))
    xy_far = sorted(((a, b) for a in range(n_rows) for b in range(ny) if a or b),
                    key=lambda o: -(ring(o[0], n_rows) + ring(o[1], ny)))
    zk_group = [(y * zk + lax.rem(z_me + a, nz) * 2 + lax.rem(core + b, 2), r) for a, b in zk_far]
    xy_group = [(lax.rem(y + b, ny) * zk + k8, lax.rem(r + a, n_rows)) for a, b in xy_far]
    for peer in zk_group + xy_group:
        pl.semaphore_signal(bar, inc=1, device_id=peer, device_id_type=MESH)

    lane = lax.broadcasted_iota(jnp.int32, (8, 128), 1)
    sub = lax.broadcasted_iota(jnp.int32, (8, 128), 0)
    first_lane = lane == 0
    last_lane = lane == 127

    kk = [[bk[a, b] for b in range(3)] for a in range(3)]
    ksum = kk[0][0]
    ksq = kk[0][0] * kk[0][0]
    for a in range(3):
        for b in range(3):
            if a + b:
                ksum = ksum + kk[a][b]
                ksq = ksq + kk[a][b] * kk[a][b]

    def sh_east(v):
        rolled = [pltpu.roll(x, 127, 1) for x in v]
        n = len(v)
        return [jnp.where(last_lane, rolled[(t + 1) % n], rolled[t]) for t in range(n)]

    def sh_west(v):
        rolled = [pltpu.roll(x, 1, 1) for x in v]
        n = len(v)
        return [jnp.where(first_lane, rolled[(t - 1) % n], rolled[t]) for t in range(n)]

    def rows_of(ref, base, n=9):
        return [ref[t, pl.ds(base, 8), :] for t in range(n)]

    for x in loads:
        x.wait()

    w0, w1, w2, w3 = cw[0], cw[1], cw[2], cw[3]

    def cond_body(i, _):
        src = pl.multiple_of(i * 8, 8)
        dst = pl.multiple_of(i * 8 + 16, 8)
        for t in range(8):
            m = cls[t, pl.ds(src, 8), :]
            cond[t, pl.ds(dst, 8), :] = jnp.where(
                m == 0, w0, jnp.where(m == 1, w1, jnp.where(m == 2, w2, w3)))
        return 0

    lax.fori_loop(0, 32, cond_body, 0)

    def rim_tile(start, n):
        lanes = lax.broadcasted_iota(jnp.int32, (n, 128), 1)
        rows = pl.ds(start, n)
        left = jnp.where(lanes < 8, obs[0, rows, :], pltpu.roll(cond[0, rows, :], 8, 1))
        right = jnp.where(lanes >= 120, obs[7, rows, :], pltpu.roll(cond[7, rows, :], 120, 1))
        return jnp.where(lanes < 64, left, right)

    tt0[0] = rim_tile(16, 128).T
    tt0[1] = rim_tile(144, 128).T
    tbuf[...] = jnp.zeros(tbuf.shape, F32)
    tbuf[64:72, :] = rim_tile(264, 8)
    tbuf[72:80, :] = rim_tile(16, 8)
    tt0[2] = tbuf[...].T

    def side_copies(tt, rx, groups_diag, width):
        low, high = pl.ds(0, width), pl.ds(128 - width, width)
        out = []
        for n, (dr, dc) in enumerate(NB):
            if dc == 0:
                continue
            groups = pl.ds(0, tt.shape[0]) if dr == 0 else groups_diag
            rows = low if dc < 0 else high
            out.append((n, n, tt.at[groups, rows, :], rx.at[n, groups]))
        return out

    def start_all(phase, copies):
        for q, n, src, dst in copies:
            dr, dc = NB[n]
            @pl.when(ok(dr, dc))
            def _():
                pltpu.make_async_remote_copy(
                    src, dst, send_sem.at[phase, q], recv_sem.at[phase, q],
                    device_id=dev(dr, dc), device_id_type=MESH).start()

    def wait_recv_all(phase, copies):
        for q, n, src, dst in copies:
            dr, dc = NB[n]
            @pl.when(ok(-dr, -dc))
            def _():
                pltpu.make_async_remote_copy(
                    src, dst, send_sem.at[phase, q], recv_sem.at[phase, q],
                    device_id=dev(-dr, -dc), device_id_type=MESH).wait_recv()

    def wait_send_all(phase, copies):
        for q, n, src, dst in copies:
            dr, dc = NB[n]
            @pl.when(ok(dr, dc))
            def _():
                pltpu.make_async_remote_copy(
                    src, dst, send_sem.at[phase, q], recv_sem.at[phase, q],
                    device_id=dev(dr, dc), device_id_type=MESH).wait_send()

    third = pl.ds(2, 1)
    own, top, low = pl.ds(0, 8), pl.ds(16, 8), pl.ds(264, 8)
    above, below = pl.ds(8, 8), pl.ds(272, 8)
    copies0 = side_copies(tt0, rx0, third, 16)
    for q, field in ((0, obs), (8, cond)):
        copies0.append((q, 0, field.at[own, top, :], field.at[own, below, :]))
        copies0.append((q + 1, 1, field.at[own, low, :], field.at[own, above, :]))
    pl.semaphore_wait(bar, peers)
    start_all(0, copies0)

    ii = lax.broadcasted_iota(jnp.int32, (1024, 128), 0)
    jj = lax.broadcasted_iota(jnp.int32, (1024, 128), 1)
    cmat[:, 0:128] = jnp.where(ii // 8 == jj, 1.0, 0.0).astype(BF16)
    cmat[:, 128:256] = jnp.where(ii == jj * 8 + 7, 1.0, 0.0).astype(BF16)
    ui = lax.broadcasted_iota(jnp.int32, (128, 1024), 0)
    uj = lax.broadcasted_iota(jnp.int32, (128, 1024), 1)
    umat[:, 0:1024] = jnp.where(uj // 8 == ui, 1.0, 0.0).astype(BF16)
    vi = lax.broadcasted_iota(jnp.int32, (128, 128), 0)
    vj = lax.broadcasted_iota(jnp.int32, (128, 128), 1)
    umat[:, 1024:1152] = jnp.where(
        ((vj < 64) & (vi == 0)) | ((vj >= 64) & (vi == 127)), 1.0, 0.0).astype(BF16)

    def blur_adjoint(up, mid, down, b):
        return kk[0][b] * down + kk[1][b] * mid + kk[2][b] * up

    def own_body(i, _):
        base = pl.multiple_of(i * 8 + 24, 8)
        here = pl.ds(base, 8)
        up, mid, down = rows_of(obs, base - 1, 8), rows_of(obs, base, 8), rows_of(obs, base + 1, 8)
        v = [[blur_adjoint(up[t], mid[t], down[t], b) for t in range(8)] for b in range(3)]
        e0 = [pltpu.roll(x, 127, 1) for x in v[0]]
        w2_ = [pltpu.roll(x, 1, 1) for x in v[2]]
        cm, csouth = rows_of(cond, base, 8), rows_of(cond, base + 1, 8)
        ceast = [pltpu.roll(x, 127, 1) for x in cm]
        for t in range(8):
            e = jnp.where(last_lane, e0[t + 1] if t < 7 else 0.0, e0[t])
            w_ = jnp.where(first_lane, w2_[t - 1] if t else 0.0, w2_[t])
            r0[t, here, :] = v[1][t] + e + w_
            ce[t, here, :] = 0.5 * (cm[t] + jnp.where(last_lane, ceast[t + 1] if t < 7 else 0.0, ceast[t]))
            cs[t, here, :] = 0.5 * (cm[t] + csouth[t])
        return 0

    lax.fori_loop(0, 30, own_body, 0, unroll=3)
    wait_recv_all(0, copies0)

    def side(rx, group, dc, in_north, in_center):
        north = rx[NB.index((1, dc)), group]
        center = rx[NB.index((0, dc)), group]
        south = rx[NB.index((-1, dc)), group]
        return jnp.where(in_north, north, jnp.where(in_center, center, south))

    lane64 = lax.rem(lane, 64)

    lane16 = lax.broadcasted_iota(jnp.int32, (16, 128), 1)
    for dc, rows in ((-1, slice(0, 16)), (1, slice(112, 128))):
        here = NB.index((0, dc))
        hbuf[0, rows, :] = rx0[here, 0]
        hbuf[1, rows, :] = rx0[here, 1]
        hbuf[2, rows, :] = side(rx0, 2, dc, lane16 < 72, lane16 < 0)

    def cond_of(x):
        lanes = lax.broadcasted_iota(jnp.int32, x.shape, 1)
        return jnp.where(lanes < 64, pltpu.roll(x, 120, 1), pltpu.roll(x, 8, 1))

    for g in range(2):
        tile = hbuf[g].T
        rows = slice(16 + 128 * g, 144 + 128 * g)
        obs[8, rows, :] = tile
        cond[8, rows, :] = cond_of(tile)
    tile = hbuf[2].T
    for rows, lo in ((slice(8, 16), 64), (slice(272, 280), 72)):
        obs[8, rows, :] = tile[lo:lo + 8]
        cond[8, rows, :] = cond_of(tile[lo:lo + 8])
    def side_body(i, _):
        base = pl.multiple_of(i * 8 + 24, 8)
        here = pl.ds(base, 8)
        def v(t, b):
            return blur_adjoint(obs[t, pl.ds(base - 1, 8), :], obs[t, here, :],
                                obs[t, pl.ds(base + 1, 8), :], b)
        e8, w8 = pltpu.roll(v(8, 0), 127, 1), pltpu.roll(v(8, 2), 1, 1)
        e0, w7 = pltpu.roll(v(0, 0), 127, 1), pltpu.roll(v(7, 2), 1, 1)
        r0[8, here, :] = v(8, 1) + jnp.where(last_lane, e0, e8) + jnp.where(first_lane, w7, w8)
        r0[7, here, :] = r0[7, here, :] + jnp.where(last_lane, e8, 0.0)
        r0[0, here, :] = r0[0, here, :] + jnp.where(first_lane, w8, 0.0)
        c8 = cond[8, here, :]
        ce8, ce0 = pltpu.roll(c8, 127, 1), pltpu.roll(cond[0, here, :], 127, 1)
        ce[8, here, :] = 0.5 * (c8 + jnp.where(last_lane, ce0, ce8))
        ce[7, here, :] = ce[7, here, :] + 0.5 * jnp.where(last_lane, ce8, 0.0)
        cs[8, here, :] = 0.5 * (c8 + cond[8, pl.ds(base + 1, 8), :])
        return 0

    lax.fori_loop(0, 30, side_body, 0, unroll=6)

    def outer_body(i, _):
        base = pl.multiple_of(jnp.where(i < 2, i * 8 + 8, i * 8 + 248), 8)
        here = pl.ds(base, 8)
        up, mid, down = rows_of(obs, base - 1), rows_of(obs, base), rows_of(obs, base + 1)
        v = [[blur_adjoint(up[t], mid[t], down[t], b) for t in range(9)] for b in range(3)]
        e0, w2_ = sh_east(v[0]), sh_west(v[2])
        cm, csouth = rows_of(cond, base), rows_of(cond, base + 1)
        ceast = sh_east(cm)
        for t in range(9):
            r0[t, here, :] = v[1][t] + e0[t] + w2_[t]
            ce[t, here, :] = 0.5 * (cm[t] + ceast[t])
            cs[t, here, :] = 0.5 * (cm[t] + csouth[t])
        return 0

    lax.fori_loop(0, 4, outer_body, 0, unroll=2)

    def clear_outside(ref):
        @pl.when(r == 0)
        def _():
            for t in range(9):
                ref[t, 8:16, :] = jnp.zeros((8, 128), F32)

        @pl.when(r == n_rows - 1)
        def _():
            for t in range(9):
                ref[t, 272:280, :] = jnp.zeros((8, 128), F32)

        lanes = lax.broadcasted_iota(jnp.int32, (272, 128), 1)

        @pl.when(c == 0)
        def _():
            ref[8, 8:280, :] = jnp.where(lanes < 64, ref[8, 8:280, :], 0.0)

        @pl.when(c == n_cols - 1)
        def _():
            ref[8, 8:280, :] = jnp.where(lanes >= 64, ref[8, 8:280, :], 0.0)

    def row_sums(ref, t):
        total = ref[t, pl.ds(16, 32, stride=8), :]
        for s in range(1, 8):
            total = total + ref[t, pl.ds(16 + s, 32, stride=8), :]
        return total

    src = jnp.concatenate([row_sums(r0, t) for t in range(8)], axis=1)
    esum = jnp.concatenate([row_sums(ce, t) for t in range(8)], axis=1)
    srow = jnp.concatenate([cs[t, pl.ds(23, 32, stride=8), :] for t in range(8)], axis=1)
    nrow = jnp.concatenate([cs[t, 8:16, :] for t in range(8)], axis=1)
    stack = jnp.concatenate([src, esum, srow, nrow], axis=0)
    sums = exact_dot(stack, cmat[...])
    source = sums[0:32, 0:128]
    c_east = sums[32:64, 128:256]
    c_south = sums[64:96, 0:128]
    outer = row_sums(ce, 8)
    lane32 = lax.broadcasted_iota(jnp.int32, (32, 128), 1)
    c_west = jnp.where(lane32 == 0, pltpu.roll(outer, 1, 1), pltpu.roll(c_east, 1, 1))
    zs[0, 0:8, :] = sums[96:104, 0:128]
    zs[0, 8:40, :] = c_south
    c_north = zs[0, 7:39, :]
    zs[...] = jnp.zeros(zs.shape, F32)
    c_diag = 64.0 * (ksum * ksum) + c_east + c_west + c_north + c_south
    scale = OMEGA / c_diag
    fields = (source * scale, c_east * scale, c_west * scale, c_north * scale, c_south * scale)
    ctab[5, 0, 8:40, :] = scale
    ctab[5, 1, 8:40, :] = c_diag * (1.0 / OMEGA)
    for f in range(5):
        ctab[f, 0, 8:40, :] = fields[f]
        sn1[f] = fields[f]
    for g in range(3):
        for h in range(2):
            f = 2 * g + h
            if f < 5:
                tbuf[64 * h:64 * h + 8, :] = fields[f][24:32]
                tbuf[64 * h + 8:64 * h + 40, :] = fields[f]
                tbuf[64 * h + 40:64 * h + 48, :] = fields[f][0:8]
        tt1[g] = tbuf[...].T

    whole = pl.ds(0, 3)
    copies1 = [(0, 0, sn1.at[:, pl.ds(0, 8), :], rs1), (1, 1, sn1.at[:, pl.ds(24, 8), :], rn1)]
    copies1 += side_copies(tt1, rx1, whole, 8)
    start_all(1, copies1)

    def diag_body(i, _):
        base = pl.multiple_of(i * 8 + 8, 8)
        here = pl.ds(base, 8)
        east = rows_of(ce, base)
        west = sh_west(east)
        for t in range(9):
            total = (east[t] + west[t]) + (cs[t, here, :] + cs[t, pl.ds(base - 1, 8), :])
            rfd[t, here, :] = 1.0 / (ksq + total)
        return 0

    lax.fori_loop(0, 34, diag_body, 0, unroll=4)
    clear_outside(rfd)
    wait_recv_all(1, copies1)

    for f in range(5):
        ctab[f, 0, 0:8, :] = rn1[f]
        ctab[f, 0, 40:48, :] = rs1[f]
    hbuf[:, 8:16, :] = jnp.zeros((3, 8, 128), F32)
    hbuf[:, 112:120, :] = jnp.zeros((3, 8, 128), F32)
    for g in range(3):
        for dc, rows in ((-1, slice(0, 8)), (1, slice(120, 128))):
            hbuf[g, rows, :] = side(rx1, g, dc, lane64 < 8, lane64 < 40)
        tile = hbuf[g].T
        for h in range(2):
            f = 2 * g + h
            if f < 5:
                ctab[f, 1, :, :] = tile[64 * h:64 * h + 48]

    lane48 = lax.broadcasted_iota(jnp.int32, (48, 128), 1)
    last48, first48 = lane48 == 127, lane48 == 0

    def sweep(_, carry):
        z = [zs[t, 8:56, :] for t in range(2)]
        east = [pltpu.roll(x, 127, 1) for x in z]
        west = [pltpu.roll(x, 1, 1) for x in z]
        new = []
        for t in range(2):
            ze = jnp.where(last48, east[1 - t], east[t])
            zw = jnp.where(first48, west[1 - t], west[t])
            zn, zso = zs[t, 7:55, :], zs[t, 9:57, :]
            new.append((ctab[0, t] + (1.0 - OMEGA) * z[t])
                       + (ctab[1, t] * ze + ctab[2, t] * zw)
                       + (ctab[3, t] * zn + ctab[4, t] * zso))
        for t in range(2):
            zs[t, 8:56, :] = new[t]
        return carry

    def jacobi():
        for t in range(2):
            zs[t, 8:56, :] = ctab[0, t]
        lax.fori_loop(0, SWEEPS - 1, sweep, 0)

    def spread():
        up = exact_dot(zs[0, 8:56, :], umat[:, 0:1024])
        for t in range(8):
            zup[t] = up[:, 128 * t:128 * t + 128]
        zup[8] = exact_dot(zs[1, 8:56, :], umat[:, 1024:1152])

    jacobi()
    spread()

    def precond(field, out):
        def body(i, _):
            base = pl.multiple_of(i * 8 + 8, 8)
            here = pl.ds(base, 8)
            for t in range(9):
                out[t, here, :] = field[t, here, :] * rfd[t, here, :] + zup[t, pl.ds(i + 7, 1), :]
            return 0

        lax.fori_loop(0, 34, body, 0, unroll=4)

    precond(r0, d0)

    def blur_rows(ref, base):
        up, mid, down = rows_of(ref, base - 1), rows_of(ref, base), rows_of(ref, base + 1)
        u = [[kk[0][b] * up[t] + kk[1][b] * mid[t] + kk[2][b] * down[t] for t in range(9)]
             for b in range(3)]
        w_, e_ = sh_west(u[0]), sh_east(u[2])
        return [u[1][t] + w_[t] + e_[t] for t in range(9)], up, mid, down

    def blur0(i, _):
        base = pl.multiple_of(i * 8 + 8, 8)
        out, _, _, _ = blur_rows(d0, base)
        for t in range(9):
            img[t, pl.ds(base, 8), :] = out[t]
        return 0

    lax.fori_loop(0, 34, blur0, 0, unroll=4)
    clear_outside(img)

    def apply_rows(field, base, n):
        up, mid, down = rows_of(img, base - 1), rows_of(img, base), rows_of(img, base + 1)
        v = [[blur_adjoint(up[t], mid[t], down[t], b) for t in range(9)] for b in range(3)]
        up, mid, down = rows_of(field, base - 1), rows_of(field, base), rows_of(field, base + 1)
        east = sh_east(mid)
        flux = [ce[t, pl.ds(base, 8), :] * (mid[t] - east[t]) for t in range(9)]
        e0 = sh_east(v[0])
        w2_ = sh_west([v[2][t] - flux[t] for t in range(9)])
        out = []
        for t in range(n):
            lap = (cs[t, pl.ds(base, 8), :] * (mid[t] - down[t])
                   - cs[t, pl.ds(base - 1, 8), :] * (up[t] - mid[t]))
            out.append(((v[1][t] + e0[t]) + (w2_[t] + flux[t])) + lap)
        return out, mid

    zero = jnp.zeros((8, 128), F32)

    def apply0(i, carry):
        gam, dad = carry
        base = pl.multiple_of(i * 8 + 16, 8)
        out, mid = apply_rows(d0, base, 9)
        q0[8, pl.ds(base, 8), :] = out[8]
        for t in range(8):
            q0[t, pl.ds(base, 8), :] = out[t]
            gam = gam + r0[t, pl.ds(base, 8), :] * mid[t]
            dad = dad + mid[t] * out[t]
        return gam, dad

    gam, dad = lax.fori_loop(0, 32, apply0, (zero, zero), unroll=4)

    src = jnp.concatenate([row_sums(q0, t) for t in range(8)], axis=1)
    cells = exact_dot(src, cmat[:, 0:128])
    b2 = cells * ctab[5, 0, 8:40, :]
    ctab[0, 0, 8:40, :] = b2

    sn2[...] = b2
    tbuf[0:8, :] = b2[24:32]
    tbuf[8:40, :] = b2
    tbuf[40:48, :] = b2[0:8]
    tt2[0] = tbuf[...].T
    copies2 = [(0, 0, sn2.at[pl.ds(0, 8), :], rs2), (1, 1, sn2.at[pl.ds(24, 8), :], rn2)]
    copies2 += side_copies(tt2, rx2, pl.ds(0, 1), 8)
    start_all(2, copies2)

    def apply0_rim(i, _):
        base = pl.multiple_of(i * 264 + 8, 8)
        out, _ = apply_rows(d0, base, 9)
        for t in range(9):
            q0[t, pl.ds(base, 8), :] = out[t]
        return 0

    lax.fori_loop(0, 2, apply0_rim, 0, unroll=2)

    def scaled(i, _):
        here = pl.ds(pl.multiple_of(i * 8 + 8, 8), 8)
        for t in range(9):
            w[t, here, :] = q0[t, here, :] * rfd[t, here, :]
        return 0

    lax.fori_loop(0, 34, scaled, 0, unroll=4)

    def blur1(i, _):
        base = pl.multiple_of(i * 8 + 8, 8)
        out, _, _, _ = blur_rows(w, base)
        for t in range(9):
            img[t, pl.ds(base, 8), :] = out[t]
        return 0

    lax.fori_loop(0, 34, blur1, 0, unroll=4)
    clear_outside(img)

    def apply1(i, carry):
        qw, waw = carry
        base = pl.multiple_of(i * 8 + 16, 8)
        out, mid = apply_rows(w, base, 8)
        for t in range(8):
            lw[t, pl.ds(base, 8), :] = out[t]
            qw = qw + q0[t, pl.ds(base, 8), :] * mid[t]
            waw = waw + mid[t] * out[t]
        return qw, waw

    qw, waw = lax.fori_loop(0, 32, apply1, (zero, zero), unroll=4)
    at_cells = exact_dot(
        jnp.concatenate([row_sums(lw, t) for t in range(8)], axis=1), cmat[:, 0:128])

    wait_recv_all(2, copies2)
    for dc, rows in ((-1, slice(0, 8)), (1, slice(120, 128))):
        hbuf[0, rows, :] = side(rx2, 0, dc, lane < 8, lane < 40)
    ctab[0, 1, :, :] = hbuf[0].T[0:48]
    ctab[0, 0, 0:8, :] = rn2[...]
    ctab[0, 0, 40:48, :] = rs2[...]
    jacobi()
    spread()

    z = zs[0, 16:48, :]
    ze = jnp.where(lane32 == 127, pltpu.roll(zs[1, 16:48, :], 127, 1), pltpu.roll(z, 127, 1))
    zw = jnp.where(lane32 == 0, pltpu.roll(zs[1, 16:48, :], 1, 1), pltpu.roll(z, 1, 1))
    g = [ctab[f, 0, 8:40, :] for f in range(5)]
    lap = (g[1] * (z - ze) + g[2] * (z - zw)) + (
        g[3] * (z - zs[0, 15:47, :]) + g[4] * (z - zs[0, 17:49, :]))

    def fold(x):
        return (x[0:8] + x[8:16]) + (x[16:24] + x[24:32])

    qw = qw + fold(cells * z)
    waw = waw + fold(z * (2.0 * at_cells + ctab[5, 1, 8:40, :] * lap))

    for n in range(6):
        rows = slice(8 * n, 8 * n + 8)
        mid = [zup[t, rows, :] for t in range(9)]
        east, west = sh_east(mid), sh_west(mid)
        for t in range(8):
            zeast[t, rows, :] = east[t]
            zwest[t, rows, :] = west[t]
    ksums = [(kk[0][b] + kk[1][b]) + kk[2][b] for b in range(3)]

    def lanes_conv(weights, parts):
        return weights[0] * parts[0] + weights[1] * parts[1] + weights[2] * parts[2]

    for n in range(4):
        at, up, down = (slice(8 * n + o, 8 * n + o + 8) for o in (8, 7, 9))
        for t in range(8):
            here = [x[t, at, :] for x in (zwest, zup, zeast)]
            north = [x[t, up, :] for x in (zwest, zup, zeast)]
            south = [x[t, down, :] for x in (zwest, zup, zeast)]
            mid = lanes_conv(ksums, here)
            first = mid + lanes_conv(kk[0], [p - q for p, q in zip(north, here)])
            last = mid + lanes_conv(kk[2], [p - q for p, q in zip(south, here)])
            waw = waw + (6.0 * (mid * mid) + (first * first + last * last))

    for n, part in enumerate((gam, dad, qw, waw)):
        red0[n:n + 1, :] = jnp.sum(part, axis=0, keepdims=True)
    red0[4:8, :] = jnp.zeros((4, 128), F32)
    redx[k8] = red0[...]
    for peer in zk_group:
        pltpu.make_async_remote_copy(
            red0, redx.at[k8], rsend.at[0], rrecv.at[0],
            device_id=peer, device_id_type=MESH).start()

    def add_coarse(i, _):
        here = pl.ds(pl.multiple_of(i * 8 + 8, 8), 8)
        for t in range(9):
            w[t, here, :] = w[t, here, :] + zup[t, pl.ds(i + 7, 1), :]
        return 0

    lax.fori_loop(0, 34, add_coarse, 0, unroll=4)
    lax.fori_loop(0, 34, blur1, 0, unroll=4)
    clear_outside(img)

    def apply2(i, _):
        base = pl.multiple_of(i * 8 + 16, 8)
        out, _ = apply_rows(w, base, 8)
        for t in range(8):
            lw[t, pl.ds(base, 8), :] = out[t]
        return 0

    def all_bytes(buf, n, sem):
        return pltpu.make_async_copy(buf.at[pl.ds(0, n)], buf.at[pl.ds(0, n)], sem)

    all_bytes(redx, zk - 1, rrecv.at[0]).wait()
    total = redx[0]
    for i in range(1, zk):
        total = total + redx[i]
    red1[...] = total
    redy[xy_me] = total
    for peer in xy_group:
        pltpu.make_async_remote_copy(
            red1, redy.at[xy_me], rsend.at[1], rrecv.at[1],
            device_id=peer, device_id_type=MESH).start()
    lax.fori_loop(0, 32, apply2, 0, unroll=4)
    wait_send_all(0, copies0)
    wait_send_all(1, copies1)
    wait_send_all(2, copies2)
    all_bytes(redx, zk - 1, rsend.at[0]).wait()
    all_bytes(redy, n_rows * ny - 1, rrecv.at[1]).wait()
    total = redy[0]
    for i in range(1, n_rows * ny):
        total = total + redy[i]
    value = jnp.broadcast_to(jnp.sum(total, axis=1, keepdims=True), (8, 128))
    g0 = jnp.broadcast_to(value[0:1], (8, 128))
    dq = jnp.broadcast_to(value[1:2], (8, 128))
    qws = jnp.broadcast_to(value[2:3], (8, 128))
    ws = jnp.broadcast_to(value[3:4], (8, 128))
    alpha = g0 / dq
    g1 = (g0 - alpha * dq) + alpha * (alpha * qws - dq)
    beta1 = 1.0 + g1 / g0
    dad1 = beta1 * (beta1 * dq - alpha * qws) + alpha * (alpha * ws - beta1 * qws)
    step = g1 / dad1
    ca = alpha + step * beta1
    cb = alpha * step

    coef[0] = ca
    coef[1] = cb
    all_bytes(redy, n_rows * ny - 1, rsend.at[1]).wait()


def finish_kernel(r0, d0, q0, w, lw, coef, sol_hbm, res_hbm, sol, res, out_sem):
    ca, cb = coef[0], coef[1]
    stores = []
    for n in range(8):
        def finish(i, _):
            dst_rows = pl.ds(pl.multiple_of(i * 8 + n * 32, 8), 8)
            src_rows = pl.ds(pl.multiple_of(i * 8 + n * 32 + 16, 8), 8)
            for t in range(8):
                lanes = slice(t * 128, t * 128 + 128)
                sol[dst_rows, lanes] = ca * d0[t, src_rows, :] - cb * w[t, src_rows, :]
                res[dst_rows, lanes] = (
                    r0[t, src_rows, :] - ca * q0[t, src_rows, :]) + cb * lw[t, src_rows, :]
            return 0

        lax.fori_loop(0, 4, finish, 0, unroll=2)
        rows = pl.ds(n * 32, 32)
        stores.append(pltpu.make_async_copy(sol.at[rows], sol_hbm.at[rows], out_sem.at[n]))
        stores.append(pltpu.make_async_copy(res.at[rows], res_hbm.at[rows], out_sem.at[8 + n]))
        stores[-2].start()
        stores[-1].start()
    for x in stores:
        x.wait()


def body(n_rows, n_cols, observed, class_map, class_weights, blur_kernel):
    zk = min(8, n_cols)
    ny = n_cols // zk
    big = pltpu.VMEM((9, 288, 128), F32)
    half = pltpu.VMEM((256, 1024), F32)

    def v(*shape):
        return pltpu.VMEM(shape, F32)

    scratch = [
        big, pltpu.VMEM((8, 256, 128), jnp.int32), big, big, big, big, big,
        v(9, 48, 128), pltpu.VMEM((1024, 256), BF16), pltpu.VMEM((128, 1152), BF16),
        v(128, 128), v(3, 128, 128), v(3, 128, 128), v(1, 128, 128), v(3, 128, 128),
        v(6, 2, 48, 128), v(2, 64, 128),
        v(8, 3, 16, 128), v(5, 32, 128), v(5, 8, 128), v(5, 8, 128), v(8, 3, 8, 128),
        v(32, 128), v(8, 128), v(8, 128), v(8, 1, 8, 128), v(8, 48, 128), v(8, 48, 128),
        v(8, 128), v(8, 128), v(zk, 8, 128), v(n_rows * ny, 8, 128),
        pltpu.SemaphoreType.DMA((16,)),
        pltpu.SemaphoreType.DMA((3, 10)), pltpu.SemaphoreType.DMA((3, 10)),
        pltpu.SemaphoreType.DMA((2,)), pltpu.SemaphoreType.DMA((2,)),
    ]
    hbm = pl.BlockSpec(memory_space=pltpu.HBM)
    vmem = pl.BlockSpec(memory_space=pltpu.VMEM)
    scalars = pl.BlockSpec(memory_space=pltpu.SMEM)
    field = pltpu.VMEM((9, 288, 128), F32)
    fields = pl.pallas_call(
        functools.partial(kernel, n_rows, n_cols, zk),
        out_shape=(field,) * 5 + (pltpu.VMEM((2, 8, 128), F32),),
        in_specs=[scalars, scalars, hbm, hbm],
        out_specs=(vmem,) * 6,
        scratch_shapes=scratch,
        compiler_params=pltpu.CompilerParams(
            collective_id=0, has_side_effects=True, vmem_limit_bytes=KERNEL_VMEM),
    )(class_weights, blur_kernel, observed, class_map)
    shape = jax.ShapeDtypeStruct(observed.shape, F32)
    return pl.pallas_call(
        finish_kernel,
        out_shape=(shape, shape),
        in_specs=[vmem] * 6,
        out_specs=(hbm, hbm),
        scratch_shapes=[half, half, pltpu.SemaphoreType.DMA((16,))],
        compiler_params=pltpu.CompilerParams(vmem_limit_bytes=FINISH_VMEM),
    )(*fields)


def solution(mesh):
    n_rows, n_cols = mesh.shape["rows"], mesh.shape["cols"]
    return jax.shard_map(
        functools.partial(body, n_rows, n_cols),
        mesh=mesh,
        in_specs=(P("rows", "cols"), P("rows", "cols"), P(), P()),
        out_specs=(P("rows", "cols"), P("rows", "cols")),
        check_vma=False,
    )
```

```python
import functools

import jax
import jax.numpy as jnp
from jax import lax
from jax.experimental import pallas as pl
from jax.experimental.pallas import tpu as pltpu
from jax.sharding import PartitionSpec as P

MESH = pl.DeviceIdType.MESH
OMEGA = 0.8
SWEEPS = 8
NB = ((-1, 0), (1, 0), (0, -1), (0, 1), (-1, -1), (-1, 1), (1, -1), (1, 1))
F32 = jnp.float32
BF16 = jnp.bfloat16
KERNEL_VMEM = 55 * 2**20
FINISH_VMEM = 16 * 2**20


def exact_dot(x, ones):
    hi = x.astype(BF16)
    lo = (x - hi.astype(F32)).astype(BF16)
    both = jnp.dot(jnp.concatenate([hi, lo], axis=0), ones, preferred_element_type=F32)
    return both[: x.shape[0]] + both[x.shape[0] :]


def kernel(
    n_rows, n_cols, zk,
    cw, bk, obs_hbm, cls_hbm, r0, d0, q0, w, lw, coef,
    obs, cls, cond, rfd, ce, cs, img,
    zup, cmat, bmat, umat, tbuf, tt0, tt2, hbuf, ctab, zs,
    rx0, sn1, sd1, rn1, rs1, rx1, pbuf, craw, sn2, rn2, rs2, rx2, zeast, zwest,
    red0, red1, redx, redy,
    in_sem, send_sem, recv_sem, rsend, rrecv,
):
    r = lax.axis_index("rows")
    c = lax.axis_index("cols")
    ny = n_cols // zk
    y, k8 = c // zk, lax.rem(c, zk)

    def ok(dr, dc):
        return (r + dr >= 0) & (r + dr < n_rows) & (c + dc >= 0) & (c + dc < n_cols)

    def dev(dr, dc):
        return (c + dc, r + dr)

    loads = []
    for t in range(8):
        lanes = pl.ds(t * 128, 128)
        loads.append(pltpu.make_async_copy(cls_hbm.at[:, lanes], cls.at[t], in_sem.at[t]))
        loads.append(pltpu.make_async_copy(
            obs_hbm.at[:, lanes], obs.at[t, pl.ds(16, 256), :], in_sem.at[8 + t]))
    for x in loads:
        x.start()

    for buf in (rx0, rn1, rs1, rx1, rn2, rs2, rx2, hbuf, zs):
        buf[...] = jnp.zeros(buf.shape, F32)
    pbuf[:, :, 0:16, :] = jnp.zeros((3, 8, 16, 128), F32)
    pbuf[:, :, 48:64, :] = jnp.zeros((3, 8, 16, 128), F32)
    for buf in (obs, cond):
        for t in range(8):
            buf[t, 8:16, :] = jnp.zeros((8, 128), F32)
            buf[t, 272:280, :] = jnp.zeros((8, 128), F32)

    bar = pltpu.get_barrier_semaphore()
    peers = zk + n_rows * ny - 2
    for dr, dc in NB:
        if dc == 0:
            continue
        fresh = ok(dr, dc)
        if dr == 0:
            fresh = fresh & (k8 == (zk - 1 if dc > 0 else 0))
        peers = peers + fresh.astype(jnp.int32)

        @pl.when(fresh)
        def _():
            pl.semaphore_signal(bar, inc=1, device_id=dev(dr, dc), device_id_type=MESH)
    nz = zk // 2
    z_me, core = k8 // 2, lax.rem(k8, 2)
    xy_me = r * ny + y

    def ring(o, n):
        return min(o, n - o)

    zk_far = sorted(((a, b) for a in range(nz) for b in range(2) if a or b),
                    key=lambda o: -(2 * ring(o[0], nz) + o[1]))
    xy_far = sorted(((a, b) for a in range(n_rows) for b in range(ny) if a or b),
                    key=lambda o: -(ring(o[0], n_rows) + ring(o[1], ny)))
    zk_group = [(y * zk + lax.rem(z_me + a, nz) * 2 + lax.rem(core + b, 2), r) for a, b in zk_far]
    xy_group = [(lax.rem(y + b, ny) * zk + k8, lax.rem(r + a, n_rows)) for a, b in xy_far]
    for peer in zk_group + xy_group:
        pl.semaphore_signal(bar, inc=1, device_id=peer, device_id_type=MESH)

    lane = lax.broadcasted_iota(jnp.int32, (8, 128), 1)
    sub = lax.broadcasted_iota(jnp.int32, (8, 128), 0)
    first_lane = lane == 0
    last_lane = lane == 127

    kk = [[bk[a, b] for b in range(3)] for a in range(3)]
    ksum = kk[0][0]
    ksq = kk[0][0] * kk[0][0]
    for a in range(3):
        for b in range(3):
            if a + b:
                ksum = ksum + kk[a][b]
                ksq = ksq + kk[a][b] * kk[a][b]

    def sh_east(v):
        rolled = [pltpu.roll(x, 127, 1) for x in v]
        n = len(v)
        return [jnp.where(last_lane, rolled[(t + 1) % n], rolled[t]) for t in range(n)]

    def sh_west(v):
        rolled = [pltpu.roll(x, 1, 1) for x in v]
        n = len(v)
        return [jnp.where(first_lane, rolled[(t - 1) % n], rolled[t]) for t in range(n)]

    def rows_of(ref, base, n=9):
        return [ref[t, pl.ds(base, 8), :] for t in range(n)]

    for x in loads:
        x.wait()

    w0, w1, w2, w3 = cw[0], cw[1], cw[2], cw[3]

    def cond_body(i, _):
        src = pl.multiple_of(i * 8, 8)
        dst = pl.multiple_of(i * 8 + 16, 8)
        for t in range(8):
            m = cls[t, pl.ds(src, 8), :]
            cond[t, pl.ds(dst, 8), :] = jnp.where(
                m == 0, w0, jnp.where(m == 1, w1, jnp.where(m == 2, w2, w3)))
        return 0

    lax.fori_loop(0, 32, cond_body, 0)

    def rim_tile(start, n):
        lanes = lax.broadcasted_iota(jnp.int32, (n, 128), 1)
        rows = pl.ds(start, n)
        left = jnp.where(lanes < 8, obs[0, rows, :], pltpu.roll(cond[0, rows, :], 8, 1))
        right = jnp.where(lanes >= 120, obs[7, rows, :], pltpu.roll(cond[7, rows, :], 120, 1))
        return jnp.where(lanes < 64, left, right)

    tt0[0] = rim_tile(16, 128).T
    tt0[1] = rim_tile(144, 128).T
    tbuf[...] = jnp.zeros(tbuf.shape, F32)
    tbuf[64:72, :] = rim_tile(264, 8)
    tbuf[72:80, :] = rim_tile(16, 8)
    tt0[2] = tbuf[...].T

    def side_copies(tt, rx, groups_diag, width):
        low, high = pl.ds(0, width), pl.ds(128 - width, width)
        out = []
        for n, (dr, dc) in enumerate(NB):
            if dc == 0:
                continue
            groups = pl.ds(0, tt.shape[0]) if dr == 0 else groups_diag
            rows = low if dc < 0 else high
            out.append((n, n, tt.at[groups, rows, :], rx.at[n, groups]))
        return out

    def start_all(phase, copies):
        for q, n, src, dst in copies:
            dr, dc = NB[n]
            @pl.when(ok(dr, dc))
            def _():
                pltpu.make_async_remote_copy(
                    src, dst, send_sem.at[phase, q], recv_sem.at[phase, q],
                    device_id=dev(dr, dc), device_id_type=MESH).start()

    def wait_recv_all(phase, copies):
        for q, n, src, dst in copies:
            dr, dc = NB[n]
            @pl.when(ok(-dr, -dc))
            def _():
                pltpu.make_async_remote_copy(
                    src, dst, send_sem.at[phase, q], recv_sem.at[phase, q],
                    device_id=dev(-dr, -dc), device_id_type=MESH).wait_recv()

    def wait_send_all(phase, copies):
        for q, n, src, dst in copies:
            dr, dc = NB[n]
            @pl.when(ok(dr, dc))
            def _():
                pltpu.make_async_remote_copy(
                    src, dst, send_sem.at[phase, q], recv_sem.at[phase, q],
                    device_id=dev(dr, dc), device_id_type=MESH).wait_send()

    third = pl.ds(2, 1)
    own, top, low = pl.ds(0, 8), pl.ds(16, 8), pl.ds(264, 8)
    above, below = pl.ds(8, 8), pl.ds(272, 8)
    copies0 = side_copies(tt0, rx0, third, 16)
    for q, field in ((0, obs), (8, cond)):
        copies0.append((q, 0, field.at[own, top, :], field.at[own, below, :]))
        copies0.append((q + 1, 1, field.at[own, low, :], field.at[own, above, :]))
    pl.semaphore_wait(bar, peers)
    start_all(0, copies0)

    ii = lax.broadcasted_iota(jnp.int32, (1024, 128), 0)
    jj = lax.broadcasted_iota(jnp.int32, (1024, 128), 1)
    for n, hit in enumerate((ii // 8 == jj, ii == jj * 8 + 7, ii == jj * 8)):
        cmat[:, 128 * n:128 * n + 128] = jnp.where(hit, 1.0, 0.0).astype(BF16)
    for b in range(3):
        hit = (ii + 7 + b) // 8 == jj + 1
        bmat[1024 * b:1024 * b + 1024, :] = jnp.where(hit, 1.0, 0.0).astype(BF16)
    ui = lax.broadcasted_iota(jnp.int32, (128, 1024), 0)
    uj = lax.broadcasted_iota(jnp.int32, (128, 1024), 1)
    umat[:, 0:1024] = jnp.where(uj // 8 == ui, 1.0, 0.0).astype(BF16)
    vi = lax.broadcasted_iota(jnp.int32, (128, 128), 0)
    vj = lax.broadcasted_iota(jnp.int32, (128, 128), 1)
    umat[:, 1024:1152] = jnp.where(
        ((vj < 64) & (vi == 0)) | ((vj >= 64) & (vi == 127)), 1.0, 0.0).astype(BF16)

    def row_sums(ref, t):
        total = ref[t, pl.ds(16, 32, stride=8), :]
        for s in range(1, 8):
            total = total + ref[t, pl.ds(16 + s, 32, stride=8), :]
        return total

    lane32 = lax.broadcasted_iota(jnp.int32, (32, 128), 1)
    row32 = lax.broadcasted_iota(jnp.int32, (32, 128), 0)
    lane48 = lax.broadcasted_iota(jnp.int32, (48, 128), 1)
    row48 = lax.broadcasted_iota(jnp.int32, (48, 128), 0)
    last48, first48 = lane48 == 127, lane48 == 0

    every = pl.ds(16, 32, stride=8)
    last_row = pl.ds(23, 32, stride=8)
    sums = exact_dot(jnp.concatenate([
        jnp.concatenate([row_sums(cond, t) for t in range(8)], axis=1),
        jnp.concatenate([cond[t, every, :] for t in range(8)], axis=1),
        jnp.concatenate([cond[t, last_row, :] for t in range(8)], axis=1)], axis=0), cmat[...])
    ec, wc = sums[0:32, 128:256], sums[0:32, 256:384]
    nc, sc = sums[32:64, 0:128], sums[64:96, 0:128]
    part = (
        0.5 * (ec + jnp.where(lane32 == 127, 0.0, pltpu.roll(wc, 127, 1))),
        0.5 * (wc + jnp.where(lane32 == 0, 0.0, pltpu.roll(ec, 1, 1))),
        0.5 * (nc + jnp.where(row32 == 0, 0.0, pltpu.roll(sc, 1, 0))),
        0.5 * (sc + jnp.where(row32 == 31, 0.0, pltpu.roll(nc, 31, 0))),
    )

    for t in range(8):
        pbuf[0, t, 16:48, :] = row_sums(obs, t)
        pbuf[1, t, 16:48, :] = obs[t, every, :]
        pbuf[2, t, 16:48, :] = obs[t, last_row, :]
    vb = [[], [], []]
    for t in range(8):
        mid = pbuf[0, t, 8:56, :]
        down = mid - pbuf[1, t, 8:56, :] + pbuf[1, t, 9:57, :]
        up = mid - pbuf[2, t, 8:56, :] + pbuf[2, t, 7:55, :]
        for b in range(3):
            vb[b].append(kk[0][b] * down + kk[1][b] * mid + kk[2][b] * up)
    own_source = exact_dot(jnp.concatenate(vb[0] + vb[1] + vb[2], axis=1), bmat[...])
    own_ring = jnp.where(lane48 == 7, pltpu.roll(vb[0][0], 7, 1),
                         jnp.where(lane48 == 8, pltpu.roll(vb[2][7], 9, 1), 0.0))

    for f in range(4):
        sn1[0, f] = part[f][0:8]
        sn1[1, f] = part[f][24:32]
        craw[f, 0, 8:40, :] = part[f]
    for h in range(2):
        sn1[0, 4 + h] = own_source[8 * h:8 * h + 8]
        sn1[0, 6 + h] = own_ring[8 * h:8 * h + 8]
        sn1[1, 4 + h] = own_source[32 + 8 * h:40 + 8 * h]
        sn1[1, 6 + h] = own_ring[32 + 8 * h:40 + 8 * h]
    for g in range(2):
        for h in range(2):
            field = part[2 * g + h]
            tbuf[64 * h:64 * h + 8, :] = field[24:32]
            tbuf[64 * h + 8:64 * h + 40, :] = field
            tbuf[64 * h + 40:64 * h + 48, :] = field[0:8]
        tile = tbuf[...].T
        sd1[0, g] = tile[0:8]
        sd1[1, g] = tile[120:128]
    tbuf[0:48, :] = own_source
    tbuf[64:112, :] = own_ring
    tile = tbuf[...].T
    in48 = lane < 48
    sd1[0, 2] = jnp.where(in48, pltpu.roll(tile[0:8], 64, 1), 0.0)
    sd1[0, 3] = jnp.where(in48, tile[0:8], 0.0)
    sd1[1, 2] = jnp.where(in48, tile[120:128], 0.0)
    sd1[1, 3] = jnp.where(in48, pltpu.roll(tile[8:16], 64, 1), 0.0)

    copies1 = [(0, 0, sn1.at[0], rs1), (1, 1, sn1.at[1], rn1)]
    for n, (dr, dc) in enumerate(NB):
        if dc:
            copies1.append((n, n, sd1.at[0 if dc < 0 else 1], rx1.at[n]))
    start_all(1, copies1)

    def blur_adjoint(up, mid, down, b):
        return kk[0][b] * down + kk[1][b] * mid + kk[2][b] * up

    def own_body(i, _):
        base = pl.multiple_of(i * 8 + 24, 8)
        here = pl.ds(base, 8)
        up, mid, down = rows_of(obs, base - 1, 8), rows_of(obs, base, 8), rows_of(obs, base + 1, 8)
        v = [[blur_adjoint(up[t], mid[t], down[t], b) for t in range(8)] for b in range(3)]
        e0 = [pltpu.roll(x, 127, 1) for x in v[0]]
        w2_ = [pltpu.roll(x, 1, 1) for x in v[2]]
        cm, csouth = rows_of(cond, base, 8), rows_of(cond, base + 1, 8)
        ceast = [pltpu.roll(x, 127, 1) for x in cm]
        for t in range(8):
            e = jnp.where(last_lane, e0[t + 1] if t < 7 else 0.0, e0[t])
            w_ = jnp.where(first_lane, w2_[t - 1] if t else 0.0, w2_[t])
            r0[t, here, :] = v[1][t] + e + w_
            ce[t, here, :] = 0.5 * (cm[t] + jnp.where(last_lane, ceast[t + 1] if t < 7 else 0.0, ceast[t]))
            cs[t, here, :] = 0.5 * (cm[t] + csouth[t])
        return 0

    lax.fori_loop(0, 30, own_body, 0, unroll=3)
    wait_recv_all(0, copies0)

    def side(rx, group, dc, in_north, in_center):
        north = rx[NB.index((1, dc)), group]
        center = rx[NB.index((0, dc)), group]
        south = rx[NB.index((-1, dc)), group]
        return jnp.where(in_north, north, jnp.where(in_center, center, south))

    lane64 = lax.rem(lane, 64)

    lane16 = lax.broadcasted_iota(jnp.int32, (16, 128), 1)
    for dc, rows in ((-1, slice(0, 16)), (1, slice(112, 128))):
        here = NB.index((0, dc))
        hbuf[0, rows, :] = rx0[here, 0]
        hbuf[1, rows, :] = rx0[here, 1]
        hbuf[2, rows, :] = side(rx0, 2, dc, lane16 < 72, lane16 < 0)

    def cond_of(x):
        lanes = lax.broadcasted_iota(jnp.int32, x.shape, 1)
        return jnp.where(lanes < 64, pltpu.roll(x, 120, 1), pltpu.roll(x, 8, 1))

    for g in range(2):
        tile = hbuf[g].T
        rows = slice(16 + 128 * g, 144 + 128 * g)
        obs[8, rows, :] = tile
        cond[8, rows, :] = cond_of(tile)
    tile = hbuf[2].T
    for rows, lo in ((slice(8, 16), 64), (slice(272, 280), 72)):
        obs[8, rows, :] = tile[lo:lo + 8]
        cond[8, rows, :] = cond_of(tile[lo:lo + 8])
    def side_body(i, _):
        base = pl.multiple_of(i * 8 + 24, 8)
        here = pl.ds(base, 8)
        def v(t, b):
            return blur_adjoint(obs[t, pl.ds(base - 1, 8), :], obs[t, here, :],
                                obs[t, pl.ds(base + 1, 8), :], b)
        e8, w8 = pltpu.roll(v(8, 0), 127, 1), pltpu.roll(v(8, 2), 1, 1)
        e0, w7 = pltpu.roll(v(0, 0), 127, 1), pltpu.roll(v(7, 2), 1, 1)
        r0[8, here, :] = v(8, 1) + jnp.where(last_lane, e0, e8) + jnp.where(first_lane, w7, w8)
        r0[7, here, :] = r0[7, here, :] + jnp.where(last_lane, e8, 0.0)
        r0[0, here, :] = r0[0, here, :] + jnp.where(first_lane, w8, 0.0)
        c8 = cond[8, here, :]
        ce8, ce0 = pltpu.roll(c8, 127, 1), pltpu.roll(cond[0, here, :], 127, 1)
        ce[8, here, :] = 0.5 * (c8 + jnp.where(last_lane, ce0, ce8))
        ce[7, here, :] = ce[7, here, :] + 0.5 * jnp.where(last_lane, ce8, 0.0)
        cs[8, here, :] = 0.5 * (c8 + cond[8, pl.ds(base + 1, 8), :])
        return 0

    lax.fori_loop(0, 30, side_body, 0, unroll=6)

    def outer_body(i, _):
        base = pl.multiple_of(jnp.where(i < 2, i * 8 + 8, i * 8 + 248), 8)
        here = pl.ds(base, 8)
        up, mid, down = rows_of(obs, base - 1), rows_of(obs, base), rows_of(obs, base + 1)
        v = [[blur_adjoint(up[t], mid[t], down[t], b) for t in range(9)] for b in range(3)]
        e0, w2_ = sh_east(v[0]), sh_west(v[2])
        cm, csouth = rows_of(cond, base), rows_of(cond, base + 1)
        ceast = sh_east(cm)
        for t in range(9):
            r0[t, here, :] = v[1][t] + e0[t] + w2_[t]
            ce[t, here, :] = 0.5 * (cm[t] + ceast[t])
            cs[t, here, :] = 0.5 * (cm[t] + csouth[t])
        return 0

    lax.fori_loop(0, 4, outer_body, 0, unroll=2)

    def clear_outside(ref):
        @pl.when(r == 0)
        def _():
            for t in range(9):
                ref[t, 8:16, :] = jnp.zeros((8, 128), F32)

        @pl.when(r == n_rows - 1)
        def _():
            for t in range(9):
                ref[t, 272:280, :] = jnp.zeros((8, 128), F32)

        lanes = lax.broadcasted_iota(jnp.int32, (272, 128), 1)

        @pl.when(c == 0)
        def _():
            ref[8, 8:280, :] = jnp.where(lanes < 64, ref[8, 8:280, :], 0.0)

        @pl.when(c == n_cols - 1)
        def _():
            ref[8, 8:280, :] = jnp.where(lanes >= 64, ref[8, 8:280, :], 0.0)

    def diag_body(i, _):
        base = pl.multiple_of(i * 8 + 8, 8)
        here = pl.ds(base, 8)
        east = rows_of(ce, base)
        west = sh_west(east)
        for t in range(9):
            total = (east[t] + west[t]) + (cs[t, here, :] + cs[t, pl.ds(base - 1, 8), :])
            rfd[t, here, :] = 1.0 / (ksq + total)
        return 0

    lax.fori_loop(0, 34, diag_body, 0, unroll=4)
    clear_outside(rfd)
    wait_recv_all(1, copies1)

    for f in range(4):
        craw[f, 0, 0:8, :] = rn1[f]
        craw[f, 0, 40:48, :] = rs1[f]
    hbuf[:, 8:16, :] = jnp.zeros((3, 8, 128), F32)
    hbuf[:, 112:120, :] = jnp.zeros((3, 8, 128), F32)
    for g in range(2):
        for dc, rows in ((-1, slice(0, 8)), (1, slice(120, 128))):
            hbuf[g, rows, :] = side(rx1, g, dc, lane64 < 8, lane64 < 40)
        tile = hbuf[g].T
        for h in range(2):
            craw[2 * g + h, 1] = tile[64 * h:64 * h + 48]
    for dc, blocks in ((-1, ((2, slice(8, 16)), (3, slice(0, 8)))),
                       (1, ((2, slice(120, 128)), (3, slice(112, 120))))):
        for q, rows in blocks:
            hbuf[2, rows, :] = rx1[NB.index((0, dc)), q] + (
                pltpu.roll(rx1[NB.index((1, dc)), q], 96, 1)
                + pltpu.roll(rx1[NB.index((-1, dc)), q], 32, 1))
    tile = hbuf[2].T[0:48]
    blank = jnp.zeros((16, 128), F32)

    def with_rows(own_part, q):
        return own_part + jnp.concatenate(
            [rn1[q], rn1[q + 1], blank, rs1[q], rs1[q + 1]], axis=0)

    ring_all = pltpu.roll(with_rows(own_ring, 6), 120, 1)
    source = [
        with_rows(own_source, 4) + jnp.where(
            last48, pltpu.roll(tile, 112, 1), jnp.where(first48, pltpu.roll(tile, 16, 1), 0.0)),
        tile + jnp.where(last48 | first48, ring_all, 0.0),
    ]
    for t in range(2):
        for a, b in ((7, 8), (39, 40)):
            both = craw[3, t, a:a + 1, :] + craw[2, t, b:b + 1, :]
            craw[3, t, a:a + 1, :] = both
            craw[2, t, b:b + 1, :] = both
    pe, pw = [craw[0, t] for t in range(2)], [craw[1, t] for t in range(2)]
    rows_ok = ((row48 >= 8) | (r > 0)) & ((row48 < 40) | (r < n_rows - 1))
    lanes_ok = ((lane48 >= 64) | (c < n_cols - 1)) & ((lane48 < 64) | (c > 0))
    for t in range(2):
        c_east = pe[t] + jnp.where(last48, pltpu.roll(pw[1 - t], 127, 1), 0.0)
        c_west = pw[t] + jnp.where(first48, pltpu.roll(pe[1 - t], 1, 1), 0.0)
        c_north, c_south = craw[2, t], craw[3, t]
        c_diag = 64.0 * (ksum * ksum) + c_east + c_west + c_north + c_south
        scale = jnp.where(rows_ok & lanes_ok if t else rows_ok, OMEGA / c_diag, 0.0)
        for f, x in enumerate((source[t], c_east, c_west, c_north, c_south)):
            ctab[f, t] = x * scale
        if t == 0:
            ctab[5, 0] = scale
            ctab[5, 1] = c_diag * (1.0 / OMEGA)

    def sweep(_, carry):
        z = [zs[t, 8:56, :] for t in range(2)]
        east = [pltpu.roll(x, 127, 1) for x in z]
        west = [pltpu.roll(x, 1, 1) for x in z]
        new = []
        for t in range(2):
            ze = jnp.where(last48, east[1 - t], east[t])
            zw = jnp.where(first48, west[1 - t], west[t])
            zn, zso = zs[t, 7:55, :], zs[t, 9:57, :]
            new.append((ctab[0, t] + (1.0 - OMEGA) * z[t])
                       + (ctab[1, t] * ze + ctab[2, t] * zw)
                       + (ctab[3, t] * zn + ctab[4, t] * zso))
        for t in range(2):
            zs[t, 8:56, :] = new[t]
        return carry

    def jacobi():
        for t in range(2):
            zs[t, 8:56, :] = ctab[0, t]
        lax.fori_loop(0, SWEEPS - 1, sweep, 0)

    def spread():
        up = exact_dot(zs[0, 8:56, :], umat[:, 0:1024])
        for t in range(8):
            zup[t] = up[:, 128 * t:128 * t + 128]
        zup[8] = exact_dot(zs[1, 8:56, :], umat[:, 1024:1152])

    jacobi()
    spread()

    def precond(field, out):
        def body(i, _):
            base = pl.multiple_of(i * 8 + 8, 8)
            here = pl.ds(base, 8)
            for t in range(9):
                out[t, here, :] = field[t, here, :] * rfd[t, here, :] + zup[t, pl.ds(i + 7, 1), :]
            return 0

        lax.fori_loop(0, 34, body, 0, unroll=4)

    precond(r0, d0)

    def blur_rows(ref, base):
        up, mid, down = rows_of(ref, base - 1), rows_of(ref, base), rows_of(ref, base + 1)
        u = [[kk[0][b] * up[t] + kk[1][b] * mid[t] + kk[2][b] * down[t] for t in range(9)]
             for b in range(3)]
        w_, e_ = sh_west(u[0]), sh_east(u[2])
        return [u[1][t] + w_[t] + e_[t] for t in range(9)], up, mid, down

    def blur0(i, _):
        base = pl.multiple_of(i * 8 + 8, 8)
        out, _, _, _ = blur_rows(d0, base)
        for t in range(9):
            img[t, pl.ds(base, 8), :] = out[t]
        return 0

    lax.fori_loop(0, 34, blur0, 0, unroll=4)
    clear_outside(img)

    def apply_rows(field, base, n):
        up, mid, down = rows_of(img, base - 1), rows_of(img, base), rows_of(img, base + 1)
        v = [[blur_adjoint(up[t], mid[t], down[t], b) for t in range(9)] for b in range(3)]
        up, mid, down = rows_of(field, base - 1), rows_of(field, base), rows_of(field, base + 1)
        east = sh_east(mid)
        flux = [ce[t, pl.ds(base, 8), :] * (mid[t] - east[t]) for t in range(9)]
        e0 = sh_east(v[0])
        w2_ = sh_west([v[2][t] - flux[t] for t in range(9)])
        out = []
        for t in range(n):
            lap = (cs[t, pl.ds(base, 8), :] * (mid[t] - down[t])
                   - cs[t, pl.ds(base - 1, 8), :] * (up[t] - mid[t]))
            out.append(((v[1][t] + e0[t]) + (w2_[t] + flux[t])) + lap)
        return out, mid

    zero = jnp.zeros((8, 128), F32)

    def apply0(i, carry):
        gam, dad = carry
        base = pl.multiple_of(i * 8 + 16, 8)
        out, mid = apply_rows(d0, base, 9)
        q0[8, pl.ds(base, 8), :] = out[8]
        for t in range(8):
            q0[t, pl.ds(base, 8), :] = out[t]
            gam = gam + r0[t, pl.ds(base, 8), :] * mid[t]
            dad = dad + mid[t] * out[t]
        return gam, dad

    gam, dad = lax.fori_loop(0, 32, apply0, (zero, zero), unroll=4)

    src = jnp.concatenate([row_sums(q0, t) for t in range(8)], axis=1)
    cells = exact_dot(src, cmat[:, 0:128])
    b2 = cells * ctab[5, 0, 8:40, :]
    ctab[0, 0, 8:40, :] = b2

    sn2[...] = b2
    tbuf[0:8, :] = b2[24:32]
    tbuf[8:40, :] = b2
    tbuf[40:48, :] = b2[0:8]
    tt2[0] = tbuf[...].T
    copies2 = [(0, 0, sn2.at[pl.ds(0, 8), :], rs2), (1, 1, sn2.at[pl.ds(24, 8), :], rn2)]
    copies2 += side_copies(tt2, rx2, pl.ds(0, 1), 8)
    start_all(2, copies2)

    def apply0_rim(i, _):
        base = pl.multiple_of(i * 264 + 8, 8)
        out, _ = apply_rows(d0, base, 9)
        for t in range(9):
            q0[t, pl.ds(base, 8), :] = out[t]
        return 0

    lax.fori_loop(0, 2, apply0_rim, 0, unroll=2)

    def scaled(i, _):
        here = pl.ds(pl.multiple_of(i * 8 + 8, 8), 8)
        for t in range(9):
            w[t, here, :] = q0[t, here, :] * rfd[t, here, :]
        return 0

    lax.fori_loop(0, 34, scaled, 0, unroll=4)

    def blur1(i, _):
        base = pl.multiple_of(i * 8 + 8, 8)
        out, _, _, _ = blur_rows(w, base)
        for t in range(9):
            img[t, pl.ds(base, 8), :] = out[t]
        return 0

    lax.fori_loop(0, 34, blur1, 0, unroll=4)
    clear_outside(img)

    def apply1(i, carry):
        qw, waw = carry
        base = pl.multiple_of(i * 8 + 16, 8)
        out, mid = apply_rows(w, base, 8)
        for t in range(8):
            lw[t, pl.ds(base, 8), :] = out[t]
            qw = qw + q0[t, pl.ds(base, 8), :] * mid[t]
            waw = waw + mid[t] * out[t]
        return qw, waw

    qw, waw = lax.fori_loop(0, 32, apply1, (zero, zero), unroll=4)
    at_cells = exact_dot(
        jnp.concatenate([row_sums(lw, t) for t in range(8)], axis=1), cmat[:, 0:128])

    wait_recv_all(2, copies2)
    for dc, rows in ((-1, slice(0, 8)), (1, slice(120, 128))):
        hbuf[0, rows, :] = side(rx2, 0, dc, lane < 8, lane < 40)
    ctab[0, 1, :, :] = hbuf[0].T[0:48]
    ctab[0, 0, 0:8, :] = rn2[...]
    ctab[0, 0, 40:48, :] = rs2[...]
    jacobi()
    spread()

    z = zs[0, 16:48, :]
    ze = jnp.where(lane32 == 127, pltpu.roll(zs[1, 16:48, :], 127, 1), pltpu.roll(z, 127, 1))
    zw = jnp.where(lane32 == 0, pltpu.roll(zs[1, 16:48, :], 1, 1), pltpu.roll(z, 1, 1))
    g = [ctab[f, 0, 8:40, :] for f in range(5)]
    lap = (g[1] * (z - ze) + g[2] * (z - zw)) + (
        g[3] * (z - zs[0, 15:47, :]) + g[4] * (z - zs[0, 17:49, :]))

    def fold(x):
        return (x[0:8] + x[8:16]) + (x[16:24] + x[24:32])

    qw = qw + fold(cells * z)
    waw = waw + fold(z * (2.0 * at_cells + ctab[5, 1, 8:40, :] * lap))

    for n in range(6):
        rows = slice(8 * n, 8 * n + 8)
        mid = [zup[t, rows, :] for t in range(9)]
        east, west = sh_east(mid), sh_west(mid)
        for t in range(8):
            zeast[t, rows, :] = east[t]
            zwest[t, rows, :] = west[t]
    ksums = [(kk[0][b] + kk[1][b]) + kk[2][b] for b in range(3)]

    def lanes_conv(weights, parts):
        return weights[0] * parts[0] + weights[1] * parts[1] + weights[2] * parts[2]

    for n in range(4):
        at, up, down = (slice(8 * n + o, 8 * n + o + 8) for o in (8, 7, 9))
        for t in range(8):
            here = [x[t, at, :] for x in (zwest, zup, zeast)]
            north = [x[t, up, :] for x in (zwest, zup, zeast)]
            south = [x[t, down, :] for x in (zwest, zup, zeast)]
            mid = lanes_conv(ksums, here)
            first = mid + lanes_conv(kk[0], [p - q for p, q in zip(north, here)])
            last = mid + lanes_conv(kk[2], [p - q for p, q in zip(south, here)])
            waw = waw + (6.0 * (mid * mid) + (first * first + last * last))

    for n, part in enumerate((gam, dad, qw, waw)):
        red0[n:n + 1, :] = jnp.sum(part, axis=0, keepdims=True)
    red0[4:8, :] = jnp.zeros((4, 128), F32)
    redx[k8] = red0[...]
    for peer in zk_group:
        pltpu.make_async_remote_copy(
            red0, redx.at[k8], rsend.at[0], rrecv.at[0],
            device_id=peer, device_id_type=MESH).start()

    def add_coarse(i, _):
        here = pl.ds(pl.multiple_of(i * 8 + 8, 8), 8)
        for t in range(9):
            w[t, here, :] = w[t, here, :] + zup[t, pl.ds(i + 7, 1), :]
        return 0

    lax.fori_loop(0, 34, add_coarse, 0, unroll=4)
    lax.fori_loop(0, 34, blur1, 0, unroll=4)
    clear_outside(img)

    def apply2(i, _):
        base = pl.multiple_of(i * 8 + 16, 8)
        out, _ = apply_rows(w, base, 8)
        for t in range(8):
            lw[t, pl.ds(base, 8), :] = out[t]
        return 0

    def all_bytes(buf, n, sem):
        return pltpu.make_async_copy(buf.at[pl.ds(0, n)], buf.at[pl.ds(0, n)], sem)

    all_bytes(redx, zk - 1, rrecv.at[0]).wait()
    total = redx[0]
    for i in range(1, zk):
        total = total + redx[i]
    red1[...] = total
    redy[xy_me] = total
    for peer in xy_group:
        pltpu.make_async_remote_copy(
            red1, redy.at[xy_me], rsend.at[1], rrecv.at[1],
            device_id=peer, device_id_type=MESH).start()
    lax.fori_loop(0, 32, apply2, 0, unroll=4)
    wait_send_all(0, copies0)
    wait_send_all(1, copies1)
    wait_send_all(2, copies2)
    all_bytes(redx, zk - 1, rsend.at[0]).wait()
    all_bytes(redy, n_rows * ny - 1, rrecv.at[1]).wait()
    total = redy[0]
    for i in range(1, n_rows * ny):
        total = total + redy[i]
    value = jnp.broadcast_to(jnp.sum(total, axis=1, keepdims=True), (8, 128))
    g0 = jnp.broadcast_to(value[0:1], (8, 128))
    dq = jnp.broadcast_to(value[1:2], (8, 128))
    qws = jnp.broadcast_to(value[2:3], (8, 128))
    ws = jnp.broadcast_to(value[3:4], (8, 128))
    alpha = g0 / dq
    g1 = (g0 - alpha * dq) + alpha * (alpha * qws - dq)
    beta1 = 1.0 + g1 / g0
    dad1 = beta1 * (beta1 * dq - alpha * qws) + alpha * (alpha * ws - beta1 * qws)
    step = g1 / dad1
    ca = alpha + step * beta1
    cb = alpha * step

    coef[0] = ca
    coef[1] = cb
    all_bytes(redy, n_rows * ny - 1, rsend.at[1]).wait()


def finish_kernel(r0, d0, q0, w, lw, coef, sol_hbm, res_hbm, sol, res, out_sem):
    ca, cb = coef[0], coef[1]
    stores = []
    for n in range(8):
        def finish(i, _):
            dst_rows = pl.ds(pl.multiple_of(i * 8 + n * 32, 8), 8)
            src_rows = pl.ds(pl.multiple_of(i * 8 + n * 32 + 16, 8), 8)
            for t in range(8):
                lanes = slice(t * 128, t * 128 + 128)
                sol[dst_rows, lanes] = ca * d0[t, src_rows, :] - cb * w[t, src_rows, :]
                res[dst_rows, lanes] = (
                    r0[t, src_rows, :] - ca * q0[t, src_rows, :]) + cb * lw[t, src_rows, :]
            return 0

        lax.fori_loop(0, 4, finish, 0, unroll=2)
        rows = pl.ds(n * 32, 32)
        stores.append(pltpu.make_async_copy(sol.at[rows], sol_hbm.at[rows], out_sem.at[n]))
        stores.append(pltpu.make_async_copy(res.at[rows], res_hbm.at[rows], out_sem.at[8 + n]))
        stores[-2].start()
        stores[-1].start()
    for x in stores:
        x.wait()


def body(n_rows, n_cols, observed, class_map, class_weights, blur_kernel):
    zk = min(8, n_cols)
    ny = n_cols // zk
    big = pltpu.VMEM((9, 288, 128), F32)
    half = pltpu.VMEM((256, 1024), F32)

    def v(*shape):
        return pltpu.VMEM(shape, F32)

    scratch = [
        big, pltpu.VMEM((8, 256, 128), jnp.int32), big, big, big, big, big,
        v(9, 48, 128), pltpu.VMEM((1024, 384), BF16), pltpu.VMEM((3072, 128), BF16),
        pltpu.VMEM((128, 1152), BF16),
        v(128, 128), v(3, 128, 128), v(1, 128, 128), v(3, 128, 128),
        v(6, 2, 48, 128), v(2, 64, 128),
        v(8, 3, 16, 128), v(2, 8, 8, 128), v(2, 4, 8, 128), v(8, 8, 128), v(8, 8, 128),
        v(8, 4, 8, 128), v(3, 8, 64, 128), v(4, 2, 48, 128),
        v(32, 128), v(8, 128), v(8, 128), v(8, 1, 8, 128), v(8, 48, 128), v(8, 48, 128),
        v(8, 128), v(8, 128), v(zk, 8, 128), v(n_rows * ny, 8, 128),
        pltpu.SemaphoreType.DMA((16,)),
        pltpu.SemaphoreType.DMA((3, 10)), pltpu.SemaphoreType.DMA((3, 10)),
        pltpu.SemaphoreType.DMA((2,)), pltpu.SemaphoreType.DMA((2,)),
    ]
    hbm = pl.BlockSpec(memory_space=pltpu.HBM)
    vmem = pl.BlockSpec(memory_space=pltpu.VMEM)
    scalars = pl.BlockSpec(memory_space=pltpu.SMEM)
    field = pltpu.VMEM((9, 288, 128), F32)
    fields = pl.pallas_call(
        functools.partial(kernel, n_rows, n_cols, zk),
        out_shape=(field,) * 5 + (pltpu.VMEM((2, 8, 128), F32),),
        in_specs=[scalars, scalars, hbm, hbm],
        out_specs=(vmem,) * 6,
        scratch_shapes=scratch,
        compiler_params=pltpu.CompilerParams(
            collective_id=0, has_side_effects=True, vmem_limit_bytes=KERNEL_VMEM),
    )(class_weights, blur_kernel, observed, class_map)
    shape = jax.ShapeDtypeStruct(observed.shape, F32)
    return pl.pallas_call(
        finish_kernel,
        out_shape=(shape, shape),
        in_specs=[vmem] * 6,
        out_specs=(hbm, hbm),
        scratch_shapes=[half, half, pltpu.SemaphoreType.DMA((16,))],
        compiler_params=pltpu.CompilerParams(vmem_limit_bytes=FINISH_VMEM),
    )(*fields)


def solution(mesh):
    n_rows, n_cols = mesh.shape["rows"], mesh.shape["cols"]
    return jax.shard_map(
        functools.partial(body, n_rows, n_cols),
        mesh=mesh,
        in_specs=(P("rows", "cols"), P("rows", "cols"), P(), P()),
        out_specs=(P("rows", "cols"), P("rows", "cols")),
        check_vma=False,
    )
```

```python
import functools

import jax
import jax.numpy as jnp
from jax import lax
from jax.experimental import pallas as pl
from jax.experimental.pallas import tpu as pltpu
from jax.sharding import PartitionSpec as P

MESH = pl.DeviceIdType.MESH
OMEGA = 0.8
SWEEPS = 8
NB = ((-1, 0), (1, 0), (0, -1), (0, 1), (-1, -1), (-1, 1), (1, -1), (1, 1))
F32 = jnp.float32
BF16 = jnp.bfloat16
KERNEL_VMEM = 55 * 2**20
FINISH_VMEM = 16 * 2**20


def exact_dot(x, ones):
    hi = x.astype(BF16)
    lo = (x - hi.astype(F32)).astype(BF16)
    both = jnp.dot(jnp.concatenate([hi, lo], axis=0), ones, preferred_element_type=F32)
    return both[: x.shape[0]] + both[x.shape[0] :]


def kernel(
    n_rows, n_cols, zk,
    cw, bk, obs_hbm, cls_hbm, r0, d0, q0, w, lw, coef,
    obs, cls, cond, rfd, ce, cs, img,
    zup, cmat, bmat, umat, tbuf, tt0, tt2, hbuf, ctab, zs,
    rx0, sn1, sd1, rn1, rs1, rx1, pbuf, craw, sn2, rn2, rs2, rx2, zeast, zwest,
    red0, red1, redx, redy,
    in_sem, send_sem, recv_sem, rsend, rrecv,
):
    r = lax.axis_index("rows")
    c = lax.axis_index("cols")
    ny = n_cols // zk
    y, k8 = c // zk, lax.rem(c, zk)

    def ok(dr, dc):
        return (r + dr >= 0) & (r + dr < n_rows) & (c + dc >= 0) & (c + dc < n_cols)

    def dev(dr, dc):
        return (c + dc, r + dr)

    loads = []
    for t in range(8):
        lanes = pl.ds(t * 128, 128)
        loads.append(pltpu.make_async_copy(cls_hbm.at[:, lanes], cls.at[t], in_sem.at[t]))
        loads.append(pltpu.make_async_copy(
            obs_hbm.at[:, lanes], obs.at[t, pl.ds(16, 256), :], in_sem.at[8 + t]))
    for x in loads:
        x.start()

    for buf in (rx0, rn1, rs1, rx1, rn2, rs2, rx2, hbuf, zs):
        buf[...] = jnp.zeros(buf.shape, F32)
    for buf in (obs, cond):
        for t in range(8):
            buf[t, 8:16, :] = jnp.zeros((8, 128), F32)
            buf[t, 272:280, :] = jnp.zeros((8, 128), F32)

    bar = pltpu.get_barrier_semaphore()
    peers = zk + n_rows * ny - 2
    for dr, dc in NB:
        if dc == 0:
            continue
        fresh = ok(dr, dc)
        if dr == 0:
            fresh = fresh & (k8 == (zk - 1 if dc > 0 else 0))
        peers = peers + fresh.astype(jnp.int32)

        @pl.when(fresh)
        def _():
            pl.semaphore_signal(bar, inc=1, device_id=dev(dr, dc), device_id_type=MESH)
    nz = zk // 2
    z_me, core = k8 // 2, lax.rem(k8, 2)
    xy_me = r * ny + y

    def ring(o, n):
        return min(o, n - o)

    zk_far = sorted(((a, b) for a in range(nz) for b in range(2) if a or b),
                    key=lambda o: -(2 * ring(o[0], nz) + o[1]))
    xy_far = sorted(((a, b) for a in range(n_rows) for b in range(ny) if a or b),
                    key=lambda o: -(ring(o[0], n_rows) + ring(o[1], ny)))
    zk_group = [(y * zk + lax.rem(z_me + a, nz) * 2 + lax.rem(core + b, 2), r) for a, b in zk_far]
    xy_group = [(lax.rem(y + b, ny) * zk + k8, lax.rem(r + a, n_rows)) for a, b in xy_far]
    for peer in zk_group + xy_group:
        pl.semaphore_signal(bar, inc=1, device_id=peer, device_id_type=MESH)

    lane = lax.broadcasted_iota(jnp.int32, (8, 128), 1)
    sub = lax.broadcasted_iota(jnp.int32, (8, 128), 0)
    first_lane = lane == 0
    last_lane = lane == 127

    kk = [[bk[a, b] for b in range(3)] for a in range(3)]
    ksum = kk[0][0]
    ksq = kk[0][0] * kk[0][0]
    for a in range(3):
        for b in range(3):
            if a + b:
                ksum = ksum + kk[a][b]
                ksq = ksq + kk[a][b] * kk[a][b]

    def sh_east(v):
        rolled = [pltpu.roll(x, 127, 1) for x in v]
        n = len(v)
        return [jnp.where(last_lane, rolled[(t + 1) % n], rolled[t]) for t in range(n)]

    def sh_west(v):
        rolled = [pltpu.roll(x, 1, 1) for x in v]
        n = len(v)
        return [jnp.where(first_lane, rolled[(t - 1) % n], rolled[t]) for t in range(n)]

    def rows_of(ref, base, n=9):
        return [ref[t, pl.ds(base, 8), :] for t in range(n)]

    ii = lax.broadcasted_iota(jnp.int32, (1024, 128), 0)
    jj = lax.broadcasted_iota(jnp.int32, (1024, 128), 1)
    cell, place = jnp.right_shift(ii, 3), jnp.bitwise_and(ii, 7)
    for n, hit in enumerate((cell == jj, (cell == jj) & (place == 7), (cell == jj) & (place == 0))):
        cmat[:, 128 * n:128 * n + 128] = jnp.where(hit, 1.0, 0.0).astype(BF16)
    for b in range(3):
        hit = jnp.right_shift(ii + (7 + b), 3) == jj + 1
        bmat[1024 * b:1024 * b + 1024, :] = jnp.where(hit, 1.0, 0.0).astype(BF16)

    for x in loads:
        x.wait()

    w0, w1, w2, w3 = cw[0], cw[1], cw[2], cw[3]

    def cond_body(i, _):
        src = pl.multiple_of(i * 8, 8)
        dst = pl.multiple_of(i * 8 + 16, 8)
        for t in range(8):
            m = cls[t, pl.ds(src, 8), :]
            cond[t, pl.ds(dst, 8), :] = jnp.where(
                m == 0, w0, jnp.where(m == 1, w1, jnp.where(m == 2, w2, w3)))
        return 0

    lax.fori_loop(0, 32, cond_body, 0)

    def rim_tile(start, n):
        lanes = lax.broadcasted_iota(jnp.int32, (n, 128), 1)
        rows = pl.ds(start, n)
        left = jnp.where(lanes < 8, obs[0, rows, :], pltpu.roll(cond[0, rows, :], 8, 1))
        right = jnp.where(lanes >= 120, obs[7, rows, :], pltpu.roll(cond[7, rows, :], 120, 1))
        return jnp.where(lanes < 64, left, right)

    tt0[0] = rim_tile(16, 128).T
    tt0[1] = rim_tile(144, 128).T
    tbuf[...] = jnp.zeros(tbuf.shape, F32)
    tbuf[64:72, :] = rim_tile(264, 8)
    tbuf[72:80, :] = rim_tile(16, 8)
    tt0[2] = tbuf[...].T

    def side_copies(tt, rx, groups_diag, width):
        low, high = pl.ds(0, width), pl.ds(128 - width, width)
        out = []
        for n, (dr, dc) in enumerate(NB):
            if dc == 0:
                continue
            groups = pl.ds(0, tt.shape[0]) if dr == 0 else groups_diag
            rows = low if dc < 0 else high
            out.append((n, n, tt.at[groups, rows, :], rx.at[n, groups]))
        return out

    def start_all(phase, copies):
        for q, n, src, dst in copies:
            dr, dc = NB[n]
            @pl.when(ok(dr, dc))
            def _():
                pltpu.make_async_remote_copy(
                    src, dst, send_sem.at[phase, q], recv_sem.at[phase, q],
                    device_id=dev(dr, dc), device_id_type=MESH).start()

    def wait_recv_all(phase, copies):
        for q, n, src, dst in copies:
            dr, dc = NB[n]
            @pl.when(ok(-dr, -dc))
            def _():
                pltpu.make_async_remote_copy(
                    src, dst, send_sem.at[phase, q], recv_sem.at[phase, q],
                    device_id=dev(-dr, -dc), device_id_type=MESH).wait_recv()

    def wait_send_all(phase, copies):
        for q, n, src, dst in copies:
            dr, dc = NB[n]
            @pl.when(ok(dr, dc))
            def _():
                pltpu.make_async_remote_copy(
                    src, dst, send_sem.at[phase, q], recv_sem.at[phase, q],
                    device_id=dev(dr, dc), device_id_type=MESH).wait_send()

    third = pl.ds(2, 1)
    own, top, low = pl.ds(0, 8), pl.ds(16, 8), pl.ds(264, 8)
    above, below = pl.ds(8, 8), pl.ds(272, 8)
    copies0 = side_copies(tt0, rx0, third, 16)
    for q, field in ((0, obs), (8, cond)):
        copies0.append((q, 0, field.at[own, top, :], field.at[own, below, :]))
        copies0.append((q + 1, 1, field.at[own, low, :], field.at[own, above, :]))
    pl.semaphore_wait(bar, peers)
    start_all(0, copies0)

    def row_sums(ref, t):
        total = ref[t, pl.ds(16, 32, stride=8), :]
        for s in range(1, 8):
            total = total + ref[t, pl.ds(16 + s, 32, stride=8), :]
        return total

    lane32 = lax.broadcasted_iota(jnp.int32, (32, 128), 1)
    row32 = lax.broadcasted_iota(jnp.int32, (32, 128), 0)
    lane48 = lax.broadcasted_iota(jnp.int32, (48, 128), 1)
    row48 = lax.broadcasted_iota(jnp.int32, (48, 128), 0)
    last48, first48 = lane48 == 127, lane48 == 0

    every = pl.ds(16, 32, stride=8)
    last_row = pl.ds(23, 32, stride=8)
    sums = exact_dot(jnp.concatenate([
        jnp.concatenate([row_sums(cond, t) for t in range(8)], axis=1),
        jnp.concatenate([cond[t, every, :] for t in range(8)], axis=1),
        jnp.concatenate([cond[t, last_row, :] for t in range(8)], axis=1)], axis=0), cmat[...])
    ec, wc = sums[0:32, 128:256], sums[0:32, 256:384]
    nc, sc = sums[32:64, 0:128], sums[64:96, 0:128]
    part = (
        0.5 * (ec + jnp.where(lane32 == 127, 0.0, pltpu.roll(wc, 127, 1))),
        0.5 * (wc + jnp.where(lane32 == 0, 0.0, pltpu.roll(ec, 1, 1))),
        0.5 * (nc + jnp.where(row32 == 0, 0.0, pltpu.roll(sc, 1, 0))),
        0.5 * (sc + jnp.where(row32 == 31, 0.0, pltpu.roll(nc, 31, 0))),
    )

    pbuf[:, :, 0:16, :] = jnp.zeros((3, 8, 16, 128), F32)
    pbuf[:, :, 48:64, :] = jnp.zeros((3, 8, 16, 128), F32)
    for t in range(8):
        pbuf[0, t, 16:48, :] = row_sums(obs, t)
        pbuf[1, t, 16:48, :] = obs[t, every, :]
        pbuf[2, t, 16:48, :] = obs[t, last_row, :]
    vb = [[], [], []]
    for t in range(8):
        mid = pbuf[0, t, 8:56, :]
        down = mid - pbuf[1, t, 8:56, :] + pbuf[1, t, 9:57, :]
        up = mid - pbuf[2, t, 8:56, :] + pbuf[2, t, 7:55, :]
        for b in range(3):
            vb[b].append(kk[0][b] * down + kk[1][b] * mid + kk[2][b] * up)
    own_source = exact_dot(jnp.concatenate(vb[0] + vb[1] + vb[2], axis=1), bmat[...])
    own_ring = jnp.where(lane48 == 7, pltpu.roll(vb[0][0], 7, 1),
                         jnp.where(lane48 == 8, pltpu.roll(vb[2][7], 9, 1), 0.0))

    for f in range(4):
        sn1[0, f] = part[f][0:8]
        sn1[1, f] = part[f][24:32]
        craw[f, 0, 8:40, :] = part[f]
    for h in range(2):
        sn1[0, 4 + h] = own_source[8 * h:8 * h + 8]
        sn1[0, 6 + h] = own_ring[8 * h:8 * h + 8]
        sn1[1, 4 + h] = own_source[32 + 8 * h:40 + 8 * h]
        sn1[1, 6 + h] = own_ring[32 + 8 * h:40 + 8 * h]
    for g in range(2):
        for h in range(2):
            field = part[2 * g + h]
            tbuf[64 * h:64 * h + 8, :] = field[24:32]
            tbuf[64 * h + 8:64 * h + 40, :] = field
            tbuf[64 * h + 40:64 * h + 48, :] = field[0:8]
        tile = tbuf[...].T
        sd1[0, g] = tile[0:8]
        sd1[1, g] = tile[120:128]
    tbuf[0:48, :] = own_source
    tbuf[64:112, :] = own_ring
    tile = tbuf[...].T
    in48 = lane < 48
    sd1[0, 2] = jnp.where(in48, pltpu.roll(tile[0:8], 64, 1), 0.0)
    sd1[0, 3] = jnp.where(in48, tile[0:8], 0.0)
    sd1[1, 2] = jnp.where(in48, tile[120:128], 0.0)
    sd1[1, 3] = jnp.where(in48, pltpu.roll(tile[8:16], 64, 1), 0.0)

    copies1 = [(0, 0, sn1.at[0], rs1), (1, 1, sn1.at[1], rn1)]
    for n, (dr, dc) in enumerate(NB):
        if dc:
            copies1.append((n, n, sd1.at[0 if dc < 0 else 1], rx1.at[n]))
    start_all(1, copies1)

    ui = lax.broadcasted_iota(jnp.int32, (128, 1024), 0)
    uj = lax.broadcasted_iota(jnp.int32, (128, 1024), 1)
    umat[:, 0:1024] = jnp.where(jnp.right_shift(uj, 3) == ui, 1.0, 0.0).astype(BF16)
    vi = lax.broadcasted_iota(jnp.int32, (128, 128), 0)
    vj = lax.broadcasted_iota(jnp.int32, (128, 128), 1)
    umat[:, 1024:1152] = jnp.where(
        ((vj < 64) & (vi == 0)) | ((vj >= 64) & (vi == 127)), 1.0, 0.0).astype(BF16)

    def blur_adjoint(up, mid, down, b):
        return kk[0][b] * down + kk[1][b] * mid + kk[2][b] * up

    def own_body(i, _):
        base = pl.multiple_of(i * 8 + 24, 8)
        here = pl.ds(base, 8)
        up, mid, down = rows_of(obs, base - 1, 8), rows_of(obs, base, 8), rows_of(obs, base + 1, 8)
        v = [[blur_adjoint(up[t], mid[t], down[t], b) for t in range(8)] for b in range(3)]
        e0 = [pltpu.roll(x, 127, 1) for x in v[0]]
        w2_ = [pltpu.roll(x, 1, 1) for x in v[2]]
        cm, csouth = rows_of(cond, base, 8), rows_of(cond, base + 1, 8)
        ceast = [pltpu.roll(x, 127, 1) for x in cm]
        for t in range(8):
            e = jnp.where(last_lane, e0[t + 1] if t < 7 else 0.0, e0[t])
            w_ = jnp.where(first_lane, w2_[t - 1] if t else 0.0, w2_[t])
            r0[t, here, :] = v[1][t] + e + w_
            ce[t, here, :] = 0.5 * (cm[t] + jnp.where(last_lane, ceast[t + 1] if t < 7 else 0.0, ceast[t]))
            cs[t, here, :] = 0.5 * (cm[t] + csouth[t])
        return 0

    lax.fori_loop(0, 30, own_body, 0, unroll=3)
    wait_recv_all(0, copies0)

    def side(rx, group, dc, in_north, in_center):
        north = rx[NB.index((1, dc)), group]
        center = rx[NB.index((0, dc)), group]
        south = rx[NB.index((-1, dc)), group]
        return jnp.where(in_north, north, jnp.where(in_center, center, south))

    lane64 = lax.rem(lane, 64)

    lane16 = lax.broadcasted_iota(jnp.int32, (16, 128), 1)
    for dc, rows in ((-1, slice(0, 16)), (1, slice(112, 128))):
        here = NB.index((0, dc))
        hbuf[0, rows, :] = rx0[here, 0]
        hbuf[1, rows, :] = rx0[here, 1]
        hbuf[2, rows, :] = side(rx0, 2, dc, lane16 < 72, lane16 < 0)

    def cond_of(x):
        lanes = lax.broadcasted_iota(jnp.int32, x.shape, 1)
        return jnp.where(lanes < 64, pltpu.roll(x, 120, 1), pltpu.roll(x, 8, 1))

    for g in range(2):
        tile = hbuf[g].T
        rows = slice(16 + 128 * g, 144 + 128 * g)
        obs[8, rows, :] = tile
        cond[8, rows, :] = cond_of(tile)
    tile = hbuf[2].T
    for rows, lo in ((slice(8, 16), 64), (slice(272, 280), 72)):
        obs[8, rows, :] = tile[lo:lo + 8]
        cond[8, rows, :] = cond_of(tile[lo:lo + 8])
    def side_body(i, _):
        base = pl.multiple_of(i * 8 + 24, 8)
        here = pl.ds(base, 8)
        def v(t, b):
            return blur_adjoint(obs[t, pl.ds(base - 1, 8), :], obs[t, here, :],
                                obs[t, pl.ds(base + 1, 8), :], b)
        e8, w8 = pltpu.roll(v(8, 0), 127, 1), pltpu.roll(v(8, 2), 1, 1)
        e0, w7 = pltpu.roll(v(0, 0), 127, 1), pltpu.roll(v(7, 2), 1, 1)
        r0[8, here, :] = v(8, 1) + jnp.where(last_lane, e0, e8) + jnp.where(first_lane, w7, w8)
        r0[7, here, :] = r0[7, here, :] + jnp.where(last_lane, e8, 0.0)
        r0[0, here, :] = r0[0, here, :] + jnp.where(first_lane, w8, 0.0)
        c8 = cond[8, here, :]
        ce8, ce0 = pltpu.roll(c8, 127, 1), pltpu.roll(cond[0, here, :], 127, 1)
        ce[8, here, :] = 0.5 * (c8 + jnp.where(last_lane, ce0, ce8))
        ce[7, here, :] = ce[7, here, :] + 0.5 * jnp.where(last_lane, ce8, 0.0)
        cs[8, here, :] = 0.5 * (c8 + cond[8, pl.ds(base + 1, 8), :])
        return 0

    lax.fori_loop(0, 30, side_body, 0, unroll=6)

    def outer_body(i, _):
        base = pl.multiple_of(jnp.where(i < 2, i * 8 + 8, i * 8 + 248), 8)
        here = pl.ds(base, 8)
        up, mid, down = rows_of(obs, base - 1), rows_of(obs, base), rows_of(obs, base + 1)
        v = [[blur_adjoint(up[t], mid[t], down[t], b) for t in range(9)] for b in range(3)]
        e0, w2_ = sh_east(v[0]), sh_west(v[2])
        cm, csouth = rows_of(cond, base), rows_of(cond, base + 1)
        ceast = sh_east(cm)
        for t in range(9):
            r0[t, here, :] = v[1][t] + e0[t] + w2_[t]
            ce[t, here, :] = 0.5 * (cm[t] + ceast[t])
            cs[t, here, :] = 0.5 * (cm[t] + csouth[t])
        return 0

    lax.fori_loop(0, 4, outer_body, 0, unroll=4)

    def clear_outside(ref):
        @pl.when(r == 0)
        def _():
            for t in range(9):
                ref[t, 8:16, :] = jnp.zeros((8, 128), F32)

        @pl.when(r == n_rows - 1)
        def _():
            for t in range(9):
                ref[t, 272:280, :] = jnp.zeros((8, 128), F32)

        lanes = lax.broadcasted_iota(jnp.int32, (272, 128), 1)

        @pl.when(c == 0)
        def _():
            ref[8, 8:280, :] = jnp.where(lanes < 64, ref[8, 8:280, :], 0.0)

        @pl.when(c == n_cols - 1)
        def _():
            ref[8, 8:280, :] = jnp.where(lanes >= 64, ref[8, 8:280, :], 0.0)

    def diag_body(i, _):
        base = pl.multiple_of(i * 8 + 8, 8)
        here = pl.ds(base, 8)
        east = rows_of(ce, base)
        west = sh_west(east)
        for t in range(9):
            total = (east[t] + west[t]) + (cs[t, here, :] + cs[t, pl.ds(base - 1, 8), :])
            rfd[t, here, :] = 1.0 / (ksq + total)
        return 0

    lax.fori_loop(0, 34, diag_body, 0, unroll=4)
    clear_outside(rfd)
    wait_recv_all(1, copies1)

    for f in range(4):
        craw[f, 0, 0:8, :] = rn1[f]
        craw[f, 0, 40:48, :] = rs1[f]
    hbuf[:, 8:16, :] = jnp.zeros((3, 8, 128), F32)
    hbuf[:, 112:120, :] = jnp.zeros((3, 8, 128), F32)
    for g in range(2):
        for dc, rows in ((-1, slice(0, 8)), (1, slice(120, 128))):
            hbuf[g, rows, :] = side(rx1, g, dc, lane64 < 8, lane64 < 40)
        tile = hbuf[g].T
        for h in range(2):
            craw[2 * g + h, 1] = tile[64 * h:64 * h + 48]
    for dc, blocks in ((-1, ((2, slice(8, 16)), (3, slice(0, 8)))),
                       (1, ((2, slice(120, 128)), (3, slice(112, 120))))):
        for q, rows in blocks:
            hbuf[2, rows, :] = rx1[NB.index((0, dc)), q] + (
                pltpu.roll(rx1[NB.index((1, dc)), q], 96, 1)
                + pltpu.roll(rx1[NB.index((-1, dc)), q], 32, 1))
    tile = hbuf[2].T[0:48]
    blank = jnp.zeros((16, 128), F32)

    def with_rows(own_part, q):
        return own_part + jnp.concatenate(
            [rn1[q], rn1[q + 1], blank, rs1[q], rs1[q + 1]], axis=0)

    ring_all = pltpu.roll(with_rows(own_ring, 6), 120, 1)
    source = [
        with_rows(own_source, 4) + jnp.where(
            last48, pltpu.roll(tile, 112, 1), jnp.where(first48, pltpu.roll(tile, 16, 1), 0.0)),
        tile + jnp.where(last48 | first48, ring_all, 0.0),
    ]
    for t in range(2):
        for a, b in ((7, 8), (39, 40)):
            both = craw[3, t, a:a + 1, :] + craw[2, t, b:b + 1, :]
            craw[3, t, a:a + 1, :] = both
            craw[2, t, b:b + 1, :] = both
    pe, pw = [craw[0, t] for t in range(2)], [craw[1, t] for t in range(2)]
    rows_ok = ((row48 >= 8) | (r > 0)) & ((row48 < 40) | (r < n_rows - 1))
    lanes_ok = ((lane48 >= 64) | (c < n_cols - 1)) & ((lane48 < 64) | (c > 0))
    for t in range(2):
        c_east = pe[t] + jnp.where(last48, pltpu.roll(pw[1 - t], 127, 1), 0.0)
        c_west = pw[t] + jnp.where(first48, pltpu.roll(pe[1 - t], 1, 1), 0.0)
        c_north, c_south = craw[2, t], craw[3, t]
        c_diag = 64.0 * (ksum * ksum) + c_east + c_west + c_north + c_south
        scale = jnp.where(rows_ok & lanes_ok if t else rows_ok, OMEGA / c_diag, 0.0)
        for f, x in enumerate((source[t], c_east, c_west, c_north, c_south)):
            ctab[f, t] = x * scale
        if t == 0:
            ctab[5, 0] = scale
            ctab[5, 1] = c_diag * (1.0 / OMEGA)

    def sweep(_, carry):
        z = [zs[t, 8:56, :] for t in range(2)]
        east = [pltpu.roll(x, 127, 1) for x in z]
        west = [pltpu.roll(x, 1, 1) for x in z]
        new = []
        for t in range(2):
            ze = jnp.where(last48, east[1 - t], east[t])
            zw = jnp.where(first48, west[1 - t], west[t])
            zn, zso = zs[t, 7:55, :], zs[t, 9:57, :]
            new.append((ctab[0, t] + (1.0 - OMEGA) * z[t])
                       + (ctab[1, t] * ze + ctab[2, t] * zw)
                       + (ctab[3, t] * zn + ctab[4, t] * zso))
        for t in range(2):
            zs[t, 8:56, :] = new[t]
        return carry

    def jacobi():
        for t in range(2):
            zs[t, 8:56, :] = ctab[0, t]
        lax.fori_loop(0, SWEEPS - 1, sweep, 0, unroll=SWEEPS - 1)

    def spread():
        up = exact_dot(zs[0, 8:56, :], umat[:, 0:1024])
        for t in range(8):
            zup[t] = up[:, 128 * t:128 * t + 128]
        zup[8] = exact_dot(zs[1, 8:56, :], umat[:, 1024:1152])

    jacobi()
    spread()

    def precond(field, out):
        def body(i, _):
            base = pl.multiple_of(i * 8 + 8, 8)
            here = pl.ds(base, 8)
            for t in range(9):
                out[t, here, :] = field[t, here, :] * rfd[t, here, :] + zup[t, pl.ds(i + 7, 1), :]
            return 0

        lax.fori_loop(0, 34, body, 0, unroll=4)

    precond(r0, d0)

    def blur_rows(ref, base):
        up, mid, down = rows_of(ref, base - 1), rows_of(ref, base), rows_of(ref, base + 1)
        u = [[kk[0][b] * up[t] + kk[1][b] * mid[t] + kk[2][b] * down[t] for t in range(9)]
             for b in range(3)]
        w_, e_ = sh_west(u[0]), sh_east(u[2])
        return [u[1][t] + w_[t] + e_[t] for t in range(9)], up, mid, down

    def blur0(i, _):
        base = pl.multiple_of(i * 8 + 8, 8)
        out, _, _, _ = blur_rows(d0, base)
        for t in range(9):
            img[t, pl.ds(base, 8), :] = out[t]
        return 0

    lax.fori_loop(0, 34, blur0, 0, unroll=4)
    clear_outside(img)

    def apply_rows(field, base, n):
        up, mid, down = rows_of(img, base - 1), rows_of(img, base), rows_of(img, base + 1)
        v = [[blur_adjoint(up[t], mid[t], down[t], b) for t in range(9)] for b in range(3)]
        up, mid, down = rows_of(field, base - 1), rows_of(field, base), rows_of(field, base + 1)
        east = sh_east(mid)
        flux = [ce[t, pl.ds(base, 8), :] * (mid[t] - east[t]) for t in range(9)]
        e0 = sh_east(v[0])
        w2_ = sh_west([v[2][t] - flux[t] for t in range(9)])
        out = []
        for t in range(n):
            lap = (cs[t, pl.ds(base, 8), :] * (mid[t] - down[t])
                   - cs[t, pl.ds(base - 1, 8), :] * (up[t] - mid[t]))
            out.append(((v[1][t] + e0[t]) + (w2_[t] + flux[t])) + lap)
        return out, mid

    zero = jnp.zeros((8, 128), F32)

    def apply0(i, carry):
        gam, dad = carry
        base = pl.multiple_of(i * 8 + 16, 8)
        out, mid = apply_rows(d0, base, 9)
        q0[8, pl.ds(base, 8), :] = out[8]
        for t in range(8):
            q0[t, pl.ds(base, 8), :] = out[t]
            gam = gam + r0[t, pl.ds(base, 8), :] * mid[t]
            dad = dad + mid[t] * out[t]
        return gam, dad

    gam, dad = lax.fori_loop(0, 32, apply0, (zero, zero), unroll=4)

    src = jnp.concatenate([row_sums(q0, t) for t in range(8)], axis=1)
    cells = exact_dot(src, cmat[:, 0:128])
    b2 = cells * ctab[5, 0, 8:40, :]
    ctab[0, 0, 8:40, :] = b2

    sn2[...] = b2
    tbuf[0:8, :] = b2[24:32]
    tbuf[8:40, :] = b2
    tbuf[40:48, :] = b2[0:8]
    tt2[0] = tbuf[...].T
    copies2 = [(0, 0, sn2.at[pl.ds(0, 8), :], rs2), (1, 1, sn2.at[pl.ds(24, 8), :], rn2)]
    copies2 += side_copies(tt2, rx2, pl.ds(0, 1), 8)
    start_all(2, copies2)

    def apply0_rim(i, _):
        base = pl.multiple_of(i * 264 + 8, 8)
        out, _ = apply_rows(d0, base, 9)
        for t in range(9):
            q0[t, pl.ds(base, 8), :] = out[t]
        return 0

    lax.fori_loop(0, 2, apply0_rim, 0, unroll=2)

    def scaled(i, _):
        here = pl.ds(pl.multiple_of(i * 8 + 8, 8), 8)
        for t in range(9):
            w[t, here, :] = q0[t, here, :] * rfd[t, here, :]
        return 0

    lax.fori_loop(0, 34, scaled, 0, unroll=4)

    def blur1(i, _):
        base = pl.multiple_of(i * 8 + 8, 8)
        out, _, _, _ = blur_rows(w, base)
        for t in range(9):
            img[t, pl.ds(base, 8), :] = out[t]
        return 0

    lax.fori_loop(0, 34, blur1, 0, unroll=4)
    clear_outside(img)

    def apply1(i, carry):
        qw, waw = carry
        base = pl.multiple_of(i * 8 + 16, 8)
        out, mid = apply_rows(w, base, 8)
        for t in range(8):
            lw[t, pl.ds(base, 8), :] = out[t]
            qw = qw + q0[t, pl.ds(base, 8), :] * mid[t]
            waw = waw + mid[t] * out[t]
        return qw, waw

    qw, waw = lax.fori_loop(0, 32, apply1, (zero, zero), unroll=4)
    at_cells = exact_dot(
        jnp.concatenate([row_sums(lw, t) for t in range(8)], axis=1), cmat[:, 0:128])

    wait_recv_all(2, copies2)
    for dc, rows in ((-1, slice(0, 8)), (1, slice(120, 128))):
        hbuf[0, rows, :] = side(rx2, 0, dc, lane < 8, lane < 40)
    ctab[0, 1, :, :] = hbuf[0].T[0:48]
    ctab[0, 0, 0:8, :] = rn2[...]
    ctab[0, 0, 40:48, :] = rs2[...]
    jacobi()
    spread()

    z = zs[0, 16:48, :]
    ze = jnp.where(lane32 == 127, pltpu.roll(zs[1, 16:48, :], 127, 1), pltpu.roll(z, 127, 1))
    zw = jnp.where(lane32 == 0, pltpu.roll(zs[1, 16:48, :], 1, 1), pltpu.roll(z, 1, 1))
    g = [ctab[f, 0, 8:40, :] for f in range(5)]
    lap = (g[1] * (z - ze) + g[2] * (z - zw)) + (
        g[3] * (z - zs[0, 15:47, :]) + g[4] * (z - zs[0, 17:49, :]))

    def fold(x):
        return (x[0:8] + x[8:16]) + (x[16:24] + x[24:32])

    qw = qw + fold(cells * z)
    waw = waw + fold(z * (2.0 * at_cells + ctab[5, 1, 8:40, :] * lap))

    for n in range(6):
        rows = slice(8 * n, 8 * n + 8)
        mid = [zup[t, rows, :] for t in range(9)]
        east, west = sh_east(mid), sh_west(mid)
        for t in range(8):
            zeast[t, rows, :] = east[t]
            zwest[t, rows, :] = west[t]
    ksums = [(kk[0][b] + kk[1][b]) + kk[2][b] for b in range(3)]

    def lanes_conv(weights, parts):
        return weights[0] * parts[0] + weights[1] * parts[1] + weights[2] * parts[2]

    for n in range(4):
        at, up, down = (slice(8 * n + o, 8 * n + o + 8) for o in (8, 7, 9))
        for t in range(8):
            here = [x[t, at, :] for x in (zwest, zup, zeast)]
            north = [x[t, up, :] for x in (zwest, zup, zeast)]
            south = [x[t, down, :] for x in (zwest, zup, zeast)]
            mid = lanes_conv(ksums, here)
            first = mid + lanes_conv(kk[0], [p - q for p, q in zip(north, here)])
            last = mid + lanes_conv(kk[2], [p - q for p, q in zip(south, here)])
            waw = waw + (6.0 * (mid * mid) + (first * first + last * last))

    for n, part in enumerate((gam, dad, qw, waw)):
        red0[n:n + 1, :] = jnp.sum(part, axis=0, keepdims=True)
    red0[4:8, :] = jnp.zeros((4, 128), F32)
    redx[k8] = red0[...]
    for peer in zk_group:
        pltpu.make_async_remote_copy(
            red0, redx.at[k8], rsend.at[0], rrecv.at[0],
            device_id=peer, device_id_type=MESH).start()

    def add_coarse(i, _):
        here = pl.ds(pl.multiple_of(i * 8 + 8, 8), 8)
        for t in range(9):
            w[t, here, :] = w[t, here, :] + zup[t, pl.ds(i + 7, 1), :]
        return 0

    lax.fori_loop(0, 34, add_coarse, 0, unroll=4)
    lax.fori_loop(0, 34, blur1, 0, unroll=4)
    clear_outside(img)

    def apply2(i, _):
        base = pl.multiple_of(i * 8 + 16, 8)
        out, _ = apply_rows(w, base, 8)
        for t in range(8):
            lw[t, pl.ds(base, 8), :] = out[t]
        return 0

    def all_bytes(buf, n, sem):
        return pltpu.make_async_copy(buf.at[pl.ds(0, n)], buf.at[pl.ds(0, n)], sem)

    all_bytes(redx, zk - 1, rrecv.at[0]).wait()
    total = redx[0]
    for i in range(1, zk):
        total = total + redx[i]
    red1[...] = total
    redy[xy_me] = total
    for peer in xy_group:
        pltpu.make_async_remote_copy(
            red1, redy.at[xy_me], rsend.at[1], rrecv.at[1],
            device_id=peer, device_id_type=MESH).start()
    lax.fori_loop(0, 32, apply2, 0, unroll=4)
    wait_send_all(0, copies0)
    wait_send_all(1, copies1)
    wait_send_all(2, copies2)
    all_bytes(redx, zk - 1, rsend.at[0]).wait()
    all_bytes(redy, n_rows * ny - 1, rrecv.at[1]).wait()
    total = redy[0]
    for i in range(1, n_rows * ny):
        total = total + redy[i]
    value = jnp.broadcast_to(jnp.sum(total, axis=1, keepdims=True), (8, 128))
    g0 = jnp.broadcast_to(value[0:1], (8, 128))
    dq = jnp.broadcast_to(value[1:2], (8, 128))
    qws = jnp.broadcast_to(value[2:3], (8, 128))
    ws = jnp.broadcast_to(value[3:4], (8, 128))
    alpha = g0 / dq
    g1 = (g0 - alpha * dq) + alpha * (alpha * qws - dq)
    beta1 = 1.0 + g1 / g0
    dad1 = beta1 * (beta1 * dq - alpha * qws) + alpha * (alpha * ws - beta1 * qws)
    step = g1 / dad1
    ca = alpha + step * beta1
    cb = alpha * step

    coef[0] = ca
    coef[1] = cb
    all_bytes(redy, n_rows * ny - 1, rsend.at[1]).wait()


def finish_kernel(r0, d0, q0, w, lw, coef, sol_hbm, res_hbm, sol, res, out_sem):
    ca, cb = coef[0], coef[1]
    stores = []
    for n in range(8):
        def finish(i, _):
            dst_rows = pl.ds(pl.multiple_of(i * 8 + n * 32, 8), 8)
            src_rows = pl.ds(pl.multiple_of(i * 8 + n * 32 + 16, 8), 8)
            for t in range(8):
                lanes = slice(t * 128, t * 128 + 128)
                sol[dst_rows, lanes] = ca * d0[t, src_rows, :] - cb * w[t, src_rows, :]
                res[dst_rows, lanes] = (
                    r0[t, src_rows, :] - ca * q0[t, src_rows, :]) + cb * lw[t, src_rows, :]
            return 0

        lax.fori_loop(0, 4, finish, 0, unroll=2)
        rows = pl.ds(n * 32, 32)
        stores.append(pltpu.make_async_copy(sol.at[rows], sol_hbm.at[rows], out_sem.at[n]))
        stores.append(pltpu.make_async_copy(res.at[rows], res_hbm.at[rows], out_sem.at[8 + n]))
        stores[-2].start()
        stores[-1].start()
    for x in stores:
        x.wait()


def body(n_rows, n_cols, observed, class_map, class_weights, blur_kernel):
    zk = min(8, n_cols)
    ny = n_cols // zk
    big = pltpu.VMEM((9, 288, 128), F32)
    half = pltpu.VMEM((256, 1024), F32)

    def v(*shape):
        return pltpu.VMEM(shape, F32)

    scratch = [
        big, pltpu.VMEM((8, 256, 128), jnp.int32), big, big, big, big, big,
        v(9, 48, 128), pltpu.VMEM((1024, 384), BF16), pltpu.VMEM((3072, 128), BF16),
        pltpu.VMEM((128, 1152), BF16),
        v(128, 128), v(3, 128, 128), v(1, 128, 128), v(3, 128, 128),
        v(6, 2, 48, 128), v(2, 64, 128),
        v(8, 3, 16, 128), v(2, 8, 8, 128), v(2, 4, 8, 128), v(8, 8, 128), v(8, 8, 128),
        v(8, 4, 8, 128), v(3, 8, 64, 128), v(4, 2, 48, 128),
        v(32, 128), v(8, 128), v(8, 128), v(8, 1, 8, 128), v(8, 48, 128), v(8, 48, 128),
        v(8, 128), v(8, 128), v(zk, 8, 128), v(n_rows * ny, 8, 128),
        pltpu.SemaphoreType.DMA((16,)),
        pltpu.SemaphoreType.DMA((3, 10)), pltpu.SemaphoreType.DMA((3, 10)),
        pltpu.SemaphoreType.DMA((2,)), pltpu.SemaphoreType.DMA((2,)),
    ]
    hbm = pl.BlockSpec(memory_space=pltpu.HBM)
    vmem = pl.BlockSpec(memory_space=pltpu.VMEM)
    scalars = pl.BlockSpec(memory_space=pltpu.SMEM)
    field = pltpu.VMEM((9, 288, 128), F32)
    fields = pl.pallas_call(
        functools.partial(kernel, n_rows, n_cols, zk),
        out_shape=(field,) * 5 + (pltpu.VMEM((2, 8, 128), F32),),
        in_specs=[scalars, scalars, hbm, hbm],
        out_specs=(vmem,) * 6,
        scratch_shapes=scratch,
        compiler_params=pltpu.CompilerParams(
            collective_id=0, has_side_effects=True, vmem_limit_bytes=KERNEL_VMEM),
    )(class_weights, blur_kernel, observed, class_map)
    shape = jax.ShapeDtypeStruct(observed.shape, F32)
    return pl.pallas_call(
        finish_kernel,
        out_shape=(shape, shape),
        in_specs=[vmem] * 6,
        out_specs=(hbm, hbm),
        scratch_shapes=[half, half, pltpu.SemaphoreType.DMA((16,))],
        compiler_params=pltpu.CompilerParams(vmem_limit_bytes=FINISH_VMEM),
    )(*fields)


def solution(mesh):
    n_rows, n_cols = mesh.shape["rows"], mesh.shape["cols"]
    return jax.shard_map(
        functools.partial(body, n_rows, n_cols),
        mesh=mesh,
        in_specs=(P("rows", "cols"), P("rows", "cols"), P(), P()),
        out_specs=(P("rows", "cols"), P("rows", "cols")),
        check_vma=False,
    )
```

```python
import functools

import jax
import jax.numpy as jnp
from jax import lax
from jax.experimental import pallas as pl
from jax.experimental.pallas import tpu as pltpu
from jax.sharding import PartitionSpec as P

MESH = pl.DeviceIdType.MESH
OMEGA = 0.8
SWEEPS = 8
NB = ((-1, 0), (1, 0), (0, -1), (0, 1), (-1, -1), (-1, 1), (1, -1), (1, 1))
F32 = jnp.float32
BF16 = jnp.bfloat16
KERNEL_VMEM = 55 * 2**20
FINISH_VMEM = 16 * 2**20


def exact_dot(x, ones):
    hi = x.astype(BF16)
    lo = (x - hi.astype(F32)).astype(BF16)
    both = jnp.dot(jnp.concatenate([hi, lo], axis=0), ones, preferred_element_type=F32)
    return both[: x.shape[0]] + both[x.shape[0] :]


def kernel(
    n_rows, n_cols, zk,
    cw, bk, obs_hbm, cls_hbm, r0, d0, q0, w, lw, coef,
    obs, cls, cond, rfd, ce, cs, img,
    zup, cmat, bmat, umat, tbuf, tt0, tt2, hbuf, ctab, zs,
    rx0, sn1, sd1, rn1, rs1, rx1, pbuf, craw, sn2, rn2, rs2, rx2, zeast, zwest,
    red0, red1, redx, redy,
    in_sem, send_sem, recv_sem, rsend, rrecv,
):
    r = lax.axis_index("rows")
    c = lax.axis_index("cols")
    ny = n_cols // zk
    y, k8 = c // zk, lax.rem(c, zk)

    def ok(dr, dc):
        return (r + dr >= 0) & (r + dr < n_rows) & (c + dc >= 0) & (c + dc < n_cols)

    def dev(dr, dc):
        return (c + dc, r + dr)

    loads = []
    for t in range(8):
        lanes = pl.ds(t * 128, 128)
        loads.append(pltpu.make_async_copy(cls_hbm.at[:, lanes], cls.at[t], in_sem.at[t]))
        loads.append(pltpu.make_async_copy(
            obs_hbm.at[:, lanes], obs.at[t, pl.ds(16, 256), :], in_sem.at[8 + t]))
    for x in loads:
        x.start()

    for buf in (rx0, rn1, rs1, rx1, rn2, rs2, rx2, hbuf, zs):
        buf[...] = jnp.zeros(buf.shape, F32)
    for buf in (obs, cond):
        for t in range(8):
            buf[t, 8:16, :] = jnp.zeros((8, 128), F32)
            buf[t, 272:280, :] = jnp.zeros((8, 128), F32)

    bar = pltpu.get_barrier_semaphore()
    peers = zk + n_rows * ny - 2
    for dr, dc in NB:
        if dc == 0:
            continue
        fresh = ok(dr, dc)
        if dr == 0:
            fresh = fresh & (k8 == (zk - 1 if dc > 0 else 0))
        peers = peers + fresh.astype(jnp.int32)

        @pl.when(fresh)
        def _():
            pl.semaphore_signal(bar, inc=1, device_id=dev(dr, dc), device_id_type=MESH)
    nz = zk // 2
    z_me, core = k8 // 2, lax.rem(k8, 2)
    xy_me = r * ny + y

    def ring(o, n):
        return min(o, n - o)

    zk_far = sorted(((a, b) for a in range(nz) for b in range(2) if a or b),
                    key=lambda o: -(2 * ring(o[0], nz) + o[1]))
    xy_far = sorted(((a, b) for a in range(n_rows) for b in range(ny) if a or b),
                    key=lambda o: -(ring(o[0], n_rows) + ring(o[1], ny)))
    zk_group = [(y * zk + lax.rem(z_me + a, nz) * 2 + lax.rem(core + b, 2), r) for a, b in zk_far]
    xy_group = [(lax.rem(y + b, ny) * zk + k8, lax.rem(r + a, n_rows)) for a, b in xy_far]
    for peer in zk_group + xy_group:
        pl.semaphore_signal(bar, inc=1, device_id=peer, device_id_type=MESH)

    lane = lax.broadcasted_iota(jnp.int32, (8, 128), 1)
    sub = lax.broadcasted_iota(jnp.int32, (8, 128), 0)
    first_lane = lane == 0
    last_lane = lane == 127

    kk = [[bk[a, b] for b in range(3)] for a in range(3)]
    ksum = kk[0][0]
    ksq = kk[0][0] * kk[0][0]
    for a in range(3):
        for b in range(3):
            if a + b:
                ksum = ksum + kk[a][b]
                ksq = ksq + kk[a][b] * kk[a][b]

    def sh_east(v):
        rolled = [pltpu.roll(x, 127, 1) for x in v]
        n = len(v)
        return [jnp.where(last_lane, rolled[(t + 1) % n], rolled[t]) for t in range(n)]

    def sh_west(v):
        rolled = [pltpu.roll(x, 1, 1) for x in v]
        n = len(v)
        return [jnp.where(first_lane, rolled[(t - 1) % n], rolled[t]) for t in range(n)]

    def rows_of(ref, base, n=9):
        return [ref[t, pl.ds(base, 8), :] for t in range(n)]

    ii = lax.broadcasted_iota(jnp.int32, (1024, 128), 0)
    jj = lax.broadcasted_iota(jnp.int32, (1024, 128), 1)
    cell, place = jnp.right_shift(ii, 3), jnp.bitwise_and(ii, 7)
    for n, hit in enumerate((cell == jj, (cell == jj) & (place == 7), (cell == jj) & (place == 0))):
        cmat[:, 128 * n:128 * n + 128] = jnp.where(hit, 1.0, 0.0).astype(BF16)
    for b in range(3):
        hit = jnp.right_shift(ii + (7 + b), 3) == jj + 1
        bmat[1024 * b:1024 * b + 1024, :] = jnp.where(hit, 1.0, 0.0).astype(BF16)

    for x in loads:
        x.wait()

    w0, w1, w2, w3 = cw[0], cw[1], cw[2], cw[3]

    def cond_body(i, _):
        src = pl.multiple_of(i * 8, 8)
        dst = pl.multiple_of(i * 8 + 16, 8)
        for t in range(8):
            m = cls[t, pl.ds(src, 8), :]
            cond[t, pl.ds(dst, 8), :] = jnp.where(
                m == 0, w0, jnp.where(m == 1, w1, jnp.where(m == 2, w2, w3)))
        return 0

    lax.fori_loop(0, 32, cond_body, 0)

    def rim_tile(start, n):
        lanes = lax.broadcasted_iota(jnp.int32, (n, 128), 1)
        rows = pl.ds(start, n)
        left = jnp.where(lanes < 8, obs[0, rows, :], pltpu.roll(cond[0, rows, :], 8, 1))
        right = jnp.where(lanes >= 120, obs[7, rows, :], pltpu.roll(cond[7, rows, :], 120, 1))
        return jnp.where(lanes < 64, left, right)

    tt0[0] = rim_tile(16, 128).T
    tt0[1] = rim_tile(144, 128).T
    tbuf[...] = jnp.zeros(tbuf.shape, F32)
    tbuf[64:72, :] = rim_tile(264, 8)
    tbuf[72:80, :] = rim_tile(16, 8)
    tt0[2] = tbuf[...].T

    def side_copies(tt, rx, groups_diag, width):
        low, high = pl.ds(0, width), pl.ds(128 - width, width)
        out = []
        for n, (dr, dc) in enumerate(NB):
            if dc == 0:
                continue
            groups = pl.ds(0, tt.shape[0]) if dr == 0 else groups_diag
            rows = low if dc < 0 else high
            out.append((n, n, tt.at[groups, rows, :], rx.at[n, groups]))
        return out

    def start_all(phase, copies):
        for q, n, src, dst in copies:
            dr, dc = NB[n]
            @pl.when(ok(dr, dc))
            def _():
                pltpu.make_async_remote_copy(
                    src, dst, send_sem.at[phase, q], recv_sem.at[phase, q],
                    device_id=dev(dr, dc), device_id_type=MESH).start()

    def wait_recv_all(phase, copies):
        for q, n, src, dst in copies:
            dr, dc = NB[n]
            @pl.when(ok(-dr, -dc))
            def _():
                pltpu.make_async_remote_copy(
                    src, dst, send_sem.at[phase, q], recv_sem.at[phase, q],
                    device_id=dev(-dr, -dc), device_id_type=MESH).wait_recv()

    def wait_send_all(phase, copies):
        for q, n, src, dst in copies:
            dr, dc = NB[n]
            @pl.when(ok(dr, dc))
            def _():
                pltpu.make_async_remote_copy(
                    src, dst, send_sem.at[phase, q], recv_sem.at[phase, q],
                    device_id=dev(dr, dc), device_id_type=MESH).wait_send()

    third = pl.ds(2, 1)
    own, top, low = pl.ds(0, 8), pl.ds(16, 8), pl.ds(264, 8)
    above, below = pl.ds(8, 8), pl.ds(272, 8)
    copies0 = side_copies(tt0, rx0, third, 16)
    for q, field in ((0, obs), (8, cond)):
        copies0.append((q, 0, field.at[own, top, :], field.at[own, below, :]))
        copies0.append((q + 1, 1, field.at[own, low, :], field.at[own, above, :]))
    pl.semaphore_wait(bar, peers)
    start_all(0, copies0)

    def row_sums(ref, t):
        total = ref[t, pl.ds(16, 32, stride=8), :]
        for s in range(1, 8):
            total = total + ref[t, pl.ds(16 + s, 32, stride=8), :]
        return total

    lane32 = lax.broadcasted_iota(jnp.int32, (32, 128), 1)
    row32 = lax.broadcasted_iota(jnp.int32, (32, 128), 0)
    lane48 = lax.broadcasted_iota(jnp.int32, (48, 128), 1)
    row48 = lax.broadcasted_iota(jnp.int32, (48, 128), 0)
    last48, first48 = lane48 == 127, lane48 == 0

    every = pl.ds(16, 32, stride=8)
    last_row = pl.ds(23, 32, stride=8)
    sums = exact_dot(jnp.concatenate([
        jnp.concatenate([row_sums(cond, t) for t in range(8)], axis=1),
        jnp.concatenate([cond[t, every, :] for t in range(8)], axis=1),
        jnp.concatenate([cond[t, last_row, :] for t in range(8)], axis=1)], axis=0), cmat[...])
    ec, wc = sums[0:32, 128:256], sums[0:32, 256:384]
    nc, sc = sums[32:64, 0:128], sums[64:96, 0:128]
    part = (
        0.5 * (ec + jnp.where(lane32 == 127, 0.0, pltpu.roll(wc, 127, 1))),
        0.5 * (wc + jnp.where(lane32 == 0, 0.0, pltpu.roll(ec, 1, 1))),
        0.5 * (nc + jnp.where(row32 == 0, 0.0, pltpu.roll(sc, 1, 0))),
        0.5 * (sc + jnp.where(row32 == 31, 0.0, pltpu.roll(nc, 31, 0))),
    )

    pbuf[:, :, 0:16, :] = jnp.zeros((3, 8, 16, 128), F32)
    pbuf[:, :, 48:64, :] = jnp.zeros((3, 8, 16, 128), F32)
    for t in range(8):
        pbuf[0, t, 16:48, :] = row_sums(obs, t)
        pbuf[1, t, 16:48, :] = obs[t, every, :]
        pbuf[2, t, 16:48, :] = obs[t, last_row, :]
    vb = [[], [], []]
    for t in range(8):
        mid = pbuf[0, t, 8:56, :]
        down = mid - pbuf[1, t, 8:56, :] + pbuf[1, t, 9:57, :]
        up = mid - pbuf[2, t, 8:56, :] + pbuf[2, t, 7:55, :]
        for b in range(3):
            vb[b].append(kk[0][b] * down + kk[1][b] * mid + kk[2][b] * up)
    own_source = exact_dot(jnp.concatenate(vb[0] + vb[1] + vb[2], axis=1), bmat[...])
    own_ring = jnp.where(lane48 == 7, pltpu.roll(vb[0][0], 7, 1),
                         jnp.where(lane48 == 8, pltpu.roll(vb[2][7], 9, 1), 0.0))

    for f in range(4):
        sn1[0, f] = part[f][0:8]
        sn1[1, f] = part[f][24:32]
        craw[f, 0, 8:40, :] = part[f]
    for h in range(2):
        sn1[0, 4 + h] = own_source[8 * h:8 * h + 8]
        sn1[0, 6 + h] = own_ring[8 * h:8 * h + 8]
        sn1[1, 4 + h] = own_source[32 + 8 * h:40 + 8 * h]
        sn1[1, 6 + h] = own_ring[32 + 8 * h:40 + 8 * h]
    for g in range(2):
        for h in range(2):
            field = part[2 * g + h]
            tbuf[64 * h:64 * h + 8, :] = field[24:32]
            tbuf[64 * h + 8:64 * h + 40, :] = field
            tbuf[64 * h + 40:64 * h + 48, :] = field[0:8]
        tile = tbuf[...].T
        sd1[0, g] = tile[0:8]
        sd1[1, g] = tile[120:128]
    tbuf[0:48, :] = own_source
    tbuf[64:112, :] = own_ring
    tile = tbuf[...].T
    in48 = lane < 48
    sd1[0, 2] = jnp.where(in48, pltpu.roll(tile[0:8], 64, 1), 0.0)
    sd1[0, 3] = jnp.where(in48, tile[0:8], 0.0)
    sd1[1, 2] = jnp.where(in48, tile[120:128], 0.0)
    sd1[1, 3] = jnp.where(in48, pltpu.roll(tile[8:16], 64, 1), 0.0)

    copies1 = [(0, 0, sn1.at[0], rs1), (1, 1, sn1.at[1], rn1)]
    for n, (dr, dc) in enumerate(NB):
        if dc:
            copies1.append((n, n, sd1.at[0 if dc < 0 else 1], rx1.at[n]))
    start_all(1, copies1)

    ui = lax.broadcasted_iota(jnp.int32, (128, 1024), 0)
    uj = lax.broadcasted_iota(jnp.int32, (128, 1024), 1)
    umat[:, 0:1024] = jnp.where(jnp.right_shift(uj, 3) == ui, 1.0, 0.0).astype(BF16)
    vi = lax.broadcasted_iota(jnp.int32, (128, 128), 0)
    vj = lax.broadcasted_iota(jnp.int32, (128, 128), 1)
    umat[:, 1024:1152] = jnp.where(
        ((vj < 64) & (vi == 0)) | ((vj >= 64) & (vi == 127)), 1.0, 0.0).astype(BF16)

    def blur_adjoint(up, mid, down, b):
        return kk[0][b] * down + kk[1][b] * mid + kk[2][b] * up

    def own_body(i, _):
        base = pl.multiple_of(i * 8 + 24, 8)
        here = pl.ds(base, 8)
        up, mid, down = rows_of(obs, base - 1, 8), rows_of(obs, base, 8), rows_of(obs, base + 1, 8)
        v = [[blur_adjoint(up[t], mid[t], down[t], b) for t in range(8)] for b in range(3)]
        e0 = [pltpu.roll(x, 127, 1) for x in v[0]]
        w2_ = [pltpu.roll(x, 1, 1) for x in v[2]]
        cm, csouth = rows_of(cond, base, 8), rows_of(cond, base + 1, 8)
        ceast = [pltpu.roll(x, 127, 1) for x in cm]
        for t in range(8):
            e = jnp.where(last_lane, e0[t + 1] if t < 7 else 0.0, e0[t])
            w_ = jnp.where(first_lane, w2_[t - 1] if t else 0.0, w2_[t])
            r0[t, here, :] = v[1][t] + e + w_
            ce[t, here, :] = 0.5 * (cm[t] + jnp.where(last_lane, ceast[t + 1] if t < 7 else 0.0, ceast[t]))
            cs[t, here, :] = 0.5 * (cm[t] + csouth[t])
        return 0

    lax.fori_loop(0, 30, own_body, 0, unroll=3)
    wait_recv_all(0, copies0)

    def side(rx, group, dc, in_north, in_center):
        north = rx[NB.index((1, dc)), group]
        center = rx[NB.index((0, dc)), group]
        south = rx[NB.index((-1, dc)), group]
        return jnp.where(in_north, north, jnp.where(in_center, center, south))

    lane64 = lax.rem(lane, 64)

    lane16 = lax.broadcasted_iota(jnp.int32, (16, 128), 1)
    for dc, rows in ((-1, slice(0, 16)), (1, slice(112, 128))):
        here = NB.index((0, dc))
        hbuf[0, rows, :] = rx0[here, 0]
        hbuf[1, rows, :] = rx0[here, 1]
        hbuf[2, rows, :] = side(rx0, 2, dc, lane16 < 72, lane16 < 0)

    def cond_of(x):
        lanes = lax.broadcasted_iota(jnp.int32, x.shape, 1)
        return jnp.where(lanes < 64, pltpu.roll(x, 120, 1), pltpu.roll(x, 8, 1))

    for g in range(2):
        tile = hbuf[g].T
        rows = slice(16 + 128 * g, 144 + 128 * g)
        obs[8, rows, :] = tile
        cond[8, rows, :] = cond_of(tile)
    tile = hbuf[2].T
    for rows, lo in ((slice(8, 16), 64), (slice(272, 280), 72)):
        obs[8, rows, :] = tile[lo:lo + 8]
        cond[8, rows, :] = cond_of(tile[lo:lo + 8])
    def side_body(i, _):
        base = pl.multiple_of(i * 8 + 24, 8)
        here = pl.ds(base, 8)
        def v(t, b):
            return blur_adjoint(obs[t, pl.ds(base - 1, 8), :], obs[t, here, :],
                                obs[t, pl.ds(base + 1, 8), :], b)
        e8, w8 = pltpu.roll(v(8, 0), 127, 1), pltpu.roll(v(8, 2), 1, 1)
        e0, w7 = pltpu.roll(v(0, 0), 127, 1), pltpu.roll(v(7, 2), 1, 1)
        r0[8, here, :] = v(8, 1) + jnp.where(last_lane, e0, e8) + jnp.where(first_lane, w7, w8)
        r0[7, here, :] = r0[7, here, :] + jnp.where(last_lane, e8, 0.0)
        r0[0, here, :] = r0[0, here, :] + jnp.where(first_lane, w8, 0.0)
        c8 = cond[8, here, :]
        ce8, ce0 = pltpu.roll(c8, 127, 1), pltpu.roll(cond[0, here, :], 127, 1)
        ce[8, here, :] = 0.5 * (c8 + jnp.where(last_lane, ce0, ce8))
        ce[7, here, :] = ce[7, here, :] + 0.5 * jnp.where(last_lane, ce8, 0.0)
        cs[8, here, :] = 0.5 * (c8 + cond[8, pl.ds(base + 1, 8), :])
        return 0

    lax.fori_loop(0, 30, side_body, 0, unroll=6)

    def outer_body(i, _):
        base = pl.multiple_of(jnp.where(i < 2, i * 8 + 8, i * 8 + 248), 8)
        here = pl.ds(base, 8)
        up, mid, down = rows_of(obs, base - 1), rows_of(obs, base), rows_of(obs, base + 1)
        v = [[blur_adjoint(up[t], mid[t], down[t], b) for t in range(9)] for b in range(3)]
        e0, w2_ = sh_east(v[0]), sh_west(v[2])
        cm, csouth = rows_of(cond, base), rows_of(cond, base + 1)
        ceast = sh_east(cm)
        for t in range(9):
            r0[t, here, :] = v[1][t] + e0[t] + w2_[t]
            ce[t, here, :] = 0.5 * (cm[t] + ceast[t])
            cs[t, here, :] = 0.5 * (cm[t] + csouth[t])
        return 0

    lax.fori_loop(0, 4, outer_body, 0, unroll=4)

    def clear_outside(ref):
        @pl.when(r == 0)
        def _():
            for t in range(9):
                ref[t, 8:16, :] = jnp.zeros((8, 128), F32)

        @pl.when(r == n_rows - 1)
        def _():
            for t in range(9):
                ref[t, 272:280, :] = jnp.zeros((8, 128), F32)

        lanes = lax.broadcasted_iota(jnp.int32, (272, 128), 1)

        @pl.when(c == 0)
        def _():
            ref[8, 8:280, :] = jnp.where(lanes < 64, ref[8, 8:280, :], 0.0)

        @pl.when(c == n_cols - 1)
        def _():
            ref[8, 8:280, :] = jnp.where(lanes >= 64, ref[8, 8:280, :], 0.0)

    def diag_body(i, _):
        base = pl.multiple_of(i * 8 + 8, 8)
        here = pl.ds(base, 8)
        east = rows_of(ce, base)
        west = sh_west(east)
        for t in range(9):
            total = (east[t] + west[t]) + (cs[t, here, :] + cs[t, pl.ds(base - 1, 8), :])
            rfd[t, here, :] = 1.0 / (ksq + total)
        return 0

    lax.fori_loop(0, 34, diag_body, 0, unroll=4)
    clear_outside(rfd)
    wait_recv_all(1, copies1)

    for f in range(4):
        craw[f, 0, 0:8, :] = rn1[f]
        craw[f, 0, 40:48, :] = rs1[f]
    hbuf[:, 8:16, :] = jnp.zeros((3, 8, 128), F32)
    hbuf[:, 112:120, :] = jnp.zeros((3, 8, 128), F32)
    for g in range(2):
        for dc, rows in ((-1, slice(0, 8)), (1, slice(120, 128))):
            hbuf[g, rows, :] = side(rx1, g, dc, lane64 < 8, lane64 < 40)
        tile = hbuf[g].T
        for h in range(2):
            craw[2 * g + h, 1] = tile[64 * h:64 * h + 48]
    for dc, blocks in ((-1, ((2, slice(8, 16)), (3, slice(0, 8)))),
                       (1, ((2, slice(120, 128)), (3, slice(112, 120))))):
        for q, rows in blocks:
            hbuf[2, rows, :] = rx1[NB.index((0, dc)), q] + (
                pltpu.roll(rx1[NB.index((1, dc)), q], 96, 1)
                + pltpu.roll(rx1[NB.index((-1, dc)), q], 32, 1))
    tile = hbuf[2].T[0:48]
    blank = jnp.zeros((16, 128), F32)

    def with_rows(own_part, q):
        return own_part + jnp.concatenate(
            [rn1[q], rn1[q + 1], blank, rs1[q], rs1[q + 1]], axis=0)

    ring_all = pltpu.roll(with_rows(own_ring, 6), 120, 1)
    source = [
        with_rows(own_source, 4) + jnp.where(
            last48, pltpu.roll(tile, 112, 1), jnp.where(first48, pltpu.roll(tile, 16, 1), 0.0)),
        tile + jnp.where(last48 | first48, ring_all, 0.0),
    ]
    for t in range(2):
        for a, b in ((7, 8), (39, 40)):
            both = craw[3, t, a:a + 1, :] + craw[2, t, b:b + 1, :]
            craw[3, t, a:a + 1, :] = both
            craw[2, t, b:b + 1, :] = both
    pe, pw = [craw[0, t] for t in range(2)], [craw[1, t] for t in range(2)]
    rows_ok = ((row48 >= 8) | (r > 0)) & ((row48 < 40) | (r < n_rows - 1))
    lanes_ok = ((lane48 >= 64) | (c < n_cols - 1)) & ((lane48 < 64) | (c > 0))
    for t in range(2):
        c_east = pe[t] + jnp.where(last48, pltpu.roll(pw[1 - t], 127, 1), 0.0)
        c_west = pw[t] + jnp.where(first48, pltpu.roll(pe[1 - t], 1, 1), 0.0)
        c_north, c_south = craw[2, t], craw[3, t]
        c_diag = 64.0 * (ksum * ksum) + c_east + c_west + c_north + c_south
        scale = jnp.where(rows_ok & lanes_ok if t else rows_ok, OMEGA / c_diag, 0.0)
        for f, x in enumerate((source[t], c_east, c_west, c_north, c_south)):
            ctab[f, t] = x * scale
        if t == 0:
            ctab[5, 0] = scale
            ctab[5, 1] = c_diag * (1.0 / OMEGA)

    def sweep(_, carry):
        z = [zs[t, 8:56, :] for t in range(2)]
        east = [pltpu.roll(x, 127, 1) for x in z]
        west = [pltpu.roll(x, 1, 1) for x in z]
        new = []
        for t in range(2):
            ze = jnp.where(last48, east[1 - t], east[t])
            zw = jnp.where(first48, west[1 - t], west[t])
            zn, zso = zs[t, 7:55, :], zs[t, 9:57, :]
            new.append((ctab[0, t] + (1.0 - OMEGA) * z[t])
                       + (ctab[1, t] * ze + ctab[2, t] * zw)
                       + (ctab[3, t] * zn + ctab[4, t] * zso))
        for t in range(2):
            zs[t, 8:56, :] = new[t]
        return carry

    def jacobi():
        for t in range(2):
            zs[t, 8:56, :] = ctab[0, t]
        lax.fori_loop(0, SWEEPS - 1, sweep, 0, unroll=SWEEPS - 1)

    def spread():
        up = exact_dot(zs[0, 8:56, :], umat[:, 0:1024])
        for t in range(8):
            zup[t] = up[:, 128 * t:128 * t + 128]
        zup[8] = exact_dot(zs[1, 8:56, :], umat[:, 1024:1152])

    jacobi()
    spread()

    def precond(field, out):
        def body(i, _):
            base = pl.multiple_of(i * 8 + 8, 8)
            here = pl.ds(base, 8)
            for t in range(9):
                out[t, here, :] = field[t, here, :] * rfd[t, here, :] + zup[t, pl.ds(i + 7, 1), :]
            return 0

        lax.fori_loop(0, 34, body, 0, unroll=4)

    precond(r0, d0)

    def blur_rows(ref, base):
        up, mid, down = rows_of(ref, base - 1), rows_of(ref, base), rows_of(ref, base + 1)
        u = [[kk[0][b] * up[t] + kk[1][b] * mid[t] + kk[2][b] * down[t] for t in range(9)]
             for b in range(3)]
        w_, e_ = sh_west(u[0]), sh_east(u[2])
        return [u[1][t] + w_[t] + e_[t] for t in range(9)], up, mid, down

    def blur0(i, _):
        base = pl.multiple_of(i * 8 + 8, 8)
        out, _, _, _ = blur_rows(d0, base)
        for t in range(9):
            img[t, pl.ds(base, 8), :] = out[t]
        return 0

    lax.fori_loop(0, 34, blur0, 0, unroll=4)
    clear_outside(img)

    def apply_rows(field, base, n):
        up, mid, down = rows_of(img, base - 1), rows_of(img, base), rows_of(img, base + 1)
        v = [[blur_adjoint(up[t], mid[t], down[t], b) for t in range(9)] for b in range(3)]
        up, mid, down = rows_of(field, base - 1), rows_of(field, base), rows_of(field, base + 1)
        east = sh_east(mid)
        flux = [ce[t, pl.ds(base, 8), :] * (mid[t] - east[t]) for t in range(9)]
        e0 = sh_east(v[0])
        w2_ = sh_west([v[2][t] - flux[t] for t in range(9)])
        out = []
        for t in range(n):
            lap = (cs[t, pl.ds(base, 8), :] * (mid[t] - down[t])
                   - cs[t, pl.ds(base - 1, 8), :] * (up[t] - mid[t]))
            out.append(((v[1][t] + e0[t]) + (w2_[t] + flux[t])) + lap)
        return out, mid

    zero = jnp.zeros((8, 128), F32)

    def apply0(i, carry):
        gam, dad = carry
        base = pl.multiple_of(i * 8 + 16, 8)
        out, mid = apply_rows(d0, base, 9)
        q0[8, pl.ds(base, 8), :] = out[8]
        w[8, pl.ds(base, 8), :] = out[8] * rfd[8, pl.ds(base, 8), :]
        for t in range(8):
            q0[t, pl.ds(base, 8), :] = out[t]
            w[t, pl.ds(base, 8), :] = out[t] * rfd[t, pl.ds(base, 8), :]
            gam = gam + r0[t, pl.ds(base, 8), :] * mid[t]
            dad = dad + mid[t] * out[t]
        return gam, dad

    gam, dad = lax.fori_loop(0, 32, apply0, (zero, zero), unroll=4)

    src = jnp.concatenate([row_sums(q0, t) for t in range(8)], axis=1)
    cells = exact_dot(src, cmat[:, 0:128])
    b2 = cells * ctab[5, 0, 8:40, :]
    ctab[0, 0, 8:40, :] = b2

    sn2[...] = b2
    tbuf[0:8, :] = b2[24:32]
    tbuf[8:40, :] = b2
    tbuf[40:48, :] = b2[0:8]
    tt2[0] = tbuf[...].T
    copies2 = [(0, 0, sn2.at[pl.ds(0, 8), :], rs2), (1, 1, sn2.at[pl.ds(24, 8), :], rn2)]
    copies2 += side_copies(tt2, rx2, pl.ds(0, 1), 8)
    start_all(2, copies2)

    def apply0_rim(i, _):
        base = pl.multiple_of(i * 264 + 8, 8)
        out, _ = apply_rows(d0, base, 9)
        for t in range(9):
            q0[t, pl.ds(base, 8), :] = out[t]
            w[t, pl.ds(base, 8), :] = out[t] * rfd[t, pl.ds(base, 8), :]
        return 0

    lax.fori_loop(0, 2, apply0_rim, 0, unroll=2)

    def blur1(i, _):
        base = pl.multiple_of(i * 8 + 8, 8)
        out, _, _, _ = blur_rows(w, base)
        for t in range(9):
            img[t, pl.ds(base, 8), :] = out[t]
        return 0

    lax.fori_loop(0, 34, blur1, 0, unroll=4)
    clear_outside(img)

    def apply1(i, carry):
        qw, waw = carry
        base = pl.multiple_of(i * 8 + 16, 8)
        out, mid = apply_rows(w, base, 8)
        for t in range(8):
            lw[t, pl.ds(base, 8), :] = out[t]
            qw = qw + q0[t, pl.ds(base, 8), :] * mid[t]
            waw = waw + mid[t] * out[t]
        return qw, waw

    qw, waw = lax.fori_loop(0, 32, apply1, (zero, zero), unroll=4)
    at_cells = exact_dot(
        jnp.concatenate([row_sums(lw, t) for t in range(8)], axis=1), cmat[:, 0:128])

    wait_recv_all(2, copies2)
    for dc, rows in ((-1, slice(0, 8)), (1, slice(120, 128))):
        hbuf[0, rows, :] = side(rx2, 0, dc, lane < 8, lane < 40)
    ctab[0, 1, :, :] = hbuf[0].T[0:48]
    ctab[0, 0, 0:8, :] = rn2[...]
    ctab[0, 0, 40:48, :] = rs2[...]
    jacobi()
    spread()

    z = zs[0, 16:48, :]
    ze = jnp.where(lane32 == 127, pltpu.roll(zs[1, 16:48, :], 127, 1), pltpu.roll(z, 127, 1))
    zw = jnp.where(lane32 == 0, pltpu.roll(zs[1, 16:48, :], 1, 1), pltpu.roll(z, 1, 1))
    g = [ctab[f, 0, 8:40, :] for f in range(5)]
    lap = (g[1] * (z - ze) + g[2] * (z - zw)) + (
        g[3] * (z - zs[0, 15:47, :]) + g[4] * (z - zs[0, 17:49, :]))

    def fold(x):
        return (x[0:8] + x[8:16]) + (x[16:24] + x[24:32])

    qw = qw + fold(cells * z)
    waw = waw + fold(z * (2.0 * at_cells + ctab[5, 1, 8:40, :] * lap))

    for n in range(6):
        rows = slice(8 * n, 8 * n + 8)
        mid = [zup[t, rows, :] for t in range(9)]
        east, west = sh_east(mid), sh_west(mid)
        for t in range(8):
            zeast[t, rows, :] = east[t]
            zwest[t, rows, :] = west[t]
    ksums = [(kk[0][b] + kk[1][b]) + kk[2][b] for b in range(3)]

    def lanes_conv(weights, parts):
        return weights[0] * parts[0] + weights[1] * parts[1] + weights[2] * parts[2]

    for n in range(4):
        at, up, down = (slice(8 * n + o, 8 * n + o + 8) for o in (8, 7, 9))
        for t in range(8):
            here = [x[t, at, :] for x in (zwest, zup, zeast)]
            north = [x[t, up, :] for x in (zwest, zup, zeast)]
            south = [x[t, down, :] for x in (zwest, zup, zeast)]
            mid = lanes_conv(ksums, here)
            first = mid + lanes_conv(kk[0], [p - q for p, q in zip(north, here)])
            last = mid + lanes_conv(kk[2], [p - q for p, q in zip(south, here)])
            waw = waw + (6.0 * (mid * mid) + (first * first + last * last))

    for n, part in enumerate((gam, dad, qw, waw)):
        red0[n:n + 1, :] = jnp.sum(part, axis=0, keepdims=True)
    red0[4:8, :] = jnp.zeros((4, 128), F32)
    redx[k8] = red0[...]
    for peer in zk_group:
        pltpu.make_async_remote_copy(
            red0, redx.at[k8], rsend.at[0], rrecv.at[0],
            device_id=peer, device_id_type=MESH).start()

    def add_coarse(i, _):
        here = pl.ds(pl.multiple_of(i * 8 + 8, 8), 8)
        for t in range(9):
            w[t, here, :] = w[t, here, :] + zup[t, pl.ds(i + 7, 1), :]
        return 0

    lax.fori_loop(0, 34, add_coarse, 0, unroll=4)
    lax.fori_loop(0, 34, blur1, 0, unroll=4)
    clear_outside(img)

    def apply2(i, _):
        base = pl.multiple_of(i * 8 + 16, 8)
        out, _ = apply_rows(w, base, 8)
        for t in range(8):
            lw[t, pl.ds(base, 8), :] = out[t]
        return 0

    def all_bytes(buf, n, sem):
        return pltpu.make_async_copy(buf.at[pl.ds(0, n)], buf.at[pl.ds(0, n)], sem)

    all_bytes(redx, zk - 1, rrecv.at[0]).wait()
    total = redx[0]
    for i in range(1, zk):
        total = total + redx[i]
    red1[...] = total
    redy[xy_me] = total
    for peer in xy_group:
        pltpu.make_async_remote_copy(
            red1, redy.at[xy_me], rsend.at[1], rrecv.at[1],
            device_id=peer, device_id_type=MESH).start()
    lax.fori_loop(0, 32, apply2, 0, unroll=4)
    wait_send_all(0, copies0)
    wait_send_all(1, copies1)
    wait_send_all(2, copies2)
    all_bytes(redx, zk - 1, rsend.at[0]).wait()
    all_bytes(redy, n_rows * ny - 1, rrecv.at[1]).wait()
    total = redy[0]
    for i in range(1, n_rows * ny):
        total = total + redy[i]
    value = jnp.broadcast_to(jnp.sum(total, axis=1, keepdims=True), (8, 128))
    g0 = jnp.broadcast_to(value[0:1], (8, 128))
    dq = jnp.broadcast_to(value[1:2], (8, 128))
    qws = jnp.broadcast_to(value[2:3], (8, 128))
    ws = jnp.broadcast_to(value[3:4], (8, 128))
    alpha = g0 / dq
    g1 = (g0 - alpha * dq) + alpha * (alpha * qws - dq)
    beta1 = 1.0 + g1 / g0
    dad1 = beta1 * (beta1 * dq - alpha * qws) + alpha * (alpha * ws - beta1 * qws)
    step = g1 / dad1
    ca = alpha + step * beta1
    cb = alpha * step

    coef[0] = ca
    coef[1] = cb
    all_bytes(redy, n_rows * ny - 1, rsend.at[1]).wait()


def finish_kernel(r0, d0, q0, w, lw, coef, sol_hbm, res_hbm, sol, res, out_sem):
    ca, cb = coef[0], coef[1]
    stores = []
    for n in range(8):
        def finish(i, _):
            dst_rows = pl.ds(pl.multiple_of(i * 8 + n * 32, 8), 8)
            src_rows = pl.ds(pl.multiple_of(i * 8 + n * 32 + 16, 8), 8)
            for t in range(8):
                lanes = slice(t * 128, t * 128 + 128)
                sol[dst_rows, lanes] = ca * d0[t, src_rows, :] - cb * w[t, src_rows, :]
                res[dst_rows, lanes] = (
                    r0[t, src_rows, :] - ca * q0[t, src_rows, :]) + cb * lw[t, src_rows, :]
            return 0

        lax.fori_loop(0, 4, finish, 0, unroll=2)
        rows = pl.ds(n * 32, 32)
        stores.append(pltpu.make_async_copy(sol.at[rows], sol_hbm.at[rows], out_sem.at[n]))
        stores.append(pltpu.make_async_copy(res.at[rows], res_hbm.at[rows], out_sem.at[8 + n]))
        stores[-2].start()
        stores[-1].start()
    for x in stores:
        x.wait()


def body(n_rows, n_cols, observed, class_map, class_weights, blur_kernel):
    zk = min(8, n_cols)
    ny = n_cols // zk
    big = pltpu.VMEM((9, 288, 128), F32)
    half = pltpu.VMEM((256, 1024), F32)

    def v(*shape):
        return pltpu.VMEM(shape, F32)

    scratch = [
        big, pltpu.VMEM((8, 256, 128), jnp.int32), big, big, big, big, big,
        v(9, 48, 128), pltpu.VMEM((1024, 384), BF16), pltpu.VMEM((3072, 128), BF16),
        pltpu.VMEM((128, 1152), BF16),
        v(128, 128), v(3, 128, 128), v(1, 128, 128), v(3, 128, 128),
        v(6, 2, 48, 128), v(2, 64, 128),
        v(8, 3, 16, 128), v(2, 8, 8, 128), v(2, 4, 8, 128), v(8, 8, 128), v(8, 8, 128),
        v(8, 4, 8, 128), v(3, 8, 64, 128), v(4, 2, 48, 128),
        v(32, 128), v(8, 128), v(8, 128), v(8, 1, 8, 128), v(8, 48, 128), v(8, 48, 128),
        v(8, 128), v(8, 128), v(zk, 8, 128), v(n_rows * ny, 8, 128),
        pltpu.SemaphoreType.DMA((16,)),
        pltpu.SemaphoreType.DMA((3, 10)), pltpu.SemaphoreType.DMA((3, 10)),
        pltpu.SemaphoreType.DMA((2,)), pltpu.SemaphoreType.DMA((2,)),
    ]
    hbm = pl.BlockSpec(memory_space=pltpu.HBM)
    vmem = pl.BlockSpec(memory_space=pltpu.VMEM)
    scalars = pl.BlockSpec(memory_space=pltpu.SMEM)
    field = pltpu.VMEM((9, 288, 128), F32)
    fields = pl.pallas_call(
        functools.partial(kernel, n_rows, n_cols, zk),
        out_shape=(field,) * 5 + (pltpu.VMEM((2, 8, 128), F32),),
        in_specs=[scalars, scalars, hbm, hbm],
        out_specs=(vmem,) * 6,
        scratch_shapes=scratch,
        compiler_params=pltpu.CompilerParams(
            collective_id=0, has_side_effects=True, vmem_limit_bytes=KERNEL_VMEM),
    )(class_weights, blur_kernel, observed, class_map)
    shape = jax.ShapeDtypeStruct(observed.shape, F32)
    return pl.pallas_call(
        finish_kernel,
        out_shape=(shape, shape),
        in_specs=[vmem] * 6,
        out_specs=(hbm, hbm),
        scratch_shapes=[half, half, pltpu.SemaphoreType.DMA((16,))],
        compiler_params=pltpu.CompilerParams(vmem_limit_bytes=FINISH_VMEM),
    )(*fields)


def solution(mesh):
    n_rows, n_cols = mesh.shape["rows"], mesh.shape["cols"]
    return jax.shard_map(
        functools.partial(body, n_rows, n_cols),
        mesh=mesh,
        in_specs=(P("rows", "cols"), P("rows", "cols"), P(), P()),
        out_specs=(P("rows", "cols"), P("rows", "cols")),
        check_vma=False,
    )
```

```python
import functools

import jax
import jax.numpy as jnp
from jax import lax
from jax.experimental import pallas as pl
from jax.experimental.pallas import tpu as pltpu
from jax.sharding import PartitionSpec as P

MESH = pl.DeviceIdType.MESH
OMEGA = 0.8
SWEEPS = 8
NB = ((-1, 0), (1, 0), (0, -1), (0, 1), (-1, -1), (-1, 1), (1, -1), (1, 1))
F32 = jnp.float32
BF16 = jnp.bfloat16
KERNEL_VMEM = 55 * 2**20
FINISH_VMEM = 16 * 2**20


def exact_dot(x, ones):
    hi = x.astype(BF16)
    lo = (x - hi.astype(F32)).astype(BF16)
    both = jnp.dot(jnp.concatenate([hi, lo], axis=0), ones, preferred_element_type=F32)
    return both[: x.shape[0]] + both[x.shape[0] :]


def kernel(
    n_rows, n_cols, zk,
    cw, bk, obs_hbm, cls_hbm, r0, d0, q0, w, lw, coef,
    obs, cls, cond, rfd, ce, cs, img,
    zup, cmat, bmat, umat, tbuf, tt0, tt2, hbuf, ctab, zs,
    rx0, sn1, sd1, rn1, rs1, rx1, pbuf, craw, sn2, rn2, rs2, rx2, zeast, zwest,
    red0, red1, redx, redy,
    in_sem, send_sem, recv_sem, rsend, rrecv,
):
    r = lax.axis_index("rows")
    c = lax.axis_index("cols")
    ny = n_cols // zk
    y, k8 = c // zk, lax.rem(c, zk)

    def ok(dr, dc):
        return (r + dr >= 0) & (r + dr < n_rows) & (c + dc >= 0) & (c + dc < n_cols)

    def dev(dr, dc):
        return (c + dc, r + dr)

    loads = []
    for t in range(8):
        lanes = pl.ds(t * 128, 128)
        loads.append(pltpu.make_async_copy(cls_hbm.at[:, lanes], cls.at[t], in_sem.at[t]))
        loads.append(pltpu.make_async_copy(
            obs_hbm.at[:, lanes], obs.at[t, pl.ds(16, 256), :], in_sem.at[8 + t]))
    for x in loads:
        x.start()

    for buf in (rx0, rn1, rs1, rx1, rn2, rs2, rx2, hbuf, zs):
        buf[...] = jnp.zeros(buf.shape, F32)
    for buf in (obs, cond):
        for t in range(8):
            buf[t, 8:16, :] = jnp.zeros((8, 128), F32)
            buf[t, 272:280, :] = jnp.zeros((8, 128), F32)

    bar = pltpu.get_barrier_semaphore()
    peers = zk + n_rows * ny - 2
    for dr, dc in NB:
        if dc == 0:
            continue
        fresh = ok(dr, dc)
        if dr == 0:
            fresh = fresh & (k8 == (zk - 1 if dc > 0 else 0))
        peers = peers + fresh.astype(jnp.int32)

        @pl.when(fresh)
        def _():
            pl.semaphore_signal(bar, inc=1, device_id=dev(dr, dc), device_id_type=MESH)
    nz = zk // 2
    z_me, core = k8 // 2, lax.rem(k8, 2)
    xy_me = r * ny + y

    def ring(o, n):
        return min(o, n - o)

    zk_far = sorted(((a, b) for a in range(nz) for b in range(2) if a or b),
                    key=lambda o: -(2 * ring(o[0], nz) + o[1]))
    xy_far = sorted(((a, b) for a in range(n_rows) for b in range(ny) if a or b),
                    key=lambda o: -(ring(o[0], n_rows) + ring(o[1], ny)))
    zk_group = [(y * zk + lax.rem(z_me + a, nz) * 2 + lax.rem(core + b, 2), r) for a, b in zk_far]
    xy_group = [(lax.rem(y + b, ny) * zk + k8, lax.rem(r + a, n_rows)) for a, b in xy_far]
    for peer in zk_group + xy_group:
        pl.semaphore_signal(bar, inc=1, device_id=peer, device_id_type=MESH)

    lane = lax.broadcasted_iota(jnp.int32, (8, 128), 1)
    sub = lax.broadcasted_iota(jnp.int32, (8, 128), 0)
    first_lane = lane == 0
    last_lane = lane == 127

    kk = [[bk[a, b] for b in range(3)] for a in range(3)]
    ksum = kk[0][0]
    ksq = kk[0][0] * kk[0][0]
    for a in range(3):
        for b in range(3):
            if a + b:
                ksum = ksum + kk[a][b]
                ksq = ksq + kk[a][b] * kk[a][b]

    def sh_east(v):
        rolled = [pltpu.roll(x, 127, 1) for x in v]
        n = len(v)
        return [jnp.where(last_lane, rolled[(t + 1) % n], rolled[t]) for t in range(n)]

    def sh_west(v):
        rolled = [pltpu.roll(x, 1, 1) for x in v]
        n = len(v)
        return [jnp.where(first_lane, rolled[(t - 1) % n], rolled[t]) for t in range(n)]

    def rows_of(ref, base, n=9):
        return [ref[t, pl.ds(base, 8), :] for t in range(n)]

    ii = lax.broadcasted_iota(jnp.int32, (1024, 128), 0)
    jj = lax.broadcasted_iota(jnp.int32, (1024, 128), 1)
    cell, place = jnp.right_shift(ii, 3), jnp.bitwise_and(ii, 7)
    for n, hit in enumerate((cell == jj, (cell == jj) & (place == 7), (cell == jj) & (place == 0))):
        cmat[:, 128 * n:128 * n + 128] = jnp.where(hit, 1.0, 0.0).astype(BF16)
    for b in range(3):
        hit = jnp.right_shift(ii + (7 + b), 3) == jj + 1
        bmat[1024 * b:1024 * b + 1024, :] = jnp.where(hit, 1.0, 0.0).astype(BF16)

    for x in loads:
        x.wait()

    w0, w1, w2, w3 = cw[0], cw[1], cw[2], cw[3]

    def cond_body(i, _):
        src = pl.multiple_of(i * 8, 8)
        dst = pl.multiple_of(i * 8 + 16, 8)
        for t in range(8):
            m = cls[t, pl.ds(src, 8), :]
            cond[t, pl.ds(dst, 8), :] = jnp.where(
                m == 0, w0, jnp.where(m == 1, w1, jnp.where(m == 2, w2, w3)))
        return 0

    lax.fori_loop(0, 32, cond_body, 0)

    def rim_tile(start, n):
        lanes = lax.broadcasted_iota(jnp.int32, (n, 128), 1)
        rows = pl.ds(start, n)
        left = jnp.where(lanes < 8, obs[0, rows, :], pltpu.roll(cond[0, rows, :], 8, 1))
        right = jnp.where(lanes >= 120, obs[7, rows, :], pltpu.roll(cond[7, rows, :], 120, 1))
        return jnp.where(lanes < 64, left, right)

    tt0[0] = rim_tile(16, 128).T
    tt0[1] = rim_tile(144, 128).T
    tbuf[...] = jnp.zeros(tbuf.shape, F32)
    tbuf[64:72, :] = rim_tile(264, 8)
    tbuf[72:80, :] = rim_tile(16, 8)
    tt0[2] = tbuf[...].T

    def side_copies(tt, rx, groups_diag, width):
        low, high = pl.ds(0, width), pl.ds(128 - width, width)
        out = []
        for n, (dr, dc) in enumerate(NB):
            if dc == 0:
                continue
            groups = pl.ds(0, tt.shape[0]) if dr == 0 else groups_diag
            rows = low if dc < 0 else high
            out.append((n, n, tt.at[groups, rows, :], rx.at[n, groups]))
        return out

    def start_all(phase, copies):
        for q, n, src, dst in copies:
            dr, dc = NB[n]
            @pl.when(ok(dr, dc))
            def _():
                pltpu.make_async_remote_copy(
                    src, dst, send_sem.at[phase, q], recv_sem.at[phase, q],
                    device_id=dev(dr, dc), device_id_type=MESH).start()

    def wait_recv_all(phase, copies):
        for q, n, src, dst in copies:
            dr, dc = NB[n]
            @pl.when(ok(-dr, -dc))
            def _():
                pltpu.make_async_remote_copy(
                    src, dst, send_sem.at[phase, q], recv_sem.at[phase, q],
                    device_id=dev(-dr, -dc), device_id_type=MESH).wait_recv()

    def wait_send_all(phase, copies):
        for q, n, src, dst in copies:
            dr, dc = NB[n]
            @pl.when(ok(dr, dc))
            def _():
                pltpu.make_async_remote_copy(
                    src, dst, send_sem.at[phase, q], recv_sem.at[phase, q],
                    device_id=dev(dr, dc), device_id_type=MESH).wait_send()

    third = pl.ds(2, 1)
    own, top, low = pl.ds(0, 8), pl.ds(16, 8), pl.ds(264, 8)
    above, below = pl.ds(8, 8), pl.ds(272, 8)
    copies0 = side_copies(tt0, rx0, third, 16)
    for q, field in ((0, obs), (8, cond)):
        copies0.append((q, 0, field.at[own, top, :], field.at[own, below, :]))
        copies0.append((q + 1, 1, field.at[own, low, :], field.at[own, above, :]))
    pl.semaphore_wait(bar, peers)
    start_all(0, copies0)

    def row_sums(ref, t):
        total = ref[t, pl.ds(16, 32, stride=8), :]
        for s in range(1, 8):
            total = total + ref[t, pl.ds(16 + s, 32, stride=8), :]
        return total

    lane32 = lax.broadcasted_iota(jnp.int32, (32, 128), 1)
    row32 = lax.broadcasted_iota(jnp.int32, (32, 128), 0)
    lane48 = lax.broadcasted_iota(jnp.int32, (48, 128), 1)
    row48 = lax.broadcasted_iota(jnp.int32, (48, 128), 0)
    last48, first48 = lane48 == 127, lane48 == 0

    every = pl.ds(16, 32, stride=8)
    last_row = pl.ds(23, 32, stride=8)
    sums = exact_dot(jnp.concatenate([
        jnp.concatenate([row_sums(cond, t) for t in range(8)], axis=1),
        jnp.concatenate([cond[t, every, :] for t in range(8)], axis=1),
        jnp.concatenate([cond[t, last_row, :] for t in range(8)], axis=1)], axis=0), cmat[...])
    ec, wc = sums[0:32, 128:256], sums[0:32, 256:384]
    nc, sc = sums[32:64, 0:128], sums[64:96, 0:128]
    part = (
        0.5 * (ec + jnp.where(lane32 == 127, 0.0, pltpu.roll(wc, 127, 1))),
        0.5 * (wc + jnp.where(lane32 == 0, 0.0, pltpu.roll(ec, 1, 1))),
        0.5 * (nc + jnp.where(row32 == 0, 0.0, pltpu.roll(sc, 1, 0))),
        0.5 * (sc + jnp.where(row32 == 31, 0.0, pltpu.roll(nc, 31, 0))),
    )

    pbuf[:, :, 0:16, :] = jnp.zeros((3, 8, 16, 128), F32)
    pbuf[:, :, 48:64, :] = jnp.zeros((3, 8, 16, 128), F32)
    for t in range(8):
        pbuf[0, t, 16:48, :] = row_sums(obs, t)
        pbuf[1, t, 16:48, :] = obs[t, every, :]
        pbuf[2, t, 16:48, :] = obs[t, last_row, :]
    vb = [[], [], []]
    for t in range(8):
        mid = pbuf[0, t, 8:56, :]
        down = mid - pbuf[1, t, 8:56, :] + pbuf[1, t, 9:57, :]
        up = mid - pbuf[2, t, 8:56, :] + pbuf[2, t, 7:55, :]
        for b in range(3):
            vb[b].append(kk[0][b] * down + kk[1][b] * mid + kk[2][b] * up)
    own_source = exact_dot(jnp.concatenate(vb[0] + vb[1] + vb[2], axis=1), bmat[...])
    own_ring = jnp.where(lane48 == 7, pltpu.roll(vb[0][0], 7, 1),
                         jnp.where(lane48 == 8, pltpu.roll(vb[2][7], 9, 1), 0.0))

    for f in range(4):
        sn1[0, f] = part[f][0:8]
        sn1[1, f] = part[f][24:32]
        craw[f, 0, 8:40, :] = part[f]
    for h in range(2):
        sn1[0, 4 + h] = own_source[8 * h:8 * h + 8]
        sn1[0, 6 + h] = own_ring[8 * h:8 * h + 8]
        sn1[1, 4 + h] = own_source[32 + 8 * h:40 + 8 * h]
        sn1[1, 6 + h] = own_ring[32 + 8 * h:40 + 8 * h]
    for g in range(2):
        for h in range(2):
            field = part[2 * g + h]
            tbuf[64 * h:64 * h + 8, :] = field[24:32]
            tbuf[64 * h + 8:64 * h + 40, :] = field
            tbuf[64 * h + 40:64 * h + 48, :] = field[0:8]
        tile = tbuf[...].T
        sd1[0, g] = tile[0:8]
        sd1[1, g] = tile[120:128]
    tbuf[0:48, :] = own_source
    tbuf[64:112, :] = own_ring
    tile = tbuf[...].T
    in48 = lane < 48
    sd1[0, 2] = jnp.where(in48, pltpu.roll(tile[0:8], 64, 1), 0.0)
    sd1[0, 3] = jnp.where(in48, tile[0:8], 0.0)
    sd1[1, 2] = jnp.where(in48, tile[120:128], 0.0)
    sd1[1, 3] = jnp.where(in48, pltpu.roll(tile[8:16], 64, 1), 0.0)

    copies1 = [(0, 0, sn1.at[0], rs1), (1, 1, sn1.at[1], rn1)]
    for n, (dr, dc) in enumerate(NB):
        if dc:
            copies1.append((n, n, sd1.at[0 if dc < 0 else 1], rx1.at[n]))
    start_all(1, copies1)

    ui = lax.broadcasted_iota(jnp.int32, (128, 1024), 0)
    uj = lax.broadcasted_iota(jnp.int32, (128, 1024), 1)
    umat[:, 0:1024] = jnp.where(jnp.right_shift(uj, 3) == ui, 1.0, 0.0).astype(BF16)
    vi = lax.broadcasted_iota(jnp.int32, (128, 128), 0)
    vj = lax.broadcasted_iota(jnp.int32, (128, 128), 1)
    umat[:, 1024:1152] = jnp.where(
        ((vj < 64) & (vi == 0)) | ((vj >= 64) & (vi == 127)), 1.0, 0.0).astype(BF16)

    def blur_adjoint(up, mid, down, b):
        return kk[0][b] * down + kk[1][b] * mid + kk[2][b] * up

    def own_body(i, _):
        base = pl.multiple_of(i * 8 + 24, 8)
        here = pl.ds(base, 8)
        up, mid, down = rows_of(obs, base - 1, 8), rows_of(obs, base, 8), rows_of(obs, base + 1, 8)
        v = [[blur_adjoint(up[t], mid[t], down[t], b) for t in range(8)] for b in range(3)]
        e0 = [pltpu.roll(x, 127, 1) for x in v[0]]
        w2_ = [pltpu.roll(x, 1, 1) for x in v[2]]
        cm, csouth = rows_of(cond, base, 8), rows_of(cond, base + 1, 8)
        ceast = [pltpu.roll(x, 127, 1) for x in cm]
        for t in range(8):
            e = jnp.where(last_lane, e0[t + 1] if t < 7 else 0.0, e0[t])
            w_ = jnp.where(first_lane, w2_[t - 1] if t else 0.0, w2_[t])
            r0[t, here, :] = v[1][t] + e + w_
            ce[t, here, :] = 0.5 * (cm[t] + jnp.where(last_lane, ceast[t + 1] if t < 7 else 0.0, ceast[t]))
            cs[t, here, :] = 0.5 * (cm[t] + csouth[t])
        return 0

    lax.fori_loop(0, 30, own_body, 0, unroll=3)
    wait_recv_all(0, copies0)

    def side(rx, group, dc, in_north, in_center):
        north = rx[NB.index((1, dc)), group]
        center = rx[NB.index((0, dc)), group]
        south = rx[NB.index((-1, dc)), group]
        return jnp.where(in_north, north, jnp.where(in_center, center, south))

    lane64 = lax.rem(lane, 64)

    lane16 = lax.broadcasted_iota(jnp.int32, (16, 128), 1)
    for dc, rows in ((-1, slice(0, 16)), (1, slice(112, 128))):
        here = NB.index((0, dc))
        hbuf[0, rows, :] = rx0[here, 0]
        hbuf[1, rows, :] = rx0[here, 1]
        hbuf[2, rows, :] = side(rx0, 2, dc, lane16 < 72, lane16 < 0)

    def cond_of(x):
        lanes = lax.broadcasted_iota(jnp.int32, x.shape, 1)
        return jnp.where(lanes < 64, pltpu.roll(x, 120, 1), pltpu.roll(x, 8, 1))

    for g in range(2):
        tile = hbuf[g].T
        rows = slice(16 + 128 * g, 144 + 128 * g)
        obs[8, rows, :] = tile
        cond[8, rows, :] = cond_of(tile)
    tile = hbuf[2].T
    for rows, lo in ((slice(8, 16), 64), (slice(272, 280), 72)):
        obs[8, rows, :] = tile[lo:lo + 8]
        cond[8, rows, :] = cond_of(tile[lo:lo + 8])
    def side_body(i, _):
        base = pl.multiple_of(i * 8 + 24, 8)
        here = pl.ds(base, 8)
        def v(t, b):
            return blur_adjoint(obs[t, pl.ds(base - 1, 8), :], obs[t, here, :],
                                obs[t, pl.ds(base + 1, 8), :], b)
        e8, w8 = pltpu.roll(v(8, 0), 127, 1), pltpu.roll(v(8, 2), 1, 1)
        e0, w7 = pltpu.roll(v(0, 0), 127, 1), pltpu.roll(v(7, 2), 1, 1)
        r0[8, here, :] = v(8, 1) + jnp.where(last_lane, e0, e8) + jnp.where(first_lane, w7, w8)
        r0[7, here, :] = r0[7, here, :] + jnp.where(last_lane, e8, 0.0)
        r0[0, here, :] = r0[0, here, :] + jnp.where(first_lane, w8, 0.0)
        c8 = cond[8, here, :]
        ce8, ce0 = pltpu.roll(c8, 127, 1), pltpu.roll(cond[0, here, :], 127, 1)
        ce[8, here, :] = 0.5 * (c8 + jnp.where(last_lane, ce0, ce8))
        ce[7, here, :] = ce[7, here, :] + 0.5 * jnp.where(last_lane, ce8, 0.0)
        cs[8, here, :] = 0.5 * (c8 + cond[8, pl.ds(base + 1, 8), :])
        return 0

    lax.fori_loop(0, 30, side_body, 0, unroll=6)

    def outer_body(i, _):
        base = pl.multiple_of(jnp.where(i < 2, i * 8 + 8, i * 8 + 248), 8)
        here = pl.ds(base, 8)
        up, mid, down = rows_of(obs, base - 1), rows_of(obs, base), rows_of(obs, base + 1)
        v = [[blur_adjoint(up[t], mid[t], down[t], b) for t in range(9)] for b in range(3)]
        e0, w2_ = sh_east(v[0]), sh_west(v[2])
        cm, csouth = rows_of(cond, base), rows_of(cond, base + 1)
        ceast = sh_east(cm)
        for t in range(9):
            r0[t, here, :] = v[1][t] + e0[t] + w2_[t]
            ce[t, here, :] = 0.5 * (cm[t] + ceast[t])
            cs[t, here, :] = 0.5 * (cm[t] + csouth[t])
        return 0

    lax.fori_loop(0, 4, outer_body, 0, unroll=4)

    def clear_outside(ref):
        @pl.when(r == 0)
        def _():
            for t in range(9):
                ref[t, 8:16, :] = jnp.zeros((8, 128), F32)

        @pl.when(r == n_rows - 1)
        def _():
            for t in range(9):
                ref[t, 272:280, :] = jnp.zeros((8, 128), F32)

        lanes = lax.broadcasted_iota(jnp.int32, (272, 128), 1)

        @pl.when(c == 0)
        def _():
            ref[8, 8:280, :] = jnp.where(lanes < 64, ref[8, 8:280, :], 0.0)

        @pl.when(c == n_cols - 1)
        def _():
            ref[8, 8:280, :] = jnp.where(lanes >= 64, ref[8, 8:280, :], 0.0)

    def diag_body(i, _):
        base = pl.multiple_of(i * 8 + 8, 8)
        here = pl.ds(base, 8)
        east = rows_of(ce, base)
        west = sh_west(east)
        for t in range(9):
            total = (east[t] + west[t]) + (cs[t, here, :] + cs[t, pl.ds(base - 1, 8), :])
            rfd[t, here, :] = 1.0 / (ksq + total)
        return 0

    lax.fori_loop(0, 34, diag_body, 0, unroll=4)
    clear_outside(rfd)

    def scale_first(i, _):
        here = pl.ds(pl.multiple_of(i * 8 + 8, 8), 8)
        for t in range(9):
            d0[t, here, :] = r0[t, here, :] * rfd[t, here, :]
        return 0

    lax.fori_loop(0, 34, scale_first, 0, unroll=4)
    wait_recv_all(1, copies1)

    for f in range(4):
        craw[f, 0, 0:8, :] = rn1[f]
        craw[f, 0, 40:48, :] = rs1[f]
    hbuf[:, 8:16, :] = jnp.zeros((3, 8, 128), F32)
    hbuf[:, 112:120, :] = jnp.zeros((3, 8, 128), F32)
    for g in range(2):
        for dc, rows in ((-1, slice(0, 8)), (1, slice(120, 128))):
            hbuf[g, rows, :] = side(rx1, g, dc, lane64 < 8, lane64 < 40)
        tile = hbuf[g].T
        for h in range(2):
            craw[2 * g + h, 1] = tile[64 * h:64 * h + 48]
    for dc, blocks in ((-1, ((2, slice(8, 16)), (3, slice(0, 8)))),
                       (1, ((2, slice(120, 128)), (3, slice(112, 120))))):
        for q, rows in blocks:
            hbuf[2, rows, :] = rx1[NB.index((0, dc)), q] + (
                pltpu.roll(rx1[NB.index((1, dc)), q], 96, 1)
                + pltpu.roll(rx1[NB.index((-1, dc)), q], 32, 1))
    tile = hbuf[2].T[0:48]
    blank = jnp.zeros((16, 128), F32)

    def with_rows(own_part, q):
        return own_part + jnp.concatenate(
            [rn1[q], rn1[q + 1], blank, rs1[q], rs1[q + 1]], axis=0)

    ring_all = pltpu.roll(with_rows(own_ring, 6), 120, 1)
    source = [
        with_rows(own_source, 4) + jnp.where(
            last48, pltpu.roll(tile, 112, 1), jnp.where(first48, pltpu.roll(tile, 16, 1), 0.0)),
        tile + jnp.where(last48 | first48, ring_all, 0.0),
    ]
    for t in range(2):
        for a, b in ((7, 8), (39, 40)):
            both = craw[3, t, a:a + 1, :] + craw[2, t, b:b + 1, :]
            craw[3, t, a:a + 1, :] = both
            craw[2, t, b:b + 1, :] = both
    pe, pw = [craw[0, t] for t in range(2)], [craw[1, t] for t in range(2)]
    rows_ok = ((row48 >= 8) | (r > 0)) & ((row48 < 40) | (r < n_rows - 1))
    lanes_ok = ((lane48 >= 64) | (c < n_cols - 1)) & ((lane48 < 64) | (c > 0))
    for t in range(2):
        c_east = pe[t] + jnp.where(last48, pltpu.roll(pw[1 - t], 127, 1), 0.0)
        c_west = pw[t] + jnp.where(first48, pltpu.roll(pe[1 - t], 1, 1), 0.0)
        c_north, c_south = craw[2, t], craw[3, t]
        c_diag = 64.0 * (ksum * ksum) + c_east + c_west + c_north + c_south
        scale = jnp.where(rows_ok & lanes_ok if t else rows_ok, OMEGA / c_diag, 0.0)
        for f, x in enumerate((source[t], c_east, c_west, c_north, c_south)):
            ctab[f, t] = x * scale
        if t == 0:
            ctab[5, 0] = scale
            ctab[5, 1] = c_diag * (1.0 / OMEGA)

    def sweep(_, carry):
        z = [zs[t, 8:56, :] for t in range(2)]
        east = [pltpu.roll(x, 127, 1) for x in z]
        west = [pltpu.roll(x, 1, 1) for x in z]
        new = []
        for t in range(2):
            ze = jnp.where(last48, east[1 - t], east[t])
            zw = jnp.where(first48, west[1 - t], west[t])
            zn, zso = zs[t, 7:55, :], zs[t, 9:57, :]
            new.append((ctab[0, t] + (1.0 - OMEGA) * z[t])
                       + (ctab[1, t] * ze + ctab[2, t] * zw)
                       + (ctab[3, t] * zn + ctab[4, t] * zso))
        for t in range(2):
            zs[t, 8:56, :] = new[t]
        return carry

    def jacobi():
        for t in range(2):
            zs[t, 8:56, :] = ctab[0, t]
        lax.fori_loop(0, SWEEPS - 1, sweep, 0, unroll=SWEEPS - 1)

    def spread():
        up = exact_dot(zs[0, 8:56, :], umat[:, 0:1024])
        for t in range(8):
            zup[t] = up[:, 128 * t:128 * t + 128]
        zup[8] = exact_dot(zs[1, 8:56, :], umat[:, 1024:1152])

    jacobi()
    spread()

    def add_first(i, _):
        here = pl.ds(pl.multiple_of(i * 8 + 8, 8), 8)
        for t in range(9):
            d0[t, here, :] = d0[t, here, :] + zup[t, pl.ds(i + 7, 1), :]
        return 0

    lax.fori_loop(0, 34, add_first, 0, unroll=4)

    def blur_rows(ref, base):
        up, mid, down = rows_of(ref, base - 1), rows_of(ref, base), rows_of(ref, base + 1)
        u = [[kk[0][b] * up[t] + kk[1][b] * mid[t] + kk[2][b] * down[t] for t in range(9)]
             for b in range(3)]
        w_, e_ = sh_west(u[0]), sh_east(u[2])
        return [u[1][t] + w_[t] + e_[t] for t in range(9)], up, mid, down

    def blur0(i, _):
        base = pl.multiple_of(i * 8 + 8, 8)
        out, _, _, _ = blur_rows(d0, base)
        for t in range(9):
            img[t, pl.ds(base, 8), :] = out[t]
        return 0

    lax.fori_loop(0, 34, blur0, 0, unroll=4)
    clear_outside(img)

    def apply_rows(field, base, n):
        up, mid, down = rows_of(img, base - 1), rows_of(img, base), rows_of(img, base + 1)
        v = [[blur_adjoint(up[t], mid[t], down[t], b) for t in range(9)] for b in range(3)]
        up, mid, down = rows_of(field, base - 1), rows_of(field, base), rows_of(field, base + 1)
        east = sh_east(mid)
        flux = [ce[t, pl.ds(base, 8), :] * (mid[t] - east[t]) for t in range(9)]
        e0 = sh_east(v[0])
        w2_ = sh_west([v[2][t] - flux[t] for t in range(9)])
        out = []
        for t in range(n):
            lap = (cs[t, pl.ds(base, 8), :] * (mid[t] - down[t])
                   - cs[t, pl.ds(base - 1, 8), :] * (up[t] - mid[t]))
            out.append(((v[1][t] + e0[t]) + (w2_[t] + flux[t])) + lap)
        return out, mid

    zero = jnp.zeros((8, 128), F32)

    def apply0(i, carry):
        gam, dad = carry
        base = pl.multiple_of(i * 8 + 16, 8)
        out, mid = apply_rows(d0, base, 9)
        q0[8, pl.ds(base, 8), :] = out[8]
        w[8, pl.ds(base, 8), :] = out[8] * rfd[8, pl.ds(base, 8), :]
        for t in range(8):
            q0[t, pl.ds(base, 8), :] = out[t]
            w[t, pl.ds(base, 8), :] = out[t] * rfd[t, pl.ds(base, 8), :]
            gam = gam + r0[t, pl.ds(base, 8), :] * mid[t]
            dad = dad + mid[t] * out[t]
        return gam, dad

    gam, dad = lax.fori_loop(0, 32, apply0, (zero, zero), unroll=4)

    src = jnp.concatenate([row_sums(q0, t) for t in range(8)], axis=1)
    cells = exact_dot(src, cmat[:, 0:128])
    b2 = cells * ctab[5, 0, 8:40, :]
    ctab[0, 0, 8:40, :] = b2

    sn2[...] = b2
    tbuf[0:8, :] = b2[24:32]
    tbuf[8:40, :] = b2
    tbuf[40:48, :] = b2[0:8]
    tt2[0] = tbuf[...].T
    copies2 = [(0, 0, sn2.at[pl.ds(0, 8), :], rs2), (1, 1, sn2.at[pl.ds(24, 8), :], rn2)]
    copies2 += side_copies(tt2, rx2, pl.ds(0, 1), 8)
    start_all(2, copies2)

    def apply0_rim(i, _):
        base = pl.multiple_of(i * 264 + 8, 8)
        out, _ = apply_rows(d0, base, 9)
        for t in range(9):
            q0[t, pl.ds(base, 8), :] = out[t]
            w[t, pl.ds(base, 8), :] = out[t] * rfd[t, pl.ds(base, 8), :]
        return 0

    lax.fori_loop(0, 2, apply0_rim, 0, unroll=2)

    def blur1(i, _):
        base = pl.multiple_of(i * 8 + 8, 8)
        out, _, _, _ = blur_rows(w, base)
        for t in range(9):
            img[t, pl.ds(base, 8), :] = out[t]
        return 0

    lax.fori_loop(0, 34, blur1, 0, unroll=4)
    clear_outside(img)

    def apply1(i, carry):
        qw, waw = carry
        base = pl.multiple_of(i * 8 + 16, 8)
        out, mid = apply_rows(w, base, 8)
        for t in range(8):
            lw[t, pl.ds(base, 8), :] = out[t]
            qw = qw + q0[t, pl.ds(base, 8), :] * mid[t]
            waw = waw + mid[t] * out[t]
        return qw, waw

    qw, waw = lax.fori_loop(0, 32, apply1, (zero, zero), unroll=4)
    at_cells = exact_dot(
        jnp.concatenate([row_sums(lw, t) for t in range(8)], axis=1), cmat[:, 0:128])

    wait_recv_all(2, copies2)
    for dc, rows in ((-1, slice(0, 8)), (1, slice(120, 128))):
        hbuf[0, rows, :] = side(rx2, 0, dc, lane < 8, lane < 40)
    ctab[0, 1, :, :] = hbuf[0].T[0:48]
    ctab[0, 0, 0:8, :] = rn2[...]
    ctab[0, 0, 40:48, :] = rs2[...]
    jacobi()
    spread()

    z = zs[0, 16:48, :]
    ze = jnp.where(lane32 == 127, pltpu.roll(zs[1, 16:48, :], 127, 1), pltpu.roll(z, 127, 1))
    zw = jnp.where(lane32 == 0, pltpu.roll(zs[1, 16:48, :], 1, 1), pltpu.roll(z, 1, 1))
    g = [ctab[f, 0, 8:40, :] for f in range(5)]
    lap = (g[1] * (z - ze) + g[2] * (z - zw)) + (
        g[3] * (z - zs[0, 15:47, :]) + g[4] * (z - zs[0, 17:49, :]))

    def fold(x):
        return (x[0:8] + x[8:16]) + (x[16:24] + x[24:32])

    qw = qw + fold(cells * z)
    waw = waw + fold(z * (2.0 * at_cells + ctab[5, 1, 8:40, :] * lap))

    for n in range(6):
        rows = slice(8 * n, 8 * n + 8)
        mid = [zup[t, rows, :] for t in range(9)]
        east, west = sh_east(mid), sh_west(mid)
        for t in range(8):
            zeast[t, rows, :] = east[t]
            zwest[t, rows, :] = west[t]
    ksums = [(kk[0][b] + kk[1][b]) + kk[2][b] for b in range(3)]

    def lanes_conv(weights, parts):
        return weights[0] * parts[0] + weights[1] * parts[1] + weights[2] * parts[2]

    for n in range(4):
        at, up, down = (slice(8 * n + o, 8 * n + o + 8) for o in (8, 7, 9))
        for t in range(8):
            here = [x[t, at, :] for x in (zwest, zup, zeast)]
            north = [x[t, up, :] for x in (zwest, zup, zeast)]
            south = [x[t, down, :] for x in (zwest, zup, zeast)]
            mid = lanes_conv(ksums, here)
            first = mid + lanes_conv(kk[0], [p - q for p, q in zip(north, here)])
            last = mid + lanes_conv(kk[2], [p - q for p, q in zip(south, here)])
            waw = waw + (6.0 * (mid * mid) + (first * first + last * last))

    for n, part in enumerate((gam, dad, qw, waw)):
        red0[n:n + 1, :] = jnp.sum(part, axis=0, keepdims=True)
    red0[4:8, :] = jnp.zeros((4, 128), F32)
    redx[k8] = red0[...]
    for peer in zk_group:
        pltpu.make_async_remote_copy(
            red0, redx.at[k8], rsend.at[0], rrecv.at[0],
            device_id=peer, device_id_type=MESH).start()

    def add_coarse(i, _):
        here = pl.ds(pl.multiple_of(i * 8 + 8, 8), 8)
        for t in range(9):
            w[t, here, :] = w[t, here, :] + zup[t, pl.ds(i + 7, 1), :]
        return 0

    lax.fori_loop(0, 34, add_coarse, 0, unroll=4)
    lax.fori_loop(0, 34, blur1, 0, unroll=4)
    clear_outside(img)

    def apply2(i, _):
        base = pl.multiple_of(i * 8 + 16, 8)
        out, _ = apply_rows(w, base, 8)
        for t in range(8):
            lw[t, pl.ds(base, 8), :] = out[t]
        return 0

    def all_bytes(buf, n, sem):
        return pltpu.make_async_copy(buf.at[pl.ds(0, n)], buf.at[pl.ds(0, n)], sem)

    all_bytes(redx, zk - 1, rrecv.at[0]).wait()
    total = redx[0]
    for i in range(1, zk):
        total = total + redx[i]
    red1[...] = total
    redy[xy_me] = total
    for peer in xy_group:
        pltpu.make_async_remote_copy(
            red1, redy.at[xy_me], rsend.at[1], rrecv.at[1],
            device_id=peer, device_id_type=MESH).start()
    lax.fori_loop(0, 32, apply2, 0, unroll=4)
    wait_send_all(0, copies0)
    wait_send_all(1, copies1)
    wait_send_all(2, copies2)
    all_bytes(redx, zk - 1, rsend.at[0]).wait()
    all_bytes(redy, n_rows * ny - 1, rrecv.at[1]).wait()
    total = redy[0]
    for i in range(1, n_rows * ny):
        total = total + redy[i]
    value = jnp.broadcast_to(jnp.sum(total, axis=1, keepdims=True), (8, 128))
    g0 = jnp.broadcast_to(value[0:1], (8, 128))
    dq = jnp.broadcast_to(value[1:2], (8, 128))
    qws = jnp.broadcast_to(value[2:3], (8, 128))
    ws = jnp.broadcast_to(value[3:4], (8, 128))
    alpha = g0 / dq
    g1 = (g0 - alpha * dq) + alpha * (alpha * qws - dq)
    beta1 = 1.0 + g1 / g0
    dad1 = beta1 * (beta1 * dq - alpha * qws) + alpha * (alpha * ws - beta1 * qws)
    step = g1 / dad1
    ca = alpha + step * beta1
    cb = alpha * step

    coef[0] = ca
    coef[1] = cb
    all_bytes(redy, n_rows * ny - 1, rsend.at[1]).wait()


def finish_kernel(r0, d0, q0, w, lw, coef, sol_hbm, res_hbm, sol, res, out_sem):
    ca, cb = coef[0], coef[1]
    stores = []
    for n in range(8):
        def finish(i, _):
            dst_rows = pl.ds(pl.multiple_of(i * 8 + n * 32, 8), 8)
            src_rows = pl.ds(pl.multiple_of(i * 8 + n * 32 + 16, 8), 8)
            for t in range(8):
                lanes = slice(t * 128, t * 128 + 128)
                sol[dst_rows, lanes] = ca * d0[t, src_rows, :] - cb * w[t, src_rows, :]
                res[dst_rows, lanes] = (
                    r0[t, src_rows, :] - ca * q0[t, src_rows, :]) + cb * lw[t, src_rows, :]
            return 0

        lax.fori_loop(0, 4, finish, 0, unroll=2)
        rows = pl.ds(n * 32, 32)
        stores.append(pltpu.make_async_copy(sol.at[rows], sol_hbm.at[rows], out_sem.at[n]))
        stores.append(pltpu.make_async_copy(res.at[rows], res_hbm.at[rows], out_sem.at[8 + n]))
        stores[-2].start()
        stores[-1].start()
    for x in stores:
        x.wait()


def body(n_rows, n_cols, observed, class_map, class_weights, blur_kernel):
    zk = min(8, n_cols)
    ny = n_cols // zk
    big = pltpu.VMEM((9, 288, 128), F32)
    half = pltpu.VMEM((256, 1024), F32)

    def v(*shape):
        return pltpu.VMEM(shape, F32)

    scratch = [
        big, pltpu.VMEM((8, 256, 128), jnp.int32), big, big, big, big, big,
        v(9, 48, 128), pltpu.VMEM((1024, 384), BF16), pltpu.VMEM((3072, 128), BF16),
        pltpu.VMEM((128, 1152), BF16),
        v(128, 128), v(3, 128, 128), v(1, 128, 128), v(3, 128, 128),
        v(6, 2, 48, 128), v(2, 64, 128),
        v(8, 3, 16, 128), v(2, 8, 8, 128), v(2, 4, 8, 128), v(8, 8, 128), v(8, 8, 128),
        v(8, 4, 8, 128), v(3, 8, 64, 128), v(4, 2, 48, 128),
        v(32, 128), v(8, 128), v(8, 128), v(8, 1, 8, 128), v(8, 48, 128), v(8, 48, 128),
        v(8, 128), v(8, 128), v(zk, 8, 128), v(n_rows * ny, 8, 128),
        pltpu.SemaphoreType.DMA((16,)),
        pltpu.SemaphoreType.DMA((3, 10)), pltpu.SemaphoreType.DMA((3, 10)),
        pltpu.SemaphoreType.DMA((2,)), pltpu.SemaphoreType.DMA((2,)),
    ]
    hbm = pl.BlockSpec(memory_space=pltpu.HBM)
    vmem = pl.BlockSpec(memory_space=pltpu.VMEM)
    scalars = pl.BlockSpec(memory_space=pltpu.SMEM)
    field = pltpu.VMEM((9, 288, 128), F32)
    fields = pl.pallas_call(
        functools.partial(kernel, n_rows, n_cols, zk),
        out_shape=(field,) * 5 + (pltpu.VMEM((2, 8, 128), F32),),
        in_specs=[scalars, scalars, hbm, hbm],
        out_specs=(vmem,) * 6,
        scratch_shapes=scratch,
        compiler_params=pltpu.CompilerParams(
            collective_id=0, has_side_effects=True, vmem_limit_bytes=KERNEL_VMEM),
    )(class_weights, blur_kernel, observed, class_map)
    shape = jax.ShapeDtypeStruct(observed.shape, F32)
    return pl.pallas_call(
        finish_kernel,
        out_shape=(shape, shape),
        in_specs=[vmem] * 6,
        out_specs=(hbm, hbm),
        scratch_shapes=[half, half, pltpu.SemaphoreType.DMA((16,))],
        compiler_params=pltpu.CompilerParams(vmem_limit_bytes=FINISH_VMEM),
    )(*fields)


def solution(mesh):
    n_rows, n_cols = mesh.shape["rows"], mesh.shape["cols"]
    return jax.shard_map(
        functools.partial(body, n_rows, n_cols),
        mesh=mesh,
        in_specs=(P("rows", "cols"), P("rows", "cols"), P(), P()),
        out_specs=(P("rows", "cols"), P("rows", "cols")),
        check_vma=False,
    )
```
